32 devices in a mesh: lon: 16 (over z, y, core), rad: 2 (over x).
Axes of the slice: x: 2, y: 2, z: 4, core: 2. Of those that a mesh axis runs over, the one named last changes fastest.
Arguments:
- logvisc: float32 [96, 64, 512], P('rad', 'lon'), may hold values from -1 to 1
- momentum: float32 [96, 64, 512], P('rad', 'lon'), may hold values from -6 to 6
- displacement: float32 [3, 96, 64, 512], P(None, 'rad', 'lon'), may hold values from -6 to 6
- ice_history: float32 [8, 64, 512], P(None, 'lon'), may hold values from -6 to 6
- load_steps: int32 [2], replicated, may hold values from 0 to 7
- site_cells: int32 [192], P('lon'), may hold values from 0 to 32767
- observed: float32 [3, 192], P(None, 'lon'), may hold values from -6 to 6
- site_weight: float32 [3, 192], P(None, 'lon'), may hold values from 2 to 6
Outputs:
- new_logvisc: float32 [96, 64, 512], P('rad', 'lon')
- half_momentum: float32 [96, 64, 512], P('rad', 'lon')
- misfit: float32 [1], replicated
The draws below stay inside these ranges and needn't reach their ends.
Inputs may be any that keep to these rules, and one draw needn't show every extreme that they name: site_cells holds lon * 512 + lat of the surface cell where the site stands. load_steps indexes the first dimension of ice_history.
All inputs are finite; a program needn't handle non-finite values.
Results may differ from the reference program's by a relative error of at most 0.0003.
Values sent between devices are 32-bit elements; how exact they have to be, the bound alone decides.
No kernel may reach another device: no remote copies, remote signals or barrier semaphores. Data moves between devices by JAX's collectives and lax.ppermute only.
A program may use at most 64 MiB of HBM per device.

```python
import math
import jax
import jax.numpy as jnp
from jax import lax

NR = 96
NLAT = 512
SITES_DEV = 12
RELAX = 2
HIST = 8
NLON = 64
SITES = 192


def set_ends(array, own_key, least, high):
    extent = array.shape
    index_at = [jax.random.randint(jax.random.fold_in(own_key, axis), (), 0, extent[axis]) for axis in range(len(extent))]
    array = array.at[tuple(index_at)].set(least)
    longest = extent.index(max(extent))
    index_at[longest] = (index_at[longest] + 1) % extent[longest]
    return array.at[tuple(index_at)].set(high)


def steps_of(key, shape, split, low, largest):
    factor_of = 1.0
    for axis_at, shards_of in split:
        steps = jax.random.uniform(jax.random.fold_in(jax.random.fold_in(key, 6), axis_at), (shards_of,), jnp.float32, low / len(split), largest / len(split))
        factor_of = factor_of * jnp.repeat(jnp.exp(steps), shape[axis_at] // shards_of).reshape((-1,) + (1,) * (len(shape) - 1 - axis_at))
    return factor_of


def gaussian(key, dims, deviation, bound, pieces=(), held_as=jnp.bfloat16):
    entries = jax.random.normal(key, dims, jnp.float32) * deviation
    if len(pieces) > 0:
        entries = steps_of(key, dims, pieces, -0.22, 0.18) * entries
    return jnp.clip(entries, min=-bound, max=bound).astype(held_as)


def setup_inputs(seed: int = 0) -> dict:
    keys = jax.random.split(jax.random.key(seed), 9)
    return {
        "logvisc": jnp.clip(jax.random.uniform(keys[0], (NR, NLON, NLAT), jnp.float32, -1.0, 1.0) * steps_of(keys[0], (NR, NLON, NLAT), ((0, 2), (1, 16)), -0.4, 0.0), -1.0, 1.0),
        "momentum": gaussian(keys[1], (NR, NLON, NLAT), 1.0, 6.0, ((0, 2), (1, 16)), jnp.float32),
        "displacement": gaussian(keys[2], (3, NR, NLON, NLAT), 1.0, 6.0, ((1, 2), (2, 16)), jnp.float32),
        "ice_history": gaussian(keys[3], (HIST, NLON, NLAT), 1.0, 6.0, ((1, 16),), jnp.float32),
        "load_steps": jax.random.randint(keys[4], (RELAX,), 0, HIST).astype(jnp.int32),
        "site_cells": set_ends(jax.random.randint(keys[5], (SITES,), 0, NLON * NLAT), jax.random.fold_in(keys[5], 1), 0, (NLON * NLAT) - 1).astype(jnp.int32),
        "observed": gaussian(keys[6], (3, SITES), 1.0, 6.0, ((1, 16),), jnp.float32),
        "site_weight": jnp.clip(jnp.exp(math.log(6.0) - 1.0986123 * jax.random.uniform(keys[7], (3, SITES), jnp.float32) ** steps_of(keys[7], (3, SITES), ((1, 16),), -0.2, 0.2)), 2.0, 6.0),
    }


RELAX_RATE = 0.05
KERNEL_WIDTH = 0.1
KERNEL_WAVE = 40.0
PRIOR_WEIGHT = 0.1
LOAD_FACTOR = 1.0

def harmonic(center_fluid, other_fluid):
    summed = center_fluid + other_fluid
    coeff = 2.0 * center_fluid * other_fluid / summed
    slope = 2.0 * other_fluid * other_fluid / (summed * summed)
    return (coeff, slope)

def neighbours(padded):
    return [padded[:, 2:, 1:-1, 1:-1], padded[:, :-2, 1:-1, 1:-1], padded[:, 1:-1, 2:, 1:-1], padded[:, 1:-1, :-2, 1:-1], padded[:, 1:-1, 1:-1, 2:], padded[:, 1:-1, 1:-1, :-2]]

def middle(padded):
    return padded[:, 1:-1, 1:-1, 1:-1]

def apply_operator(field_pad, fluid_pad):
    fluid_mid = middle(fluid_pad)
    field_mid = middle(field_pad)
    total = jnp.zeros(field_mid.shape, jnp.float32)
    for fluid_side, field_side in zip(neighbours(fluid_pad), neighbours(field_pad)):
        coeff, slope = harmonic(fluid_mid, fluid_side)
        total = total + coeff * (field_side - field_mid)
    return total

def fluid_gradient(state_pad, adjoint_pad, fluid_pad):
    fluid_mid = middle(fluid_pad)
    state_mid = middle(state_pad)
    adjoint_mid = middle(adjoint_pad)
    total = jnp.zeros(fluid_mid.shape, jnp.float32)
    for fluid_side, state_side, adjoint_side in zip(neighbours(fluid_pad), neighbours(state_pad), neighbours(adjoint_pad)):
        coeff, slope = harmonic(fluid_mid, fluid_side)
        product = lax.optimization_barrier(jnp.sum((state_side - state_mid) * (adjoint_side - adjoint_mid), axis=0, keepdims=True))
        total = total + slope * product
    return -RELAX_RATE * total

def pad_whole(field):
    wrapped = jnp.concatenate([field[:, :, -1:], field, field[:, :, :1]], axis=2)
    return jnp.pad(wrapped, ((0, 0), (1, 1), (0, 0), (1, 1)))

def cell_features(lon_index, lat_index, total_lon, total_lat):
    theta = math.pi * (lat_index.astype(jnp.float32) + 0.5) / total_lat
    phi = 2.0 * math.pi * lon_index.astype(jnp.float32) / total_lon
    upward = jnp.broadcast_to(jnp.cos(theta)[None, :], (phi.shape[0], theta.shape[0]))
    eastern = jnp.sin(theta)[None, :] * jnp.cos(phi)[:, None]
    northern = jnp.sin(theta)[None, :] * jnp.sin(phi)[:, None]
    return jnp.stack([upward, eastern, northern]).reshape(3, -1)

def site_features(cells, total_lon, total_lat):
    lon_index = cells // total_lat
    lat_index = cells % total_lat
    theta = math.pi * (lat_index.astype(jnp.float32) + 0.5) / total_lat
    phi = 2.0 * math.pi * lon_index.astype(jnp.float32) / total_lon
    return jnp.stack([jnp.cos(theta), jnp.sin(theta) * jnp.cos(phi), jnp.sin(theta) * jnp.sin(phi)], axis=1)

def kernel(site_feats, cell_feats):
    cosine = site_feats[:, 0:1] * cell_feats[0:1] + site_feats[:, 1:2] * cell_feats[1:2] + site_feats[:, 2:3] * cell_feats[2:3]
    chord = 2.0 - 2.0 * cosine
    return 1.0 / (1.0 + chord / KERNEL_WIDTH) + 0.5 * jnp.cos(KERNEL_WAVE * chord)

def reference(logvisc, momentum, displacement, ice_history, load_steps, site_cells, observed, site_weight):
    fluidity = jnp.exp(-logvisc)
    fluid_pad = pad_whole(fluidity[None])
    radial = jnp.arange(NR).astype(jnp.float32)
    depth_weight = jnp.exp(4.0 * (radial - (NR - 1)) / NR)
    top_row = (jnp.arange(NR) == NR - 1).astype(jnp.float32)[None, :, None, None]
    upward = (jnp.arange(3) == 0).astype(jnp.float32)[:, None, None, None]
    state = displacement
    saved = []
    for level in range(RELAX):
        saved.append(state)
        padded = pad_whole(state)
        load = lax.dynamic_index_in_dim(ice_history, load_steps[level], 0, keepdims=False)
        state = state + RELAX_RATE * apply_operator(padded, fluid_pad) - LOAD_FACTOR * upward * top_row * load[None, None]
    surface = lax.optimization_barrier(jnp.sum(depth_weight[None, :, None, None] * state, axis=1)).reshape(3, -1)
    scale = 1.0 / math.sqrt(NLON * NLAT)
    cells_all = cell_features(jnp.arange(NLON), jnp.arange(NLAT), NLON, NLAT)
    feats = site_features(site_cells, NLON, NLAT)
    blocks = feats.reshape(-1, SITES_DEV, 3)

    def predict_block(block):
        weights = kernel(block, cells_all)
        return jnp.einsum('sm,cm->sc', weights, surface, precision=lax.Precision.HIGHEST, preferred_element_type=jnp.float32)
    predicted = (lax.map(predict_block, blocks).reshape(-1, 3) * scale).T
    weighted = site_weight * (predicted - observed)
    misfit = jnp.sum(weighted * weighted) / (3 * SITES)
    pulled = (site_weight * weighted).T.reshape(-1, SITES_DEV, 3)

    def spread_block(total, item):
        block, values = item
        weights = kernel(block, cells_all)
        return (total + jnp.einsum('sc,sm->cm', values, weights, precision=lax.Precision.HIGHEST, preferred_element_type=jnp.float32), None)
    summed, unused = lax.scan(spread_block, jnp.zeros((3, NLON * NLAT), jnp.float32), (blocks, pulled))
    surface_adjoint = (summed * scale).reshape(3, NLON, NLAT)
    adjoint = depth_weight[None, :, None, None] * surface_adjoint[:, None]
    gradient_fluid = jnp.zeros((1, NR, NLON, NLAT), jnp.float32)
    for level in range(RELAX - 1, -1, -1):
        adjoint_pad = pad_whole(adjoint)
        gradient_fluid = gradient_fluid + fluid_gradient(pad_whole(saved[level]), adjoint_pad, fluid_pad)
        if level > 0:
            adjoint = adjoint + RELAX_RATE * apply_operator(adjoint_pad, fluid_pad)
    gradient = -fluidity * gradient_fluid[0] + PRIOR_WEIGHT * logvisc
    half_momentum = momentum - 0.5 * gradient
    new_logvisc = logvisc + half_momentum
    return (new_logvisc, half_momentum, misfit.reshape(1))
```

```python
import functools
import math

import jax
import jax.numpy as jnp
from jax import lax
from jax.experimental import pallas as pl
from jax.experimental.pallas import tpu as pltpu
from jax.sharding import PartitionSpec as P

RELAX_RATE = 0.05
KERNEL_WIDTH = 0.1
KERNEL_WAVE = 40.0
PRIOR_WEIGHT = 0.1
COLS = 8
F32 = jnp.float32
VMEM_LIMIT = 56 * 1024 * 1024


def reciprocal(x):
    r = pl.reciprocal(x, approx=True)
    return r * (2.0 - x * r)


def sub_index(width):
    return lax.broadcasted_iota(jnp.int32, (8, width), 0)


def lat_next(x):
    return pltpu.roll(x, x.shape[1] - 1, 1)


def lat_prev(x):
    return pltpu.roll(x, 1, 1)


def lon_next(x):
    return pltpu.roll(x, 7, 0)


def lon_prev(x):
    return pltpu.roll(x, 1, 0)


def swap_halves(x):
    return pltpu.roll(x, 4, 0)


def pack(low, high):
    return jnp.concatenate([low, high], axis=0)


def site_kernel(d):
    x = 1.0 + d * (1.0 / KERNEL_WIDTH)
    turns = d * (KERNEL_WAVE / (2.0 * math.pi))
    u = turns - jnp.round(turns)
    z = u * u
    p = 0.0821458866
    p = p * z - 0.599264529
    p = p * z + 2.55016404
    p = p * z - 5.16771278
    p = p * z + 3.14159265
    s = p * u
    return (reciprocal(x) + 0.5) - s * s


def weights_kernel(sites_ref, lat_ref, out_ref):
    width = lat_ref.shape[1]
    cos_lat = lat_ref[0:1, :]
    sin_lat = lat_ref[1:2, :]

    def chunk(j, carry):
        rows = pl.ds(pl.multiple_of(j * 8, 8), 8)
        cols = sites_ref[rows, :]
        a = 2.0 + cols[:, 0:1] * cos_lat
        b = cols[:, 1:2] * sin_lat
        for col in range(COLS):
            out_ref[col, rows, :] = site_kernel(a + b * cols[:, 2 + col : 3 + col])
        return carry

    lax.fori_loop(0, out_ref.shape[1] // 8, chunk, 0)


def forward_kernel(
    steps_ref, wr_ref, flag_ref, v_ref, s_ref, west_ref, east_ref, low_ref, high_ref, ice_ref, k_ref,
    fluid_ref, field_ref, fluid_side_ref, field_side_ref, next_ref, to_west_ref, to_east_ref,
    to_low_ref, to_high_ref, pred_ref,
    ge_ref, gn_ref, gw_ref, gu_ref, surf_ref,
):
    nr, nl, width = v_ref.shape
    half = nr // 2
    sub = sub_index(width)
    lon = sub % 4
    lane = lax.broadcasted_iota(jnp.int32, (8, width), 1)
    lower = sub < 4
    has_low, has_high = flag_ref[0], flag_ref[1]

    def wr_row(i):
        return jnp.where(lower, wr_ref[i + 2], wr_ref[i + half + 2])

    def side(ref, i):
        return [
            jnp.where(
                lower,
                jnp.where(lon < 2, west_ref[n, i], east_ref[n, i]),
                jnp.where(lon < 2, west_ref[n, i + half], east_ref[n, i + half]),
            )
            for n in range(4)
        ]

    def pack_row(i, carry):
        fluid_ref[i + 1] = jnp.exp(-pack(v_ref[i], v_ref[i + half]))
        sides = side(None, i)
        fluid_side_ref[i] = jnp.exp(-sides[0])
        for c in range(3):
            field_ref[c, i + 1] = pack(s_ref[c, i], s_ref[c, i + half])
            field_side_ref[c, i] = sides[1 + c]
        return carry

    lax.fori_loop(0, half, pack_row, 0)
    fluid_ref[0] = pack(has_low * jnp.exp(-low_ref[0]), jnp.exp(-v_ref[half - 1]))
    fluid_ref[half + 1] = pack(jnp.exp(-v_ref[half]), has_high * jnp.exp(-high_ref[0]))
    for c in range(3):
        field_ref[c, 0] = pack(low_ref[1 + c], s_ref[c, half - 1])
        field_ref[c, half + 1] = pack(s_ref[c, half], high_ref[1 + c])

    def face(a, b):
        return 2.0 * a * b * reciprocal(a + b)

    f_low = fluid_ref[0]
    f_first = fluid_ref[1]
    face_low = face(f_low, f_first)
    gu_ref[0] = (wr_row(0) - wr_row(-1)) * face_low

    def relax_row(i, carry):
        flux_low = carry
        f = fluid_ref[i + 1]
        f_up = fluid_ref[i + 2]
        f_side = fluid_side_ref[i]
        wr = wr_row(i)
        h_east = face(f, jnp.where(lon == 3, f_side, lon_next(f)))
        h_cut = face(f, f_side)
        h_west = jnp.where(lon == 0, h_cut, lon_prev(h_east))
        h_north = jnp.where(lane < width - 1, face(f, lat_next(f)), 0.0)
        h_up = face(f, f_up)
        ge_ref[i] = wr * h_east
        gw_ref[i] = wr * h_cut
        gn_ref[i] = wr * h_north
        gu_ref[i + 1] = (wr_row(i + 1) - wr) * h_up
        flux_out = []
        for c in range(3):
            s = field_ref[c, i + 1]
            s_side = field_side_ref[c, i]
            s_east = jnp.where(lon == 3, s_side, lon_next(s))
            s_west = jnp.where(lon == 0, s_side, lon_prev(s))
            north = h_north * (lat_next(s) - s)
            up = h_up * (field_ref[c, i + 2] - s)
            total = h_east * (s_east - s) + h_west * (s_west - s)
            total = total + (north - lat_prev(north))
            total = total + (up - flux_low[c])
            next_ref[c, i] = s + RELAX_RATE * total
            flux_out.append(up)
        return tuple(flux_out)

    first = tuple(face_low * (field_ref[c, 1] - field_ref[c, 0]) for c in range(3))
    lax.fori_loop(0, half, relax_row, first)

    load = ice_ref[steps_ref[0]] * (1.0 - has_high)
    next_ref[0, half - 1] = next_ref[0, half - 1] - pack(jnp.zeros_like(load), load)

    for c in range(3):
        top = next_ref[c, half - 1]
        to_low_ref[c] = next_ref[c, 0][0:4, :]
        to_high_ref[c] = top[4:8, :]
        below = jnp.where(lower, 0.0, swap_halves(top))

        def column_row(i, carry):
            below, column, east, north, cut = carry
            s = next_ref[c, i]
            to_west_ref[c, i] = s[0:1, :]
            to_west_ref[c, i + half] = s[4:5, :]
            to_east_ref[c, i] = s[3:4, :]
            to_east_ref[c, i + half] = s[7:8, :]
            column = column + wr_row(i) * s - RELAX_RATE * (gu_ref[i] * (s - below))
            east = east + ge_ref[i] * (jnp.where(lon == 3, 0.0, lon_next(s)) - s)
            north = north + gn_ref[i] * (lat_next(s) - s)
            cut = cut + gw_ref[i] * s
            return s, column, east, north, cut

        zero = jnp.zeros((8, width), F32)
        last, column, east, north, cut = lax.fori_loop(
            0, half, column_row, (below, zero, zero, zero, zero)
        )
        column = column + jnp.where(lower, 0.0, RELAX_RATE * (gu_ref[half] * last))
        column = column + swap_halves(column)
        east = east + swap_halves(east)
        north = north + swap_halves(north)
        cut = cut + swap_halves(cut)
        west = jnp.where(lon == 0, cut, lon_prev(east))
        own = column + RELAX_RATE * ((east - west) + (north - lat_prev(north)))
        if c == 0:
            second = ice_ref[steps_ref[1]] * ((1.0 - has_high) * wr_ref[nr + 1])
            own = own - pack(second, second)
        surf_ref[0, c : c + 1, :] = RELAX_RATE * cut[0:1, :]
        for col in range(4):
            surf_ref[col + 1, c : c + 1, :] = own[col : col + 1, :]
        surf_ref[5, c : c + 1, :] = -RELAX_RATE * east[3:4, :]

    for col in range(6):
        surf_ref[col, 3:8, :] = jnp.zeros((5, width), F32)
    total = jnp.zeros((8, k_ref.shape[1]), F32)
    for col in range(6):
        total = total + lax.dot_general(
            surf_ref[col],
            k_ref[col + 1],
            (((1,), (1,)), ((), ())),
            precision=lax.Precision.HIGHEST,
            preferred_element_type=F32,
        )

    def spread(n, carry):
        pred_ref[n] = total[0:3, :]
        return carry

    lax.fori_loop(0, pred_ref.shape[0], spread, 0)


def prepare_kernel(
    wr_ref, flag_ref, v_ref, m_ref, fluid_ref, field_ref, fluid_side_ref, field_side_ref, next_ref,
    west_ref, east_ref, low_ref, high_ref, west2_ref, east2_ref, low2_ref, high2_ref,
    d0_ref, q_ref, d0_up_ref, q_up_ref, u_ref, base_ref, own_ref, side_ref, ring_ref,
):
    nr, nl, width = v_ref.shape
    half = nr // 2
    sub = sub_index(width)
    lon = sub % 4
    lane = lax.broadcasted_iota(jnp.int32, (8, width), 1)
    lower = sub < 4
    has_low, has_high = flag_ref[0], flag_ref[1]

    def wr_row(i):
        return jnp.where(lower, wr_ref[i + 2], wr_ref[i + half + 2])

    def share(f, other):
        return other * reciprocal(f + other)

    def safe_share(f, other):
        return other * reciprocal(jnp.maximum(f + other, 1e-30))

    def pick(ref_w, ref_e, i):
        return jnp.where(
            lower,
            jnp.where(lon < 2, ref_w[i], ref_e[i]),
            jnp.where(lon < 2, ref_w[i + half], ref_e[i + half]),
        )

    def north_of(f):
        return jnp.where(lane < width - 1, lat_next(f), 0.0)

    def south_of(f):
        return jnp.where(lane > 0, lat_prev(f), 0.0)

    def coefficients(ref, f, wr, wr_up, wr_down, shares):
        scaled = (2.0 * RELAX_RATE) * f
        weighted = scaled * wr
        for n in range(4):
            ref(n, weighted * shares[n])
        ref(4, scaled * (shares[4] * (wr_up - wr) + shares[5] * (wr_down - wr)))

    def prepare_row(i, s_up, f_up):
        f = fluid_ref[i + 1]
        f_down = fluid_ref[i]
        f_side = fluid_side_ref[i]
        wr, wr_up, wr_down = wr_row(i), wr_row(i + 1), wr_row(i - 1)
        shares = [
            share(f, jnp.where(lon == 3, f_side, lon_next(f))),
            share(f, jnp.where(lon == 0, f_side, lon_prev(f))),
            share(f, north_of(f)),
            share(f, south_of(f)),
            share(f, f_up),
            share(f, f_down),
        ]

        def store_own(n, value):
            own_ref[n, i] = value

        coefficients(store_own, f, wr, wr_up, wr_down, shares)
        scaled = (-0.5 * 2.0 * RELAX_RATE) * f
        for n in range(6):
            u_ref[n, i] = scaled * (shares[n] * shares[n])
        base_ref[i] = pack(
            m_ref[i] - (0.5 * PRIOR_WEIGHT) * v_ref[i],
            m_ref[i + half] - (0.5 * PRIOR_WEIGHT) * v_ref[i + half],
        )
        f_far = jnp.exp(-pick(west2_ref, east2_ref, i))
        edge = jnp.where(lon < 2, f_far, f)
        other = jnp.where(lon < 2, f, f_far)
        up_side = fluid_side_ref[jnp.minimum(i + 1, half - 1)]
        down_side = fluid_side_ref[jnp.maximum(i - 1, 0)]
        seam_up = swap_halves(fluid_side_ref[0])
        seam_down = swap_halves(fluid_side_ref[half - 1])
        corner_low = has_low * jnp.exp(-jnp.where(lon < 2, west2_ref[nr], east2_ref[nr]))
        corner_high = has_high * jnp.exp(-jnp.where(lon < 2, west2_ref[nr + 1], east2_ref[nr + 1]))
        up_side = jnp.where(i == half - 1, jnp.where(lower, seam_up, corner_high), up_side)
        down_side = jnp.where(i == 0, jnp.where(lower, corner_low, seam_down), down_side)
        side_shares = [
            share(f_side, other),
            share(f_side, edge),
            share(f_side, north_of(f_side)),
            share(f_side, south_of(f_side)),
            share(f_side, up_side),
            share(f_side, down_side),
        ]

        def store_side(n, value):
            side_ref[n, i] = value

        coefficients(store_side, f_side, wr, wr_up, wr_down, side_shares)
        dwr = wr_up - wr
        for c in range(3):
            s0 = field_ref[c, i + 1]
            s1 = next_ref[c, i]
            s0_side = field_side_ref[c, i]
            s1_side = jnp.where(
                lower,
                jnp.where(lon < 2, west_ref[c, i], east_ref[c, i]),
                jnp.where(lon < 2, west_ref[c, i + half], east_ref[c, i + half]),
            )
            cut = s0_side - s0
            east = jnp.where(lon == 3, s0_side, lon_next(s0)) - s0
            north = lat_next(s0) - s0
            cut1 = s1_side - s1
            east1 = jnp.where(lon == 3, s1_side, lon_next(s1)) - s1
            north1 = lat_next(s1) - s1
            for n, (first, second) in enumerate(((east, east1), (cut, cut1), (north, north1))):
                d0_ref[n, c, i] = first
                q_ref[n, c, i] = wr * (first + second)
            up = field_ref[c, i + 2] - s0
            d0_up_ref[c, i + 1] = up
            q_up_ref[c, i + 1] = dwr * (up + (s_up[c] - s1))

    def loop(i, carry):
        prepare_row(i, [next_ref[c, i + 1] for c in range(3)], fluid_ref[i + 2])
        return carry

    lax.fori_loop(0, half - 1, loop, 0)
    top_rows = [pack(next_ref[c, 0][4:8, :], high_ref[c]) for c in range(3)]
    prepare_row(half - 1, top_rows, fluid_ref[half + 1])
    dwr_low = wr_row(0) - wr_row(-1)
    for c in range(3):
        low_row = pack(low_ref[c], next_ref[c, half - 1][0:4, :])
        up = field_ref[c, 1] - field_ref[c, 0]
        d0_up_ref[c, 0] = up
        q_up_ref[c, 0] = dwr_low * (up + (next_ref[c, 0] - low_row))
    ring = jnp.where(lower, fluid_ref[0], fluid_ref[half + 1])
    inner = jnp.where(lower, fluid_ref[1], fluid_ref[half])
    far = pack(has_low * jnp.exp(-low2_ref[...]), has_high * jnp.exp(-high2_ref[...]))
    corner_w = jnp.where(
        lower, has_low * jnp.exp(-west2_ref[nr]), has_high * jnp.exp(-west2_ref[nr + 1])
    )
    corner_e = jnp.where(
        lower, has_low * jnp.exp(-east2_ref[nr]), has_high * jnp.exp(-east2_ref[nr + 1])
    )
    far = jnp.where(lower, flag_ref[2] * far, flag_ref[3] * far)
    wr_ring = jnp.where(lower, wr_ref[1], wr_ref[nr + 2])
    wr_in = jnp.where(lower, wr_ref[2], wr_ref[nr + 1])
    wr_far = jnp.where(lower, wr_ref[0], wr_ref[nr + 3])
    ring_shares = [
        safe_share(ring, jnp.where(lon == 3, corner_e, lon_next(ring))),
        safe_share(ring, jnp.where(lon == 0, corner_w, lon_prev(ring))),
        safe_share(ring, north_of(ring)),
        safe_share(ring, south_of(ring)),
        safe_share(ring, far),
        safe_share(ring, inner),
    ]

    def store_ring(n, value):
        ring_ref[n] = value

    coefficients(store_ring, ring, wr_ring, wr_far, wr_in, ring_shares)


def gradient_kernel(
    v_ref, pred_ref, obs_ref, wt_ref, k_ref,
    d0_ref, q_ref, d0_up_ref, q_up_ref, u_ref, base_ref, own_ref, side_ref, ring_ref,
    new_ref, half_ref, misfit_ref,
    sa_ref, d_ref,
    *, scale,
):
    nr, nl, width = v_ref.shape
    half = nr // 2
    sites = k_ref.shape[1]
    sub = sub_index(width)
    lon = sub % 4
    lower = sub < 4

    predicted = lax.fori_loop(
        1, pred_ref.shape[0], lambda n, acc: acc + pred_ref[n], pred_ref[0]
    )
    weight = wt_ref[...]
    weighted = weight * (predicted * scale - obs_ref[...])
    squares = jnp.sum(weighted * weighted, axis=1, keepdims=True)
    squares = jnp.sum(squares, axis=0, keepdims=True)
    misfit_ref[...] = squares * (1.0 / (3 * sites))
    pulled = (weight * weighted) * scale
    pulled = jnp.concatenate([pulled, jnp.zeros((5, sites), F32)], axis=0)
    for col in range(COLS):
        spread = jnp.dot(
            pulled, k_ref[col], precision=lax.Precision.HIGHEST, preferred_element_type=F32
        )
        for c in range(3):
            sa_ref[c, col : col + 1, :] = spread[c : c + 1, :]

    for c in range(3):
        x = sa_ref[c]

        def window(start):
            return jnp.where(
                lower,
                x if start == 0 else pltpu.roll(x, 8 - start, 0),
                x if start == 4 else pltpu.roll(x, (4 - start) % 8, 0),
            )

        own = window(2)
        east = window(3)
        west = window(1)
        outside = jnp.where(lon < 2, west, east)
        d_ref[0, c] = east - own
        d_ref[1, c] = west - own
        d_ref[2, c] = lat_next(own) - own
        d_ref[3, c] = lat_prev(own) - own
        d_ref[4, c] = own
        d_ref[5, c] = jnp.where(lon < 2, own, window(4)) - outside
        d_ref[6, c] = jnp.where(lon < 2, window(0), own) - outside
        d_ref[7, c] = lat_next(outside) - outside
        d_ref[8, c] = lat_prev(outside) - outside
        d_ref[9, c] = outside

    def change(coeff, first):
        out = []
        for c in range(3):
            total = coeff(0) * d_ref[first, c]
            for n in range(1, 5):
                total = total + coeff(n) * d_ref[first + n, c]
            out.append(total)
        return out

    def own_row(i):
        return change(lambda n: own_ref[n, i], 0)

    ring = change(lambda n: ring_ref[n], 0)
    e_first = own_row(0)
    e_last = own_row(half - 1)
    e_low = [jnp.where(lower, ring[c], swap_halves(e_last[c])) for c in range(3)]
    e_high = [jnp.where(lower, swap_halves(e_first[c]), ring[c]) for c in range(3)]

    def up_product(k, e_a, e_b):
        total = None
        for c in range(3):
            term = q_up_ref[c, k] * d_ref[4, c] + d0_up_ref[c, k] * (e_b[c] - e_a[c])
            total = term if total is None else total + term
        return total

    def finish_row(i, e, e_up, p_down):
        outside = change(lambda n: side_ref[n, i], 5)
        p_up = up_product(i + 1, e, e_up)
        p_east = p_cut = p_north = None
        for c in range(3):
            to_side = outside[c] - e[c]
            to_east = jnp.where(lon == 3, outside[c], lon_next(e[c])) - e[c]
            to_north = lat_next(e[c]) - e[c]
            t_east = q_ref[0, c, i] * d_ref[0, c] + d0_ref[0, c, i] * to_east
            t_cut = q_ref[1, c, i] * d_ref[1, c] + d0_ref[1, c, i] * to_side
            t_north = q_ref[2, c, i] * d_ref[2, c] + d0_ref[2, c, i] * to_north
            p_east = t_east if p_east is None else p_east + t_east
            p_cut = t_cut if p_cut is None else p_cut + t_cut
            p_north = t_north if p_north is None else p_north + t_north
        p_west = jnp.where(lon == 0, p_cut, lon_prev(p_east))
        total = base_ref[i] + u_ref[0, i] * p_east + u_ref[1, i] * p_west
        total = total + u_ref[2, i] * p_north + u_ref[3, i] * lat_prev(p_north)
        total = total + u_ref[4, i] * p_up + u_ref[5, i] * p_down
        half_ref[i] = total[0:4, :]
        half_ref[i + half] = total[4:8, :]
        new_ref[i] = v_ref[i] + total[0:4, :]
        new_ref[i + half] = v_ref[i + half] + total[4:8, :]
        return p_up

    def loop(i, carry):
        e, p_down = carry
        e_up = own_row(i + 1)
        p_up = finish_row(i, e, e_up, p_down)
        return e_up, p_up

    e, p_down = lax.fori_loop(
        0, half - 1, loop, (e_first, up_product(0, e_low, e_first))
    )
    finish_row(half - 1, e, e_high, p_down)


def call(kernel, out_shapes, in_smem, arity, scratch=(), flops=1, name=None):
    vmem = pl.BlockSpec(memory_space=pltpu.VMEM)
    smem = pl.BlockSpec(memory_space=pltpu.SMEM)
    return pl.pallas_call(
        kernel,
        out_shape=[jax.ShapeDtypeStruct(s, F32) for s in out_shapes],
        in_specs=[smem] * in_smem + [vmem] * (arity - in_smem),
        out_specs=[vmem] * len(out_shapes),
        scratch_shapes=[pltpu.VMEM(s, F32) for s in scratch],
        compiler_params=pltpu.CompilerParams(vmem_limit_bytes=VMEM_LIMIT),
        cost_estimate=pl.CostEstimate(flops=flops, bytes_accessed=1 << 20, transcendentals=0),
        name=name,
    )


def body(
    logvisc, momentum, displacement, ice_history, load_steps, site_cells, observed, site_weight
):
    nr, nl, nlat = logvisc.shape
    own_sites = site_cells.shape[0]
    lon_n = lax.axis_size("lon")
    rad_n = lax.axis_size("rad")
    total_rad = nr * rad_n
    total_lon = nl * lon_n
    sites = own_sites * lon_n
    devices = lon_n * rad_n
    half = nr // 2
    scale = 1.0 / math.sqrt(total_lon * nlat)
    rad_at = lax.axis_index("rad")
    lon_at = lax.axis_index("lon")

    packet = jnp.concatenate(
        [site_cells.astype(F32)[None, :], observed, site_weight], axis=0
    )
    gathered = lax.all_to_all(
        jnp.broadcast_to(packet[None], (lon_n,) + packet.shape), "lon", 0, 0
    )

    fields = jnp.concatenate([logvisc[None], displacement], axis=0)
    eastward = [(i, (i + 1) % lon_n) for i in range(lon_n)]
    westward = [(t, s) for s, t in eastward]
    upward = [(i, i + 1) for i in range(rad_n - 1)]
    downward = [(t, s) for s, t in upward]
    west = lax.ppermute(fields[:, :, nl - 1 : nl, :], "lon", eastward)
    east = lax.ppermute(fields[:, :, 0:1, :], "lon", westward)
    low = lax.ppermute(
        jnp.concatenate([fields[:, nr - 1], logvisc[None, nr - 2]], axis=0), "rad", upward
    )
    high = lax.ppermute(
        jnp.concatenate([fields[:, 0], logvisc[None, 1]], axis=0), "rad", downward
    )

    layers = (rad_at * nr - 2 + jnp.arange(nr + 4)).astype(F32)
    wr = jnp.exp(4.0 * (layers - (total_rad - 1)) / total_rad)
    flags = jnp.stack(
        [rad_at > 0, rad_at < rad_n - 1, rad_at * nr > 1, rad_at * nr + nr + 1 < total_rad]
    ).astype(F32)

    lat_angle = math.pi * (jnp.arange(nlat).astype(F32) + 0.5) / nlat
    lat_rows = jnp.stack([jnp.cos(lat_angle), jnp.sin(lat_angle)])
    col_index = (lon_at * nl - 2 + jnp.arange(COLS) + total_lon) % total_lon
    col_angle = 2.0 * math.pi * col_index.astype(F32) / total_lon
    cells = gathered[:, 0].reshape(sites)
    cell_index = cells.astype(jnp.int32)
    lon_index = cell_index // nlat
    site_angle = math.pi * ((cell_index - lon_index * nlat).astype(F32) + 0.5) / nlat
    site_phi = 2.0 * math.pi * lon_index.astype(F32) / total_lon
    columns = jnp.concatenate(
        [
            (-2.0 * jnp.cos(site_angle))[:, None],
            (-2.0 * jnp.sin(site_angle))[:, None],
            jnp.cos(site_phi)[:, None] * jnp.cos(col_angle)[None, :]
            + jnp.sin(site_phi)[:, None] * jnp.sin(col_angle)[None, :],
        ],
        axis=1,
    )
    (weights,) = call(
        weights_kernel, [(COLS, sites, nlat)], 0, 2, flops=20000000, name="site_weights"
    )(columns, lat_rows)
    obs_all = gathered[:, 1:4].transpose(1, 0, 2).reshape(3, sites)
    wt_all = gathered[:, 4:7].transpose(1, 0, 2).reshape(3, sites)

    row = (8, nlat)
    (
        fluid, field, fluid_side, field_side, state, to_west, to_east, to_low, to_high, partial,
    ) = call(
        forward_kernel,
        [
            (half + 2,) + row,
            (3, half + 2) + row,
            (half,) + row,
            (3, half) + row,
            (3, half) + row,
            (3, nr, 1, nlat),
            (3, nr, 1, nlat),
            (3, nl, nlat),
            (3, nl, nlat),
            (devices, 3, sites),
        ],
        3,
        11,
        scratch=[(half,) + row, (half,) + row, (half,) + row, (half + 1,) + row, (6,) + row],
        flops=20000000,
        name="forward",
    )(
        load_steps, wr, flags, logvisc, displacement, west, east, low, high, ice_history, weights
    )

    predicted = lax.all_to_all(partial, ("lon", "rad"), 0, 0)

    west_next = lax.ppermute(to_east, "lon", eastward)
    east_next = lax.ppermute(to_west, "lon", westward)
    corners_w = jnp.stack([low[0, 0:1], high[0, 0:1]])
    corners_e = jnp.stack([low[0, nl - 1 : nl], high[0, nl - 1 : nl]])
    west_far = lax.ppermute(
        jnp.concatenate([logvisc[:, nl - 2 : nl - 1], corners_e]), "lon", eastward
    )
    east_far = lax.ppermute(jnp.concatenate([logvisc[:, 1:2], corners_w]), "lon", westward)
    low_next = lax.ppermute(to_high, "rad", upward)
    high_next = lax.ppermute(to_low, "rad", downward)

    prepared = call(
        prepare_kernel,
        [
            (3, 3, half) + row,
            (3, 3, half) + row,
            (3, half + 1) + row,
            (3, half + 1) + row,
            (6, half) + row,
            (half,) + row,
            (5, half) + row,
            (5, half) + row,
            (5,) + row,
        ],
        2,
        17,
        flops=40000000,
        name="prepare",
    )(
        wr, flags, logvisc, momentum, fluid, field, fluid_side, field_side, state,
        west_next, east_next, low_next, high_next, west_far, east_far, low[4], high[4],
    )

    new_logvisc, half_momentum, misfit = call(
        functools.partial(gradient_kernel, scale=scale),
        [(nr, nl, nlat), (nr, nl, nlat), (1, 1)],
        0,
        14,
        scratch=[(3,) + row, (10, 3) + row],
        flops=20000000,
        name="gradient",
    )(logvisc, predicted, obs_all, wt_all, weights, *prepared)
    return (new_logvisc, half_momentum, misfit.reshape(1))


def solution(mesh):
    return jax.shard_map(
        body,
        mesh=mesh,
        in_specs=(
            P("rad", "lon", None),
            P("rad", "lon", None),
            P(None, "rad", "lon", None),
            P(None, "lon", None),
            P(),
            P("lon"),
            P(None, "lon"),
            P(None, "lon"),
        ),
        out_specs=(P("rad", "lon", None), P("rad", "lon", None), P()),
        check_vma=False,
    )
```

```python
import functools
import math

import jax
import jax.numpy as jnp
from jax import lax
from jax.experimental import pallas as pl
from jax.experimental.pallas import tpu as pltpu
from jax.sharding import PartitionSpec as P

RELAX_RATE = 0.05
KERNEL_WIDTH = 0.1
KERNEL_WAVE = 40.0
PRIOR_WEIGHT = 0.1
COLS = 8
F32 = jnp.float32
BF16 = jnp.bfloat16
VMEM_LIMIT = 40 * 1024 * 1024


def reciprocal(x):
    r = pl.reciprocal(x, approx=True)
    return r * (2.0 - x * r)


def lat_next(x):
    return pltpu.roll(x, x.shape[1] - 1, 1)


def lat_prev(x):
    return pltpu.roll(x, 1, 1)


def lon_next(x):
    return pltpu.roll(x, 7, 0)


def lon_prev(x):
    return pltpu.roll(x, 1, 0)


def swap_halves(x):
    return pltpu.roll(x, 4, 0)


def pack(low, high):
    return jnp.concatenate([low, high], axis=0)


class Shape:
    def __init__(self, nr, width, rad_n):
        self.nr, self.width, self.half = nr, width, nr // 2
        sub = lax.broadcasted_iota(jnp.int32, (8, width), 0)
        lane = lax.broadcasted_iota(jnp.int32, (8, width), 1)
        self.lon = sub % 4
        self.lower = sub < 4
        self.upper = sub >= 4
        self.western = self.lon < 2
        self.not_last = lane < width - 1
        self.not_first = lane > 0
        self.rate = 4.0 / (nr * rad_n)
        at = lax.axis_index("rad")
        self.has_low = (at > 0).astype(F32)
        self.has_high = (at < rad_n - 1).astype(F32)
        layer = jnp.where(self.lower, 0, self.half) + (at * nr - (nr * rad_n - 1))
        self.first_weight = jnp.exp(layer.astype(F32) * self.rate)

    def step(self, i):
        return math.exp(self.rate * i)

    def sides(self, west, east):
        return jnp.where(
            self.lower,
            jnp.where(self.western, west[0], east[0]),
            jnp.where(self.western, west[1], east[1]),
        )


def face(a, b):
    return 2.0 * a * b * reciprocal(a + b)


def sin_pi(u):
    z = u * u
    p = 0.0772201269865036
    p = p * z - 0.5980451703071594
    p = p * z + 2.5500314235687256
    p = p * z - 5.1677069664001465
    p = p * z + 3.141592502593994
    return p * u


def site_kernel(d):
    turns = d * (KERNEL_WAVE / (2.0 * math.pi))
    s = sin_pi(turns - jnp.round(turns))
    return (reciprocal(1.0 + d * (1.0 / KERNEL_WIDTH)) + 0.5) - s * s


def message_kernel(
    steps_ref, v_ref, s_ref, ice_ref, cells_ref, obs_ref, wt_ref,
    west_ref, east_ref, west2_ref, east2_ref, low_ref, high_ref, packet_ref,
):
    nr, nl, width = v_ref.shape
    packet = jnp.concatenate(
        [
            cells_ref[...].astype(F32),
            obs_ref[...],
            wt_ref[...],
            jnp.zeros((1, obs_ref.shape[1]), F32),
        ],
        axis=0,
    )
    for n in range(packet_ref.shape[0]):
        packet_ref[n] = packet

    def field(n, r):
        return v_ref[r] if n == 0 else s_ref[n - 1, r]

    for r in range(nr):
        for n in range(4):
            x = field(n, r)
            west_ref[n * nr + r] = x[0:1, :]
            east_ref[n * nr + r] = x[nl - 1 : nl, :]
            west2_ref[n * nr + r] = x[1:2, :]
            east2_ref[n * nr + r] = x[nl - 2 : nl - 1, :]
    load = ice_ref[steps_ref[0]]
    west_ref[4 * nr] = load[0:1, :]
    east_ref[4 * nr] = load[nl - 1 : nl, :]
    for n in range(4):
        low_ref[n] = field(n, 0)
        low_ref[4 + n] = field(n, 1)
        high_ref[n] = field(n, nr - 1)
        high_ref[4 + n] = field(n, nr - 2)


def weights_kernel(gathered_ref, high_ref, low_ref, data_ref, rows_ref, *, total_lon):
    devices, _, own = gathered_ref.shape
    sites = high_ref.shape[1]
    width = high_ref.shape[2]
    for d in range(devices):
        data_ref[:, d * own : (d + 1) * own] = gathered_ref[d]
    cells = data_ref[0:1, :]
    lon = jnp.floor((cells + 0.5) * (1.0 / width))
    theta = (cells - lon * width + 0.5) * (1.0 / width)
    phi = lon * (1.0 / total_lon)

    def sin_whole(t):
        return sin_pi(jnp.minimum(t, 1.0 - t))

    def circle(t):
        u = t - jnp.round(t)
        s = sin_pi(u)
        y = jnp.abs(2.0 * u)
        wave = sin_pi(jnp.minimum(y, 1.0 - y))
        return 1.0 - 2.0 * s * s, jnp.where(u < 0, -wave, wave)

    site_cos, site_sin = circle(phi)
    first = lax.axis_index("lon") * 4 - 2 + total_lon
    col = (lax.broadcasted_iota(jnp.int32, (COLS, sites), 0) + first).astype(F32)
    turns = col * (1.0 / total_lon)
    col_cos, col_sin = circle(turns - jnp.floor(turns))
    rows_ref[0:8, :] = col_cos * site_cos + col_sin * site_sin
    rows_ref[8:9, :] = -2.0 * sin_pi(0.5 - theta)
    rows_ref[9:10, :] = -2.0 * sin_whole(theta)
    rows_ref[10:16, :] = jnp.zeros((6, sites), F32)
    columns = jnp.transpose(rows_ref[...])
    lat = (lax.broadcasted_iota(jnp.int32, (16, width), 1).astype(F32) + 0.5) * (1.0 / width)
    cos_lat = sin_pi(0.5 - lat)
    sin_lat = sin_whole(lat)
    for at in range(0, sites, 16):
        part = columns[at : at + 16, :]
        a = 2.0 + part[:, 8:9] * cos_lat
        b = part[:, 9:10] * sin_lat
        for n in range(COLS):
            k = site_kernel(a + b * part[:, n : n + 1])
            high = k.astype(BF16)
            high_ref[n, at : at + 16, :] = high
            low_ref[n, at : at + 16, :] = (k - high.astype(F32)).astype(BF16)


def two_parts(x):
    high = x.astype(BF16).astype(F32)
    return jnp.concatenate([high, x - high], axis=0).astype(BF16)


def product(x, high, low, contract):
    dims = (((1,), (contract,)), ((), ()))
    parts = two_parts(x)
    both = lax.dot_general(parts, high, dims, preferred_element_type=F32)
    rest = lax.dot_general(parts, low, dims, preferred_element_type=F32)
    return both[0:8, :] + (both[8:16, :] + rest[0:8, :])


class Rows:
    def __init__(self, half):
        self.fluid = 1
        self.field = [half + 3 + c * (half + 2) for c in range(3)]
        self.next = [4 * (half + 2) + c * half for c in range(3)]
        self.count = 4 * (half + 2) + 3 * half


def interior_kernel(v_ref, s_ref, out_ref, *, rad_n):
    nr, nl, width = v_ref.shape
    shape = Shape(nr, width, rad_n)
    half = shape.half
    at = Rows(half)
    for i in range(half):
        out_ref[at.fluid + i] = jnp.exp(-pack(v_ref[i], v_ref[i + half]))
        for c in range(3):
            out_ref[at.field[c] + i] = pack(s_ref[c, i], s_ref[c, i + half])

    def fluid(i):
        return out_ref[at.fluid + i]

    for base in [at.fluid] + at.field:
        out_ref[base - 1] = swap_halves(out_ref[base + half - 1])
        out_ref[base + half] = swap_halves(out_ref[base])
    seam = jnp.where(shape.upper, face(fluid(-1), fluid(0)), 0.0)
    carry = [seam * (out_ref[at.field[c]] - out_ref[at.field[c] - 1]) for c in range(3)]
    for i in range(half):
        f = fluid(i)
        h_east = jnp.where(shape.lon < 3, face(f, lon_next(f)), 0.0)
        h_north = jnp.where(shape.not_last, face(f, lat_next(f)), 0.0)
        h_up = face(f, fluid(i + 1))
        if i == half - 1:
            h_up = jnp.where(shape.lower, h_up, 0.0)
        for c in range(3):
            s = out_ref[at.field[c] + i]
            east = h_east * (lon_next(s) - s)
            north = h_north * (lat_next(s) - s)
            up = h_up * (out_ref[at.field[c] + i + 1] - s)
            total = (east - lon_prev(east)) + (north - lat_prev(north)) + (up - carry[c])
            out_ref[at.next[c] + i] = s + RELAX_RATE * total
            carry[c] = up


def forward_kernel(
    steps_ref, rows_ref, west_ref, east_ref, low_ref, high_ref, ice_ref, k_high_ref, k_low_ref,
    pred_ref, next_ref, surf_ref, *, rad_n,
):
    width = rows_ref.shape[2]
    nr = west_ref.shape[0] // 4
    shape = Shape(nr, width, rad_n)
    half = shape.half
    at = Rows(half)
    lower, lon = shape.lower, shape.lon
    ends = (lon == 0) | (lon == 3)

    def fluid(i):
        return rows_ref[at.fluid + i]

    ring = pack(shape.has_low * jnp.exp(-low_ref[0]), shape.has_high * jnp.exp(-high_ref[0]))
    h_ring = face(ring, jnp.where(lower, fluid(0), fluid(half - 1)))
    load = ice_ref[steps_ref[0]] * (1.0 - shape.has_high)
    load = pack(jnp.zeros_like(load), load)
    h_cuts = []
    for i in range(half):

        def side(n):
            return shape.sides(
                (west_ref[n * nr + i], west_ref[n * nr + i + half]),
                (east_ref[n * nr + i], east_ref[n * nr + i + half]),
            )

        h_cut = jnp.where(ends, face(fluid(i), jnp.exp(-side(0))), 0.0)
        h_cuts.append(h_cut)
        for c in range(3):
            s = rows_ref[at.field[c] + i]
            total = h_cut * (side(1 + c) - s)
            if i in (0, half - 1):
                beyond = h_ring * (pack(low_ref[1 + c], high_ref[1 + c]) - s)
                if i == 0:
                    total = total + jnp.where(lower, beyond, 0.0)
                if i == half - 1:
                    total = total + jnp.where(lower, 0.0, beyond)
            s1 = rows_ref[at.next[c] + i] + RELAX_RATE * total
            if c == 0 and i == half - 1:
                s1 = s1 - load
            next_ref[c, i] = s1

    zero = jnp.zeros((8, width), F32)
    column, east, north, cut = [zero] * 3, [zero] * 3, [zero] * 3, [zero] * 3
    below = [None] * 3
    for i in range(half):
        f = fluid(i)
        weight = shape.step(i)
        g_east = weight * face(f, lon_next(f))
        g_north = weight * face(f, lat_next(f))
        g_cut = weight * h_cuts[i]
        g_low = (RELAX_RATE * (weight - shape.step(i - 1))) * face(fluid(i - 1), f)
        if i == 0:
            g_low = jnp.where(lower, 0.0, g_low)
        for c in range(3):
            s = next_ref[c, i]
            if i == 0:
                below[c] = swap_halves(next_ref[c, half - 1])
            column[c] = column[c] + (weight * s - g_low * (s - below[c]))
            east[c] = east[c] + g_east * (lon_next(s) - s)
            north[c] = north[c] + g_north * (lat_next(s) - s)
            cut[c] = cut[c] + g_cut * s
            below[c] = s
    top = shape.step(half - 1)
    g_ring = (RELAX_RATE * h_ring) * jnp.where(
        lower, shape.step(-1) - 1.0, shape.step(half) - top
    )
    for c in range(3):
        inner = jnp.where(lower, next_ref[c, 0], next_ref[c, half - 1])

        def folded(x):
            x = shape.first_weight * x
            return x + swap_halves(x)

        sum_east = jnp.where(lon < 3, folded(east[c]), 0.0)
        sum_north = jnp.where(shape.not_last, folded(north[c]), 0.0)
        sum_cut = folded(cut[c])
        own = folded(column[c] + g_ring * inner)
        spread = (sum_east - lon_prev(sum_east)) + (sum_north - lat_prev(sum_north)) - sum_cut
        own = own + RELAX_RATE * spread
        if c == 0:
            second = ice_ref[steps_ref[1]] * (1.0 - shape.has_high)
            own = own - pack(second, second)
        surf_ref[0, c : c + 1, :] = RELAX_RATE * sum_cut[0:1, :]
        for col in range(4):
            surf_ref[col + 1, c : c + 1, :] = own[col : col + 1, :]
        surf_ref[5, c : c + 1, :] = RELAX_RATE * sum_cut[3:4, :]
    total = None
    for col in range(6):
        surf_ref[col, 3:8, :] = jnp.zeros((5, width), F32)
        term = product(surf_ref[col], k_high_ref[col + 1], k_low_ref[col + 1], 1)
        total = term if total is None else total + term
    for n in range(pred_ref.shape[0]):
        pred_ref[n] = total[0:3, :]


EAST, CUT, NORTH, UP = 0, 1, 2, 3
D0, Q, U, BASE, OWN, SIDE, BLOCK = 0, 12, 24, 30, 31, 36, 41
RING, LAST, D0_LOW, Q_LOW, ENDS = 0, 5, 10, 13, 16


def prepare_kernel(
    steps_ref, v_ref, m_ref, s_ref, ice_ref, west_ref, east_ref, west2_ref, east2_ref, low_ref,
    high_ref, corner_low_ref, corner_high_ref, blocks_ref, ends_ref,
    fluid_ref, field_ref, fluid_side_ref, field_side_ref, next_ref, next_side_ref, out_ref, sems,
    *, rad_n,
):
    nr, nl, width = v_ref.shape
    shape = Shape(nr, width, rad_n)
    half = shape.half
    lower, lon, western = shape.lower, shape.lon, shape.western

    def share(f, other):
        return other * reciprocal(f + other)

    def safe_share(f, other):
        return other * reciprocal(jnp.maximum(f + other, 1e-30))

    def north_of(f):
        return jnp.where(shape.not_last, lat_next(f), 0.0)

    def south_of(f):
        return jnp.where(shape.not_first, lat_prev(f), 0.0)

    def two(ref, n, i):
        return ref[n * nr + i], ref[n * nr + i + half]

    def corner(ref, n):
        return jnp.where(western, ref[n, 0], ref[n, 1])

    def weight(i):
        return shape.step(i) * shape.first_weight

    for i in range(half):
        fluid_ref[i + 1] = jnp.exp(-pack(v_ref[i], v_ref[i + half]))
        fluid_side_ref[i + 1] = jnp.exp(-shape.sides(two(west_ref, 0, i), two(east_ref, 0, i)))
        for c in range(3):
            field_ref[c, i + 1] = pack(s_ref[c, i], s_ref[c, i + half])
            field_side_ref[c, i + 1] = shape.sides(
                two(west_ref, 1 + c, i), two(east_ref, 1 + c, i)
            )
    ring = pack(shape.has_low * jnp.exp(-low_ref[0]), shape.has_high * jnp.exp(-high_ref[0]))
    ring_side = jnp.where(
        lower,
        shape.has_low * jnp.exp(-corner(corner_low_ref, 0)),
        shape.has_high * jnp.exp(-corner(corner_high_ref, 0)),
    )
    ring_field = [pack(low_ref[1 + c], high_ref[1 + c]) for c in range(3)]
    ring_field_side = [
        jnp.where(lower, corner(corner_low_ref, 1 + c), corner(corner_high_ref, 1 + c))
        for c in range(3)
    ]

    def close(ref, ring):
        ref[0] = jnp.where(lower, ring, swap_halves(ref[half]))
        ref[half + 1] = jnp.where(lower, swap_halves(ref[1]), ring)

    close(fluid_ref, ring)
    close(fluid_side_ref, ring_side)
    for c in range(3):
        close(field_ref.at[c], ring_field[c])
        close(field_side_ref.at[c], ring_field_side[c])

    def coefficients(ref, first, f, shares, here, above, below):
        scaled = (2.0 * RELAX_RATE) * f
        weighted = scaled * here
        for n in range(4):
            ref[first + n] = weighted * shares[n]
        ref[first + 4] = scaled * (shares[4] * (above - here) + shares[5] * (below - here))

    def relaxed(f, shares, s, others):
        total = shares[0] * (others[0] - s)
        for n in range(1, 6):
            total = total + shares[n] * (others[n] - s)
        return s + (2.0 * RELAX_RATE) * (f * total)

    outer = pack(shape.has_low * jnp.exp(-low_ref[4]), shape.has_high * jnp.exp(-high_ref[4]))
    inner = jnp.where(lower, fluid_ref[1], fluid_ref[half])
    ring_shares = [
        safe_share(ring, jnp.where(lon == 3, ring_side, lon_next(ring))),
        safe_share(ring, jnp.where(lon == 0, ring_side, lon_prev(ring))),
        safe_share(ring, north_of(ring)),
        safe_share(ring, south_of(ring)),
        safe_share(ring, outer),
        safe_share(ring, inner),
    ]
    coefficients(
        ends_ref,
        RING,
        ring,
        ring_shares,
        jnp.where(lower, weight(-1), weight(half)),
        jnp.where(lower, weight(-2), weight(half + 1)),
        jnp.where(lower, weight(0), weight(half - 1)),
    )
    ring_next = []
    for c in range(3):
        s, s_side = ring_field[c], ring_field_side[c]
        others = [
            jnp.where(lon == 3, s_side, lon_next(s)),
            jnp.where(lon == 0, s_side, lon_prev(s)),
            lat_next(s),
            lat_prev(s),
            pack(low_ref[5 + c], high_ref[5 + c]),
            jnp.where(lower, field_ref[c, 1], field_ref[c, half]),
        ]
        ring_next.append(relaxed(ring, ring_shares, s, others))
    load = ice_ref[steps_ref[0]]
    load = (1.0 - shape.has_high) * pack(jnp.zeros_like(load), load)
    load_side = jnp.where(western, west_ref[4 * nr], east_ref[4 * nr])
    load_side = (1.0 - shape.has_high) * jnp.where(lower, 0.0, load_side)

    def first_pass(i):
        f, f_side = fluid_ref[i + 1], fluid_side_ref[i + 1]
        here, above, below = weight(i), weight(i + 1), weight(i - 1)
        shares = [
            share(f, jnp.where(lon == 3, f_side, lon_next(f))),
            share(f, jnp.where(lon == 0, f_side, lon_prev(f))),
            share(f, north_of(f)),
            share(f, south_of(f)),
            share(f, fluid_ref[i + 2]),
            share(f, fluid_ref[i]),
        ]
        coefficients(out_ref.at[i], OWN, f, shares, here, above, below)
        scaled = (-0.5 * 2.0 * RELAX_RATE) * f
        for n in range(6):
            out_ref[i, U + n] = scaled * (shares[n] * shares[n])
        out_ref[i, BASE] = pack(
            m_ref[i] - (0.5 * PRIOR_WEIGHT) * v_ref[i],
            m_ref[i + half] - (0.5 * PRIOR_WEIGHT) * v_ref[i + half],
        )
        f_far = jnp.exp(-shape.sides(two(west2_ref, 0, i), two(east2_ref, 0, i)))
        side_shares = [
            share(f_side, jnp.where(western, f, f_far)),
            share(f_side, jnp.where(western, f_far, f)),
            share(f_side, north_of(f_side)),
            share(f_side, south_of(f_side)),
            share(f_side, fluid_side_ref[i + 2]),
            share(f_side, fluid_side_ref[i]),
        ]
        coefficients(out_ref.at[i], SIDE, f_side, side_shares, here, above, below)
        for c in range(3):
            s, s_side = field_ref[c, i + 1], field_side_ref[c, i + 1]
            s_far = shape.sides(two(west2_ref, 1 + c, i), two(east2_ref, 1 + c, i))
            others = [
                jnp.where(lon == 3, s_side, lon_next(s)),
                jnp.where(lon == 0, s_side, lon_prev(s)),
                lat_next(s),
                lat_prev(s),
                field_ref[c, i + 2],
                field_ref[c, i],
            ]
            out_ref[i, D0 + 3 * EAST + c] = others[0] - s
            out_ref[i, D0 + 3 * CUT + c] = s_side - s
            out_ref[i, D0 + 3 * NORTH + c] = others[2] - s
            out_ref[i, D0 + 3 * UP + c] = others[4] - s
            s1 = relaxed(f, shares, s, others)
            others = [
                jnp.where(western, s, s_far),
                jnp.where(western, s_far, s),
                lat_next(s_side),
                lat_prev(s_side),
                field_side_ref[c, i + 2],
                field_side_ref[c, i],
            ]
            s1_side = relaxed(f_side, side_shares, s_side, others)
            if c == 0 and i == half - 1:
                s1 = s1 - load
                s1_side = s1_side - load_side
            next_ref[c, i] = s1
            next_side_ref[c, i] = s1_side

    def second_pass(i):
        here = weight(i)
        step = weight(i + 1) - here
        for c in range(3):
            s, s_side = next_ref[c, i], next_side_ref[c, i]
            if i < half - 1:
                s_up = next_ref[c, i + 1]
            else:
                s_up = jnp.where(lower, swap_halves(next_ref[c, 0]), ring_next[c])
            ones = [jnp.where(lon == 3, s_side, lon_next(s)), s_side, lat_next(s)]
            for n, other in enumerate(ones):
                out_ref[i, Q + 3 * n + c] = here * (out_ref[i, D0 + 3 * n + c] + (other - s))
            out_ref[i, Q + 3 * UP + c] = step * (out_ref[i, D0 + 3 * UP + c] + (s_up - s))
        copies.append(
            pltpu.make_async_copy(out_ref.at[i], blocks_ref.at[i], sems.at[i])
        )
        copies[-1].start()

    copies = []
    for i in range(half):
        first_pass(i)
        if i > 0:
            second_pass(i - 1)
    second_pass(half - 1)
    for n in range(5):
        ends_ref[LAST + n] = out_ref[half - 1, OWN + n]
    step = weight(0) - weight(-1)
    for c in range(3):
        up = field_ref[c, 1] - field_ref[c, 0]
        low_state = jnp.where(lower, ring_next[c], swap_halves(next_ref[c, half - 1]))
        ends_ref[D0_LOW + c] = up
        ends_ref[Q_LOW + c] = step * (up + (next_ref[c, 0] - low_state))
    for copy in copies:
        copy.wait()


def gradient_kernel(
    v_ref, pred_ref, data_ref, k_high_ref, k_low_ref, ends_ref, blocks_ref,
    new_ref, half_ref, misfit_ref, sa_ref, d_ref, in_ref, sems, *, scale,
):
    nr, nl, width = v_ref.shape
    half = nr // 2
    sites = k_high_ref.shape[1]
    sub = lax.broadcasted_iota(jnp.int32, (8, width), 0)
    lon = sub % 4
    lower = sub < 4
    copies = [
        pltpu.make_async_copy(blocks_ref.at[i], in_ref.at[i], sems.at[i]) for i in range(half)
    ]
    for copy in copies:
        copy.start()

    predicted = pred_ref[0]
    for n in range(1, pred_ref.shape[0]):
        predicted = predicted + pred_ref[n]
    weight = data_ref[4:7, :]
    weighted = weight * (predicted * scale - data_ref[1:4, :])
    squares = jnp.sum(weighted * weighted, axis=1, keepdims=True)
    misfit_ref[...] = jnp.sum(squares, axis=0, keepdims=True) * (1.0 / (3 * sites))
    pulled = (weight * weighted) * scale
    pulled = jnp.concatenate([pulled, jnp.zeros((5, sites), F32)], axis=0)
    for col in range(COLS):
        spread = product(pulled, k_high_ref[col], k_low_ref[col], 0)
        for c in range(3):
            sa_ref[c, col : col + 1, :] = spread[c : c + 1, :]

    for c in range(3):
        x = sa_ref[c]

        def window(start):
            return jnp.where(
                lower,
                x if start == 0 else pltpu.roll(x, 8 - start, 0),
                x if start == 4 else pltpu.roll(x, (4 - start) % 8, 0),
            )

        own = window(2)
        east = window(3)
        west = window(1)
        outside = jnp.where(lon < 2, west, east)
        d_ref[0, c] = east - own
        d_ref[1, c] = west - own
        d_ref[2, c] = lat_next(own) - own
        d_ref[3, c] = lat_prev(own) - own
        d_ref[4, c] = own
        d_ref[5, c] = jnp.where(lon < 2, own, window(4)) - outside
        d_ref[6, c] = jnp.where(lon < 2, window(0), own) - outside
        d_ref[7, c] = lat_next(outside) - outside
        d_ref[8, c] = lat_prev(outside) - outside
        d_ref[9, c] = outside

    def change(ref, at, first):
        coeffs = [ref[at + n] for n in range(5)]
        out = []
        for c in range(3):
            total = coeffs[0] * d_ref[first, c]
            for n in range(1, 5):
                total = total + coeffs[n] * d_ref[first + n, c]
            out.append(total)
        return out

    def up_product(ref, d0, q, e_a, e_b):
        total = None
        for c in range(3):
            term = ref[q + c] * d_ref[4, c] + ref[d0 + c] * (e_b[c] - e_a[c])
            total = term if total is None else total + term
        return total

    ring = change(ends_ref, RING, 0)
    e_last = change(ends_ref, LAST, 0)
    copies[0].wait()
    e_first = e = change(in_ref.at[0], OWN, 0)
    e_low = [jnp.where(lower, ring[c], swap_halves(e_last[c])) for c in range(3)]
    p_down = up_product(ends_ref, D0_LOW, Q_LOW, e_low, e)
    for i in range(half):
        block = in_ref.at[i]
        if i < half - 1:
            copies[i + 1].wait()
            e_up = change(in_ref.at[i + 1], OWN, 0)
        else:
            e_up = [jnp.where(lower, swap_halves(e_first[c]), ring[c]) for c in range(3)]
        outside = change(block, SIDE, 5)
        p_up = up_product(block, D0 + 3 * UP, Q + 3 * UP, e, e_up)
        sums = [None, None, None]
        for c in range(3):
            others = [
                jnp.where(lon == 3, outside[c], lon_next(e[c])), outside[c], lat_next(e[c])
            ]
            slopes = [d_ref[0, c], d_ref[1, c], d_ref[2, c]]
            for n in range(3):
                term = block[Q + 3 * n + c] * slopes[n]
                term = term + block[D0 + 3 * n + c] * (others[n] - e[c])
                sums[n] = term if sums[n] is None else sums[n] + term
        p_east, p_cut, p_north = sums
        p_west = jnp.where(lon == 0, p_cut, lon_prev(p_east))
        total = block[BASE] + block[U] * p_east + block[U + 1] * p_west
        total = total + block[U + 2] * p_north + block[U + 3] * lat_prev(p_north)
        total = total + block[U + 4] * p_up + block[U + 5] * p_down
        half_ref[i] = total[0:4, :]
        half_ref[i + half] = total[4:8, :]
        new_ref[i] = v_ref[i] + total[0:4, :]
        new_ref[i + half] = v_ref[i + half] + total[4:8, :]
        e, p_down = e_up, p_up


def call(
    kernel, outs, ins, scratch=(), flops=1, name=None, held_in=(), held_out=(), far_out=()
):
    spaces = {"s": pltpu.SMEM, "v": pltpu.VMEM, "a": pl.ANY}
    made = pl.pallas_call(
        kernel,
        out_shape=[
            pltpu.VMEM(shape, dtype) if n in held_out else jax.ShapeDtypeStruct(shape, dtype)
            for n, (shape, dtype) in enumerate(outs)
        ],
        in_specs=[pl.BlockSpec(memory_space=spaces[k]) for k in ins],
        out_specs=[
            pl.BlockSpec(memory_space=pl.ANY if n in far_out else pltpu.VMEM)
            for n in range(len(outs))
        ],
        scratch_shapes=list(scratch),
        compiler_params=pltpu.CompilerParams(vmem_limit_bytes=VMEM_LIMIT),
        cost_estimate=pl.CostEstimate(flops=flops, bytes_accessed=1 << 20, transcendentals=0),
        name=name,
    )

    def run(*args):
        return made(
            *[
                pltpu.with_memory_space_constraint(a, pltpu.VMEM if n in held_in else pltpu.HBM)
                if ins[n] != "s"
                else a
                for n, a in enumerate(args)
            ]
        )

    return run


def body(
    logvisc, momentum, displacement, ice_history, load_steps, site_cells, observed, site_weight
):
    nr, nl, nlat = logvisc.shape
    own_sites = site_cells.shape[0]
    lon_n = lax.axis_size("lon")
    rad_n = lax.axis_size("rad")
    total_lon = nl * lon_n
    sites = own_sites * lon_n
    devices = lon_n * rad_n
    half = nr // 2
    scale = 1.0 / math.sqrt(total_lon * nlat)
    rad_at = lax.axis_index("rad")
    row = (8, nlat)

    column, first_column, layers = (4 * nr, 1, nlat), (4 * nr + 1, 1, nlat), (8, nl, nlat)
    to_west, to_east, to_west2, to_east2, to_low, to_high, packets = call(
        message_kernel,
        [
            (shape, F32)
            for shape in [first_column] * 2 + [column] * 2 + [layers] * 2 + [(lon_n, 8, own_sites)]
        ],
        "svvvvvv",
        name="messages",
    )(
        load_steps, logvisc, displacement, ice_history, site_cells[None], observed, site_weight
    )
    gathered = lax.all_to_all(packets, "lon", 0, 0)

    eastward = [(i, (i + 1) % lon_n) for i in range(lon_n)]
    westward = [(t, s) for s, t in eastward]
    upward = [(i, i + 1) for i in range(rad_n - 1)]
    downward = [(t, s) for s, t in upward]

    def across_rad(down, up):
        if rad_n == 2:
            both = lax.ppermute(jnp.where(rad_at == 0, up, down), "rad", [(0, 1), (1, 0)])
            return both, both
        return lax.ppermute(up, "rad", upward), lax.ppermute(down, "rad", downward)

    west = lax.ppermute(to_east, "lon", eastward)
    east = lax.ppermute(to_west, "lon", westward)
    low, high = across_rad(to_low, to_high)

    (rows,) = call(
        functools.partial(interior_kernel, rad_n=rad_n),
        [((Rows(half).count,) + row, F32)],
        "vv",
        flops=20000000,
        name="interior",
        held_out=(0,),
    )(logvisc, displacement)

    k_high, k_low, data = call(
        functools.partial(weights_kernel, total_lon=total_lon),
        [((COLS, sites, nlat), BF16)] * 2 + [((8, sites), F32)],
        "v",
        scratch=[pltpu.VMEM((16, sites), F32)],
        flops=20000000,
        name="site_weights",
        held_out=(0, 1, 2),
    )(gathered)

    (partial,) = call(
        functools.partial(forward_kernel, rad_n=rad_n),
        [((devices, 3, sites), F32)],
        "svvvvvvvv",
        scratch=[pltpu.VMEM((3, half) + row, F32), pltpu.VMEM((6,) + row, F32)],
        flops=20000000,
        name="forward",
        held_in=(1, 7, 8),
    )(load_steps, rows, west, east, low, high, ice_history, k_high, k_low)
    predicted = lax.all_to_all(partial, ("lon", "rad"), 0, 0)

    west2 = lax.ppermute(to_east2, "lon", eastward)
    east2 = lax.ppermute(to_west2, "lon", westward)
    ends = [
        jnp.stack([x[: 4 * nr].reshape(4, nr, 1, nlat)[:, r] for x in (west, east)], axis=1)
        for r in (0, nr - 1)
    ]
    corner_low, corner_high = across_rad(*ends)

    blocks, ends = call(
        functools.partial(prepare_kernel, rad_n=rad_n),
        [((half, BLOCK) + row, F32), ((ENDS,) + row, F32)],
        "s" + "v" * 12,
        scratch=[
            pltpu.VMEM((half + 2,) + row, F32),
            pltpu.VMEM((3, half + 2) + row, F32),
            pltpu.VMEM((half + 2,) + row, F32),
            pltpu.VMEM((3, half + 2) + row, F32),
            pltpu.VMEM((3, half) + row, F32),
            pltpu.VMEM((3, half) + row, F32),
            pltpu.VMEM((half, BLOCK) + row, F32),
            pltpu.SemaphoreType.DMA((half,)),
        ],
        flops=40000000,
        name="prepare",
        far_out=(0,),
    )(
        load_steps, logvisc, momentum, displacement, ice_history, west, east, west2, east2, low,
        high, corner_low, corner_high,
    )

    new_logvisc, half_momentum, misfit = call(
        functools.partial(gradient_kernel, scale=scale),
        [((nr, nl, nlat), F32), ((nr, nl, nlat), F32), ((1, 1), F32)],
        "vvvvvva",
        scratch=[
            pltpu.VMEM((3,) + row, F32),
            pltpu.VMEM((10, 3) + row, F32),
            pltpu.VMEM((half, BLOCK) + row, F32),
            pltpu.SemaphoreType.DMA((half,)),
        ],
        flops=20000000,
        name="gradient",
        held_in=(2, 3, 4),
    )(logvisc, predicted, data, k_high, k_low, ends, blocks)
    return (new_logvisc, half_momentum, misfit.reshape(1))


def solution(mesh):
    return jax.shard_map(
        body,
        mesh=mesh,
        in_specs=(
            P("rad", "lon", None),
            P("rad", "lon", None),
            P(None, "rad", "lon", None),
            P(None, "lon", None),
            P(),
            P("lon"),
            P(None, "lon"),
            P(None, "lon"),
        ),
        out_specs=(P("rad", "lon", None), P("rad", "lon", None), P()),
        check_vma=False,
    )
```

```python
import functools
import math

import jax
import jax.numpy as jnp
from jax import lax
from jax.experimental import pallas as pl
from jax.experimental.pallas import tpu as pltpu
from jax.sharding import PartitionSpec as P

RELAX_RATE = 0.05
KERNEL_WIDTH = 0.1
KERNEL_WAVE = 40.0
PRIOR_WEIGHT = 0.1
COLS = 8
F32 = jnp.float32
BF16 = jnp.bfloat16
VMEM_LIMIT = 40 * 1024 * 1024


def reciprocal(x):
    r = pl.reciprocal(x, approx=True)
    return r * (2.0 - x * r)


def lat_next(x):
    return pltpu.roll(x, x.shape[1] - 1, 1)


def lat_prev(x):
    return pltpu.roll(x, 1, 1)


def lon_next(x):
    return pltpu.roll(x, 7, 0)


def lon_prev(x):
    return pltpu.roll(x, 1, 0)


def swap_halves(x):
    return pltpu.roll(x, 4, 0)


def pack(low, high):
    return jnp.concatenate([low, high], axis=0)


class Shape:
    def __init__(self, nr, width, rad_n):
        self.nr, self.width, self.half = nr, width, nr // 2
        sub = lax.broadcasted_iota(jnp.int32, (8, width), 0)
        lane = lax.broadcasted_iota(jnp.int32, (8, width), 1)
        self.lon = sub % 4
        self.lower = sub < 4
        self.upper = sub >= 4
        self.western = self.lon < 2
        self.not_last = lane < width - 1
        self.not_first = lane > 0
        self.rate = 4.0 / (nr * rad_n)
        at = lax.axis_index("rad")
        self.has_low = (at > 0).astype(F32)
        self.has_high = (at < rad_n - 1).astype(F32)
        layer = jnp.where(self.lower, 0, self.half) + (at * nr - (nr * rad_n - 1))
        self.first_weight = jnp.exp(layer.astype(F32) * self.rate)

    def step(self, i):
        return math.exp(self.rate * i)

    def sides(self, west, east):
        return jnp.where(
            self.lower,
            jnp.where(self.western, west[0], east[0]),
            jnp.where(self.western, west[1], east[1]),
        )


def face(a, b):
    return 2.0 * a * b * reciprocal(a + b)


def sin_pi(u):
    z = u * u
    p = 0.0772201269865036
    p = p * z - 0.5980451703071594
    p = p * z + 2.5500314235687256
    p = p * z - 5.1677069664001465
    p = p * z + 3.141592502593994
    return p * u


def site_kernel(d):
    turns = d * (KERNEL_WAVE / (2.0 * math.pi))
    s = sin_pi(turns - jnp.round(turns))
    return (reciprocal(1.0 + d * (1.0 / KERNEL_WIDTH)) + 0.5) - s * s


def packet_kernel(cells_ref, obs_ref, wt_ref, packet_ref):
    packet = jnp.concatenate(
        [
            cells_ref[...].astype(F32),
            obs_ref[...],
            wt_ref[...],
            jnp.zeros((1, obs_ref.shape[1]), F32),
        ],
        axis=0,
    )
    for n in range(packet_ref.shape[0]):
        packet_ref[n] = packet


def message_kernel(
    v_ref, s_ref, ice_ref, west_ref, east_ref, west2_ref, east2_ref, low_ref, high_ref, *, rad_n
):
    nr, nl, width = v_ref.shape

    def field(n, r):
        return v_ref[r] if n == 0 else s_ref[n - 1, r]

    for r in range(nr):
        for n in range(4):
            x = field(n, r)
            west_ref[n * nr + r] = x[0:1, :]
            east_ref[n * nr + r] = x[nl - 1 : nl, :]
            west2_ref[n * nr + r] = x[1:2, :]
            east2_ref[n * nr + r] = x[nl - 2 : nl - 1, :]
    for n in range(ice_ref.shape[0]):
        west_ref[4 * nr + n] = ice_ref[n, 0:1, :]
        east_ref[4 * nr + n] = ice_ref[n, nl - 1 : nl, :]
    bottom = lax.axis_index("rad") == 0
    for n in range(4):
        for k in range(2):
            down, up = field(n, k), field(n, nr - 1 - k)
            if rad_n == 2:
                low_ref[n + 4 * k] = jnp.where(bottom, up, down)
            else:
                low_ref[n + 4 * k] = down
                high_ref[n + 4 * k] = up
    if rad_n == 2:
        high_ref[...] = jnp.zeros_like(high_ref)


def weights_kernel(gathered_ref, high_ref, low_ref, data_ref, rows_ref, *, total_lon):
    devices, _, own = gathered_ref.shape
    sites = high_ref.shape[1]
    width = high_ref.shape[2]
    for d in range(devices):
        data_ref[:, d * own : (d + 1) * own] = gathered_ref[d]
    cells = data_ref[0:1, :]
    lon = jnp.floor((cells + 0.5) * (1.0 / width))
    theta = (cells - lon * width + 0.5) * (1.0 / width)
    phi = lon * (1.0 / total_lon)

    def sin_whole(t):
        return sin_pi(jnp.minimum(t, 1.0 - t))

    def circle(t):
        u = t - jnp.round(t)
        s = sin_pi(u)
        y = jnp.abs(2.0 * u)
        wave = sin_pi(jnp.minimum(y, 1.0 - y))
        return 1.0 - 2.0 * s * s, jnp.where(u < 0, -wave, wave)

    site_cos, site_sin = circle(phi)
    first = lax.axis_index("lon") * 4 - 2 + total_lon
    col = (lax.broadcasted_iota(jnp.int32, (COLS, sites), 0) + first).astype(F32)
    turns = col * (1.0 / total_lon)
    col_cos, col_sin = circle(turns - jnp.floor(turns))
    rows_ref[0:8, :] = col_cos * site_cos + col_sin * site_sin
    rows_ref[8:9, :] = -2.0 * sin_pi(0.5 - theta)
    rows_ref[9:10, :] = -2.0 * sin_whole(theta)
    rows_ref[10:16, :] = jnp.zeros((6, sites), F32)
    columns = jnp.transpose(rows_ref[...])
    lat = (lax.broadcasted_iota(jnp.int32, (16, width), 1).astype(F32) + 0.5) * (1.0 / width)
    cos_lat = sin_pi(0.5 - lat)
    sin_lat = sin_whole(lat)
    for at in range(0, sites, 16):
        part = columns[at : at + 16, :]
        a = 2.0 + part[:, 8:9] * cos_lat
        b = part[:, 9:10] * sin_lat
        for n in range(COLS):
            k = site_kernel(a + b * part[:, n : n + 1])
            high = k.astype(BF16)
            high_ref[n, at : at + 16, :] = high
            low_ref[n, at : at + 16, :] = (k - high.astype(F32)).astype(BF16)


def two_parts(x):
    high = x.astype(BF16).astype(F32)
    return jnp.concatenate([high, x - high], axis=0).astype(BF16)


def product(x, high, low, contract):
    dims = (((1,), (contract,)), ((), ()))
    parts = two_parts(x)
    both = lax.dot_general(parts, high, dims, preferred_element_type=F32)
    rest = lax.dot_general(parts, low, dims, preferred_element_type=F32)
    return both[0:8, :] + (both[8:16, :] + rest[0:8, :])


def forward_kernel(
    steps_ref, v_ref, s_ref, west_ref, east_ref, low_ref, high_ref, ice_ref, k_high_ref, k_low_ref,
    pred_ref, corner_low_ref, corner_high_ref,
    fluid_ref, fluid_north_ref, field_ref, north_ref, south_ref, h_east_ref, h_north_ref,
    h_south_ref, h_up_ref, h_cut_ref, next_ref, next_north_ref, surf_ref, *, rad_n,
):
    nr, nl, width = v_ref.shape
    shape = Shape(nr, width, rad_n)
    half = shape.half
    lower, lon = shape.lower, shape.lon
    ends = (lon == 0) | (lon == 3)

    bottom = lax.axis_index("rad") == 0
    for n in range(4):
        for k, ref in enumerate((west_ref, east_ref)):
            down, up = ref[n * nr], ref[n * nr + nr - 1]
            if rad_n == 2:
                corner_low_ref[2 * n + k] = jnp.where(bottom, up, down)
            else:
                corner_low_ref[2 * n + k] = down
                corner_high_ref[2 * n + k] = up
    if rad_n == 2:
        corner_high_ref[...] = jnp.zeros_like(corner_high_ref)

    for i in range(half):
        f = jnp.exp(-pack(v_ref[i], v_ref[i + half]))
        fluid_ref[i] = f
        fluid_north_ref[i] = lat_next(f)
        for c in range(3):
            x = pack(s_ref[c, i], s_ref[c, i + half])
            field_ref[c, i] = x
            north_ref[c, i] = lat_next(x)
            south_ref[c, i] = lat_prev(x)
    for i in range(half):
        h_north = jnp.where(shape.not_last, face(fluid_ref[i], fluid_north_ref[i]), 0.0)
        h_north_ref[i] = h_north
        h_south_ref[i] = lat_prev(h_north)

    ring = pack(shape.has_low * jnp.exp(-low_ref[0]), shape.has_high * jnp.exp(-high_ref[0]))
    h_ring = face(ring, jnp.where(lower, fluid_ref[0], fluid_ref[half - 1]))
    seam = face(swap_halves(fluid_ref[0]), fluid_ref[half - 1])
    h_up_ref[half] = jnp.where(lower, seam, 0.0)
    h_up_ref[0] = swap_halves(h_up_ref[half])
    load = ice_ref[steps_ref[0]] * (1.0 - shape.has_high)
    load = pack(jnp.zeros_like(load), load)
    carry = [h_up_ref[0] * (field_ref[c, 0] - swap_halves(field_ref[c, half - 1])) for c in range(3)]
    for i in range(half):

        def side(n):
            return shape.sides(
                (west_ref[n * nr + i], west_ref[n * nr + i + half]),
                (east_ref[n * nr + i], east_ref[n * nr + i + half]),
            )

        f = fluid_ref[i]
        h_cut = jnp.where(ends, face(f, jnp.exp(-side(0))), 0.0)
        h_cut_ref[i] = h_cut
        h_east = jnp.where(lon < 3, face(f, lon_next(f)), 0.0)
        h_east_ref[i] = h_east
        if i < half - 1:
            h_up_ref[i + 1] = face(f, fluid_ref[i + 1])
        h_north, h_south, h_up = h_north_ref[i], h_south_ref[i], h_up_ref[i + 1]
        for c in range(3):
            x = field_ref[c, i]
            above = field_ref[c, i + 1] if i < half - 1 else swap_halves(field_ref[c, 0])
            east = h_east * (lon_next(x) - x)
            up = h_up * (above - x)
            total = (east - lon_prev(east)) + (up - carry[c]) + h_cut * (side(1 + c) - x)
            total = total + h_north * (north_ref[c, i] - x) + h_south * (south_ref[c, i] - x)
            if i in (0, half - 1):
                beyond = h_ring * (pack(low_ref[1 + c], high_ref[1 + c]) - x)
                if i == 0:
                    total = total + jnp.where(lower, beyond, 0.0)
                if i == half - 1:
                    total = total + jnp.where(lower, 0.0, beyond)
            s1 = x + RELAX_RATE * total
            if c == 0 and i == half - 1:
                s1 = s1 - load
            next_ref[c, i] = s1
            next_north_ref[c, i] = lat_next(s1)
            carry[c] = up

    zero = jnp.zeros((8, width), F32)
    column, east, north, cut = [zero] * 3, [zero] * 3, [zero] * 3, [zero] * 3
    below = [swap_halves(next_ref[c, half - 1]) for c in range(3)]
    for i in range(half):
        weight = shape.step(i)
        g_east = weight * h_east_ref[i]
        g_north = weight * h_north_ref[i]
        g_cut = weight * h_cut_ref[i]
        g_low = (RELAX_RATE * (weight - shape.step(i - 1))) * h_up_ref[i]
        for c in range(3):
            x = next_ref[c, i]
            column[c] = column[c] + (weight * x - g_low * (x - below[c]))
            east[c] = east[c] + g_east * (lon_next(x) - x)
            north[c] = north[c] + g_north * (next_north_ref[c, i] - x)
            cut[c] = cut[c] + g_cut * x
            below[c] = x
    top = shape.step(half - 1)
    g_ring = (RELAX_RATE * h_ring) * jnp.where(
        lower, shape.step(-1) - 1.0, shape.step(half) - top
    )
    for c in range(3):
        inner = jnp.where(lower, next_ref[c, 0], next_ref[c, half - 1])

        def folded(x):
            x = shape.first_weight * x
            return x + swap_halves(x)

        sum_east = folded(east[c])
        sum_north = folded(north[c])
        sum_cut = folded(cut[c])
        own = folded(column[c] + g_ring * inner)
        spread = (sum_east - lon_prev(sum_east)) + (sum_north - lat_prev(sum_north)) - sum_cut
        own = own + RELAX_RATE * spread
        if c == 0:
            second = ice_ref[steps_ref[1]] * (1.0 - shape.has_high)
            own = own - pack(second, second)
        surf_ref[0, c : c + 1, :] = RELAX_RATE * sum_cut[0:1, :]
        for col in range(4):
            surf_ref[col + 1, c : c + 1, :] = own[col : col + 1, :]
        surf_ref[5, c : c + 1, :] = RELAX_RATE * sum_cut[3:4, :]
    total = None
    for col in range(6):
        surf_ref[col, 3:8, :] = jnp.zeros((5, width), F32)
        term = product(surf_ref[col], k_high_ref[col + 1], k_low_ref[col + 1], 1)
        total = term if total is None else total + term
    sites = total.shape[1]
    spare = pred_ref.shape[2] - 3 * sites
    flat = [total[c : c + 1, :] for c in range(3)]
    if spare > 0:
        flat.append(jnp.zeros((1, spare), F32))
    flat = jnp.concatenate(flat, axis=1)
    for n in range(pred_ref.shape[0]):
        pred_ref[n] = flat


FIELD, FIELD_SIDE, BOTH, BOTH_SIDE, SHARE, FLUID, SIDE, BASE, BLOCK = 0, 3, 6, 9, 12, 18, 19, 24, 25
RING, LAST, LOW, LOW_BOTH, HIGH, HIGH_BOTH, ENDS = 0, 5, 12, 15, 18, 21, 24


def prepare_kernel(
    steps_ref, v_ref, m_ref, s_ref, ice_ref, west_ref, east_ref, west2_ref, east2_ref, low_ref,
    high_ref, corner_low_ref, corner_high_ref, blocks_ref,
    fluid_ref, field_ref, fluid_side_ref, field_side_ref, north_ref, south_ref, out_ref, sems,
    *, rad_n,
):
    nr, nl, width = v_ref.shape
    shape = Shape(nr, width, rad_n)
    half = shape.half
    lower, lon, western = shape.lower, shape.lon, shape.western

    def share(f, other):
        return other * reciprocal(f + other)

    def safe_share(f, other):
        return other * reciprocal(jnp.maximum(f + other, 1e-30))

    def north_of(f):
        return jnp.where(shape.not_last, lat_next(f), 0.0)

    def south_of(f):
        return jnp.where(shape.not_first, lat_prev(f), 0.0)

    def two(ref, n, i):
        return ref[n * nr + i], ref[n * nr + i + half]

    def corner(ref, n):
        return jnp.where(western, ref[2 * n], ref[2 * n + 1])

    for i in range(half):
        f = jnp.exp(-pack(v_ref[i], v_ref[i + half]))
        f_side = jnp.exp(-shape.sides(two(west_ref, 0, i), two(east_ref, 0, i)))
        fluid_ref[i + 1] = f
        fluid_side_ref[i + 1] = f_side
        north_ref[0, i], south_ref[0, i] = north_of(f), south_of(f)
        north_ref[1, i], south_ref[1, i] = north_of(f_side), south_of(f_side)
        for c in range(3):
            x = pack(s_ref[c, i], s_ref[c, i + half])
            x_side = shape.sides(two(west_ref, 1 + c, i), two(east_ref, 1 + c, i))
            field_ref[c, i + 1] = x
            field_side_ref[c, i + 1] = x_side
            north_ref[2 + c, i], south_ref[2 + c, i] = lat_next(x), lat_prev(x)
            north_ref[5 + c, i], south_ref[5 + c, i] = lat_next(x_side), lat_prev(x_side)
    ring = pack(shape.has_low * jnp.exp(-low_ref[0]), shape.has_high * jnp.exp(-high_ref[0]))
    ring_side = jnp.where(
        lower,
        shape.has_low * jnp.exp(-corner(corner_low_ref, 0)),
        shape.has_high * jnp.exp(-corner(corner_high_ref, 0)),
    )
    ring_field = [pack(low_ref[1 + c], high_ref[1 + c]) for c in range(3)]
    ring_field_side = [
        jnp.where(lower, corner(corner_low_ref, 1 + c), corner(corner_high_ref, 1 + c))
        for c in range(3)
    ]

    def close(ref, ring):
        ref[0] = jnp.where(lower, ring, swap_halves(ref[half]))
        ref[half + 1] = jnp.where(lower, swap_halves(ref[1]), ring)

    close(fluid_ref, ring)
    close(fluid_side_ref, ring_side)
    for c in range(3):
        close(field_ref.at[c], ring_field[c])
        close(field_side_ref.at[c], ring_field_side[c])

    def coefficients(f, shares, here, above, below):
        scaled = (2.0 * RELAX_RATE) * f
        weighted = scaled * here
        radial = scaled * (shares[4] * (above - here) + shares[5] * (below - here))
        return [weighted * shares[n] for n in range(4)] + [radial]

    def relaxed(f, shares, s, others):
        total = shares[0] * (others[0] - s)
        for n in range(1, 6):
            total = total + shares[n] * (others[n] - s)
        return s + (2.0 * RELAX_RATE) * (f * total)

    outer = pack(shape.has_low * jnp.exp(-low_ref[4]), shape.has_high * jnp.exp(-high_ref[4]))
    inner = jnp.where(lower, fluid_ref[1], fluid_ref[half])
    ring_shares = [
        safe_share(ring, jnp.where(lon == 3, ring_side, lon_next(ring))),
        safe_share(ring, jnp.where(lon == 0, ring_side, lon_prev(ring))),
        safe_share(ring, north_of(ring)),
        safe_share(ring, south_of(ring)),
        safe_share(ring, outer),
        safe_share(ring, inner),
    ]
    ring_coefficients = coefficients(
        ring,
        ring_shares,
        jnp.where(lower, shape.step(-1), shape.step(half)),
        jnp.where(lower, shape.step(-2), shape.step(half + 1)),
        jnp.where(lower, shape.step(0), shape.step(half - 1)),
    )
    for n in range(5):
        out_ref[half, RING + n] = ring_coefficients[n]
    ring_both = []
    for c in range(3):
        s, s_side = ring_field[c], ring_field_side[c]
        others = [
            jnp.where(lon == 3, s_side, lon_next(s)),
            jnp.where(lon == 0, s_side, lon_prev(s)),
            lat_next(s),
            lat_prev(s),
            pack(low_ref[5 + c], high_ref[5 + c]),
            jnp.where(lower, field_ref[c, 1], field_ref[c, half]),
        ]
        ring_both.append(s + relaxed(ring, ring_shares, s, others))
    load = ice_ref[steps_ref[0]]
    load = (1.0 - shape.has_high) * pack(jnp.zeros_like(load), load)
    load_side = jnp.where(
        western, west_ref[4 * nr + steps_ref[0]], east_ref[4 * nr + steps_ref[0]]
    )
    load_side = (1.0 - shape.has_high) * jnp.where(lower, 0.0, load_side)

    copies = []
    both_ends = {}

    def send(i):
        copies.append(pltpu.make_async_copy(out_ref.at[i], blocks_ref.at[i], sems.at[i]))
        copies[-1].start()

    for i in range(half):
        f, f_side = fluid_ref[i + 1], fluid_side_ref[i + 1]
        shares = [
            share(f, jnp.where(lon == 3, f_side, lon_next(f))),
            share(f, jnp.where(lon == 0, f_side, lon_prev(f))),
            share(f, north_ref[0, i]),
            share(f, south_ref[0, i]),
            share(f, fluid_ref[i + 2]),
            share(f, fluid_ref[i]),
        ]
        for n in range(6):
            out_ref[i, SHARE + n] = shares[n]
        out_ref[i, FLUID] = f
        if i == half - 1:
            for n in range(6):
                out_ref[half, LAST + n] = shares[n]
            out_ref[half, LAST + 6] = f
        out_ref[i, BASE] = pack(
            m_ref[i] - (0.5 * PRIOR_WEIGHT) * v_ref[i],
            m_ref[i + half] - (0.5 * PRIOR_WEIGHT) * v_ref[i + half],
        )
        f_far = jnp.exp(-shape.sides(two(west2_ref, 0, i), two(east2_ref, 0, i)))
        side_shares = [
            share(f_side, jnp.where(western, f, f_far)),
            share(f_side, jnp.where(western, f_far, f)),
            share(f_side, north_ref[1, i]),
            share(f_side, south_ref[1, i]),
            share(f_side, fluid_side_ref[i + 2]),
            share(f_side, fluid_side_ref[i]),
        ]
        side = coefficients(
            f_side, side_shares, shape.step(i), shape.step(i + 1), shape.step(i - 1)
        )
        for n in range(5):
            out_ref[i, SIDE + n] = side[n]
        for c in range(3):
            s, s_side = field_ref[c, i + 1], field_side_ref[c, i + 1]
            s_far = shape.sides(two(west2_ref, 1 + c, i), two(east2_ref, 1 + c, i))
            others = [
                jnp.where(lon == 3, s_side, lon_next(s)),
                jnp.where(lon == 0, s_side, lon_prev(s)),
                north_ref[2 + c, i],
                south_ref[2 + c, i],
                field_ref[c, i + 2],
                field_ref[c, i],
            ]
            both = s + relaxed(f, shares, s, others)
            others = [
                jnp.where(western, s, s_far),
                jnp.where(western, s_far, s),
                north_ref[5 + c, i],
                south_ref[5 + c, i],
                field_side_ref[c, i + 2],
                field_side_ref[c, i],
            ]
            both_side = s_side + relaxed(f_side, side_shares, s_side, others)
            if c == 0 and i == half - 1:
                both = both - load
                both_side = both_side - load_side
            out_ref[i, FIELD + c] = s
            out_ref[i, FIELD_SIDE + c] = s_side
            out_ref[i, BOTH + c] = both
            out_ref[i, BOTH_SIDE + c] = both_side
            if i in (0, half - 1):
                both_ends[c, i] = both
        send(i)
    low_step = shape.step(0) - shape.step(-1)
    high_step = shape.step(half) - shape.step(half - 1)
    for c in range(3):
        first, last = both_ends[c, 0], both_ends[c, half - 1]
        out_ref[half, LOW + c] = field_ref[c, 1] - field_ref[c, 0]
        out_ref[half, LOW_BOTH + c] = low_step * (
            first - jnp.where(lower, ring_both[c], swap_halves(last))
        )
        out_ref[half, HIGH + c] = field_ref[c, half + 1] - field_ref[c, half]
        out_ref[half, HIGH_BOTH + c] = high_step * (
            jnp.where(lower, swap_halves(first), ring_both[c]) - last
        )
    out_ref[half, ENDS:BLOCK] = jnp.zeros((BLOCK - ENDS, 8, width), F32)
    send(half)
    for copy in copies:
        copy.wait()


def gradient_kernel(
    v_ref, pred_ref, data_ref, k_high_ref, k_low_ref, blocks_ref,
    new_ref, half_ref, misfit_ref, sa_ref, d_ref, in_ref, e_ref, side_ref, north_ref, product_ref,
    total_ref, sems, *, scale, rad_n,
):
    nr, nl, width = v_ref.shape
    shape = Shape(nr, width, rad_n)
    half = shape.half
    sites = k_high_ref.shape[1]
    lon, lower = shape.lon, shape.lower
    copies = [
        pltpu.make_async_copy(blocks_ref.at[i], in_ref.at[i], sems.at[i]) for i in range(half + 1)
    ]
    copies[half].start()
    for i in range(half):
        copies[i].start()
    ends_ref = in_ref.at[half]

    flat = pred_ref[0]
    for n in range(1, pred_ref.shape[0]):
        flat = flat + pred_ref[n]
    predicted = jnp.concatenate(
        [flat[:, c * sites : (c + 1) * sites] for c in range(3)], axis=0
    )
    weight = data_ref[4:7, :]
    weighted = weight * (predicted * scale - data_ref[1:4, :])
    squares = jnp.sum(weighted * weighted, axis=1, keepdims=True)
    misfit_ref[...] = jnp.sum(squares, axis=0, keepdims=True) * (1.0 / (3 * sites))
    pulled = (weight * weighted) * scale
    pulled = jnp.concatenate([pulled, jnp.zeros((5, sites), F32)], axis=0)
    for col in range(COLS):
        spread = product(pulled, k_high_ref[col], k_low_ref[col], 0)
        for c in range(3):
            sa_ref[c, col : col + 1, :] = spread[c : c + 1, :]

    for c in range(3):
        x = sa_ref[c]

        def window(start):
            return shape.first_weight * jnp.where(
                lower,
                x if start == 0 else pltpu.roll(x, 8 - start, 0),
                x if start == 4 else pltpu.roll(x, (4 - start) % 8, 0),
            )

        own = window(2)
        east = window(3)
        west = window(1)
        outside = jnp.where(lon < 2, west, east)
        d_ref[0, c] = east - own
        d_ref[1, c] = west - own
        d_ref[2, c] = lat_next(own) - own
        d_ref[3, c] = lat_prev(own) - own
        d_ref[4, c] = own
        d_ref[5, c] = jnp.where(lon < 2, own, window(4)) - outside
        d_ref[6, c] = jnp.where(lon < 2, window(0), own) - outside
        d_ref[7, c] = lat_next(outside) - outside
        d_ref[8, c] = lat_prev(outside) - outside
        d_ref[9, c] = outside

    def change(coeffs, first):
        out = []
        for c in range(3):
            total = coeffs[0] * d_ref[first, c]
            for n in range(1, 5):
                total = total + coeffs[n] * d_ref[first + n, c]
            out.append(total)
        return out

    above, below = shape.step(1) - 1.0, shape.step(-1) - 1.0

    def own_change(ref, at, fluid, i):
        shares = [ref[at + n] for n in range(6)]
        scaled = (2.0 * RELAX_RATE * shape.step(i)) * fluid
        coeffs = shares[:4] + [above * shares[4] + below * shares[5]]
        return [scaled * x for x in change(coeffs, 0)]

    def first_pass(i):
        copies[i].wait()
        e = own_change(in_ref.at[i], SHARE, in_ref[i, FLUID], i)
        side = change([in_ref[i, SIDE + n] for n in range(5)], 5)
        for c in range(3):
            e_ref[c, i] = e[c]
            side_ref[c, i] = side[c]
            north_ref[c, i] = lat_next(in_ref[i, FIELD + c])
            north_ref[3 + c, i] = lat_next(in_ref[i, BOTH + c])
            north_ref[6 + c, i] = lat_next(e[c])

    def second_pass(i, p_down):
        here, step = shape.step(i), shape.step(i + 1) - shape.step(i)
        weighted = [0.0] * 4
        plain = [0.0] * 4
        for c in range(3):
            s, s_side = in_ref[i, FIELD + c], in_ref[i, FIELD_SIDE + c]
            both, both_side = in_ref[i, BOTH + c], in_ref[i, BOTH_SIDE + c]
            e, e_side = e_ref[c, i], side_ref[c, i]

            def differences(x, x_side, x_north):
                return [jnp.where(lon == 3, x_side, lon_next(x)) - x, x_side - x, x_north - x]

            d_field = differences(s, s_side, north_ref[c, i])
            d_both = differences(both, both_side, north_ref[3 + c, i])
            d_e = differences(e, e_side, north_ref[6 + c, i])
            if i < half - 1:
                d_field.append(in_ref[i + 1, FIELD + c] - s)
                d_both.append(step * (in_ref[i + 1, BOTH + c] - both))
                d_e.append(e_ref[c, i + 1] - e)
            else:
                d_field.append(ends_ref[HIGH + c])
                d_both.append(ends_ref[HIGH_BOTH + c])
                d_e.append(jnp.where(lower, swap_halves(e_ref[c, 0]), ring[c]) - e)
            slopes = [d_ref[0, c], d_ref[1, c], d_ref[2, c], d_ref[4, c]]
            for n in range(4):
                weighted[n] = weighted[n] + d_both[n] * slopes[n]
                plain[n] = plain[n] + d_field[n] * d_e[n]
        p_east, p_cut, p_north = [here * weighted[n] + plain[n] for n in range(3)]
        p_up = weighted[3] + plain[3]
        p_west = jnp.where(lon == 0, p_cut, lon_prev(p_east))
        product_ref[i] = lat_prev(p_north)
        total = None
        for n, x in ((0, p_east), (1, p_west), (2, p_north), (4, p_up), (5, p_down)):
            share = in_ref[i, SHARE + n]
            term = (share * share) * x
            total = term if total is None else total + term
        total_ref[i] = total
        return p_up

    def third_pass(i):
        share = in_ref[i, SHARE + 3]
        total = total_ref[i] + (share * share) * product_ref[i]
        total = in_ref[i, BASE] - RELAX_RATE * (in_ref[i, FLUID] * total)
        half_ref[i] = total[0:4, :]
        half_ref[i + half] = total[4:8, :]
        new_ref[i] = v_ref[i] + total[0:4, :]
        new_ref[i + half] = v_ref[i + half] + total[4:8, :]

    copies[half].wait()
    ring = change([ends_ref[RING + n] for n in range(5)], 0)
    e_last = own_change(ends_ref, LAST, ends_ref[LAST + 6], half - 1)
    lead = min(2, half)
    for i in range(lead):
        first_pass(i)
    p_down = None
    for c in range(3):
        e_low = jnp.where(lower, ring[c], swap_halves(e_last[c]))
        term = ends_ref[LOW_BOTH + c] * d_ref[4, c] + ends_ref[LOW + c] * (e_ref[c, 0] - e_low)
        p_down = term if p_down is None else p_down + term
    for i in range(half):
        if i + lead < half:
            first_pass(i + lead)
        p_down = second_pass(i, p_down)
        if i > 0:
            third_pass(i - 1)
    third_pass(half - 1)


def call(
    kernel, outs, ins, scratch=(), flops=1, name=None, held_in=(), held_out=(), far_in=(),
    far_out=(), near_out=(),
):
    spaces = {"s": pltpu.SMEM, "v": pltpu.VMEM, "h": pltpu.HBM}
    made = pl.pallas_call(
        kernel,
        out_shape=[
            pltpu.VMEM(shape, dtype)
            if n in held_out
            else pltpu.HBM(shape, dtype)
            if n in far_out or n in near_out
            else jax.ShapeDtypeStruct(shape, dtype)
            for n, (shape, dtype) in enumerate(outs)
        ],
        in_specs=[pl.BlockSpec(memory_space=spaces[k]) for k in ins],
        out_specs=[
            pl.BlockSpec(memory_space=pltpu.HBM if n in far_out else pltpu.VMEM)
            for n in range(len(outs))
        ],
        scratch_shapes=list(scratch),
        compiler_params=pltpu.CompilerParams(vmem_limit_bytes=VMEM_LIMIT),
        cost_estimate=pl.CostEstimate(flops=flops, bytes_accessed=1 << 20, transcendentals=0),
        name=name,
    )

    def run(*args):
        return made(
            *[
                pltpu.with_memory_space_constraint(a, pltpu.VMEM if n in held_in else pltpu.HBM)
                if n in held_in or n in far_in
                else a
                for n, a in enumerate(args)
            ]
        )

    return run


def body(
    logvisc, momentum, displacement, ice_history, load_steps, site_cells, observed, site_weight
):
    nr, nl, nlat = logvisc.shape
    own_sites = site_cells.shape[0]
    lon_n = lax.axis_size("lon")
    rad_n = lax.axis_size("rad")
    total_lon = nl * lon_n
    sites = own_sites * lon_n
    devices = lon_n * rad_n
    half = nr // 2
    scale = 1.0 / math.sqrt(total_lon * nlat)
    row = (8, nlat)

    def across_rad(down, up):
        if rad_n == 2:
            both = lax.ppermute(down, "rad", [(0, 1), (1, 0)])
            return both, both
        upward = [(i, i + 1) for i in range(rad_n - 1)]
        downward = [(t, s) for s, t in upward]
        return lax.ppermute(up, "rad", upward), lax.ppermute(down, "rad", downward)

    eastward = [(i, (i + 1) % lon_n) for i in range(lon_n)]
    westward = [(t, s) for s, t in eastward]
    column, layers = (4 * nr, 1, nlat), (8, nl, nlat)
    first_column = (4 * nr + ice_history.shape[0], 1, nlat)
    (packets,) = call(
        packet_kernel,
        [((lon_n, 8, own_sites), F32)],
        "vvv",
        name="packet",
        flops=575000000,
        far_in=(0, 1, 2),
    )(site_cells[None], observed, site_weight)
    gathered = lax.all_to_all(packets, "lon", 0, 0)
    to_west, to_east, to_west2, to_east2, to_low, to_high = call(
        functools.partial(message_kernel, rad_n=rad_n),
        [(shape, F32) for shape in [first_column] * 2 + [column] * 2 + [layers] * 2],
        "vvv",
        name="messages",
        flops=2875000000,
        far_in=(0, 1, 2),
    )(logvisc, displacement, ice_history)
    west = lax.ppermute(to_east, "lon", eastward)
    east = lax.ppermute(to_west, "lon", westward)
    low, high = across_rad(to_low, to_high)
    west2 = lax.ppermute(to_east2, "lon", eastward)
    east2 = lax.ppermute(to_west2, "lon", westward)

    k_high, k_low, data = call(
        functools.partial(weights_kernel, total_lon=total_lon),
        [((COLS, sites, nlat), BF16)] * 2 + [((8, sites), F32)],
        "v",
        scratch=[pltpu.VMEM((16, sites), F32)],
        name="site_weights",
        flops=3680000000,
        held_out=(0, 1, 2),
    )(gathered)

    padded = -(-3 * sites // 128) * 128
    partial, to_corner_low, to_corner_high = call(
        functools.partial(forward_kernel, rad_n=rad_n),
        [((devices, 1, padded), F32), ((8, 1, nlat), F32), ((8, 1, nlat), F32)],
        "s" + "v" * 9,
        scratch=[
            pltpu.VMEM(shape + row, F32)
            for shape in [(half,)] * 2 + [(3, half)] * 3 + [(half,)] * 3 + [(half + 1,), (half,)]
            + [(3, half)] * 2 + [(6,)]
        ],
        name="forward",
        flops=6325000000,
        held_in=(8, 9),
        far_in=(1, 2, 7),
        near_out=(0, 1, 2),
    )(load_steps, logvisc, displacement, west, east, low, high, ice_history, k_high, k_low)
    predicted = lax.all_to_all(partial, ("lon", "rad"), 0, 0)

    corner_low, corner_high = across_rad(to_corner_low, to_corner_high)
    (blocks,) = call(
        functools.partial(prepare_kernel, rad_n=rad_n),
        [((half + 1, BLOCK) + row, F32)],
        "s" + "v" * 12,
        scratch=[
            pltpu.VMEM(shape + row, F32)
            for shape in [(half + 2,), (3, half + 2)] * 2 + [(8, half)] * 2 + [(half + 1, BLOCK)]
        ]
        + [pltpu.SemaphoreType.DMA((half + 1,))],
        name="prepare",
        flops=8050000000,
        far_in=(1, 2, 3, 4),
        far_out=(0,),
    )(
        load_steps, logvisc, momentum, displacement, ice_history, west, east, west2, east2, low,
        high, corner_low, corner_high,
    )

    new_logvisc, half_momentum, misfit = call(
        functools.partial(gradient_kernel, scale=scale, rad_n=rad_n),
        [((nr, nl, nlat), F32), ((nr, nl, nlat), F32), ((1, 1), F32)],
        "vvvvvh",
        scratch=[
            pltpu.VMEM(shape + row, F32)
            for shape in [(3,), (10, 3), (half + 1, BLOCK), (3, half), (3, half), (9, half)]
            + [(half,)] * 2
        ]
        + [pltpu.SemaphoreType.DMA((half + 1,))],
        name="gradient",
        flops=6900000000,
        held_in=(2, 3, 4),
        far_in=(0, 5),
    )(logvisc, predicted, data, k_high, k_low, blocks)
    return (new_logvisc, half_momentum, misfit.reshape(1))


def solution(mesh):
    return jax.shard_map(
        body,
        mesh=mesh,
        in_specs=(
            P("rad", "lon", None),
            P("rad", "lon", None),
            P(None, "rad", "lon", None),
            P(None, "lon", None),
            P(),
            P("lon"),
            P(None, "lon"),
            P(None, "lon"),
        ),
        out_specs=(P("rad", "lon", None), P("rad", "lon", None), P()),
        check_vma=False,
    )
```

```python
import functools
import math

import jax
import jax.numpy as jnp
from jax import lax
from jax.experimental import pallas as pl
from jax.experimental.pallas import tpu as pltpu
from jax.sharding import PartitionSpec as P

RELAX_RATE = 0.05
KERNEL_WIDTH = 0.1
KERNEL_WAVE = 40.0
PRIOR_WEIGHT = 0.1
COLS = 8
F32 = jnp.float32
BF16 = jnp.bfloat16
VMEM_LIMIT = 40 * 1024 * 1024


def reciprocal(x):
    r = pl.reciprocal(x, approx=True)
    return r * (2.0 - x * r)


def lat_next(x):
    return pltpu.roll(x, x.shape[1] - 1, 1)


def lat_prev(x):
    return pltpu.roll(x, 1, 1)


def lon_next(x):
    return pltpu.roll(x, 7, 0)


def lon_prev(x):
    return pltpu.roll(x, 1, 0)


def swap_halves(x):
    return pltpu.roll(x, 4, 0)


def pack(low, high):
    return jnp.concatenate([low, high], axis=0)


class Shape:
    def __init__(self, nr, width, rad_n):
        self.nr, self.width, self.half = nr, width, nr // 2
        sub = lax.broadcasted_iota(jnp.int32, (8, width), 0)
        lane = lax.broadcasted_iota(jnp.int32, (8, width), 1)
        self.lon = sub % 4
        self.lower = sub < 4
        self.upper = sub >= 4
        self.western = self.lon < 2
        self.not_last = lane < width - 1
        self.not_first = lane > 0
        self.rate = 4.0 / (nr * rad_n)
        at = lax.axis_index("rad")
        self.has_low = (at > 0).astype(F32)
        self.has_high = (at < rad_n - 1).astype(F32)
        layer = jnp.where(self.lower, 0, self.half) + (at * nr - (nr * rad_n - 1))
        self.first_weight = jnp.exp(layer.astype(F32) * self.rate)

    def step(self, i):
        return math.exp(self.rate * i)

    def sides(self, west, east):
        return jnp.where(
            self.lower,
            jnp.where(self.western, west[0], east[0]),
            jnp.where(self.western, west[1], east[1]),
        )


def face(a, b):
    return 2.0 * a * b * reciprocal(a + b)


def sin_pi(u):
    z = u * u
    p = 0.0772201269865036
    p = p * z - 0.5980451703071594
    p = p * z + 2.5500314235687256
    p = p * z - 5.1677069664001465
    p = p * z + 3.141592502593994
    return p * u


TURNS = KERNEL_WAVE / (2.0 * math.pi)


def site_kernel(turns):
    s = sin_pi(turns - jnp.round(turns))
    return (reciprocal(1.0 + turns * (1.0 / (KERNEL_WIDTH * TURNS))) + 0.5) - s * s


def message_kernel(
    v_ref, s_ref, ice_ref, cells_ref, obs_ref, wt_ref,
    west_ref, east_ref, west2_ref, east2_ref, low_ref, high_ref, packet_ref, *, rad_n,
):
    nr, nl, width = v_ref.shape
    packet = jnp.concatenate(
        [
            cells_ref[...].astype(F32),
            obs_ref[...],
            wt_ref[...],
            jnp.zeros((1, obs_ref.shape[1]), F32),
        ],
        axis=0,
    )
    for n in range(packet_ref.shape[0]):
        packet_ref[n] = packet

    def field(n, r):
        return v_ref[r] if n == 0 else s_ref[n - 1, r]

    for r in range(nr):
        for n in range(4):
            x = field(n, r)
            west_ref[n * nr + r] = x[0:1, :]
            east_ref[n * nr + r] = x[nl - 1 : nl, :]
            west2_ref[n * nr + r] = x[1:2, :]
            east2_ref[n * nr + r] = x[nl - 2 : nl - 1, :]
    for n in range(ice_ref.shape[0]):
        west_ref[4 * nr + n] = ice_ref[n, 0:1, :]
        east_ref[4 * nr + n] = ice_ref[n, nl - 1 : nl, :]
    bottom = lax.axis_index("rad") == 0
    for n in range(4):
        for k in range(2):
            down, up = field(n, k), field(n, nr - 1 - k)
            if rad_n == 2:
                low_ref[n + 4 * k] = jnp.where(bottom, up, down)
            else:
                low_ref[n + 4 * k] = down
                high_ref[n + 4 * k] = up
    if rad_n == 2:
        high_ref[...] = jnp.zeros_like(high_ref)


def weights_kernel(gathered_ref, high_ref, low_ref, data_ref, rows_ref, *, total_lon):
    devices, _, own = gathered_ref.shape
    sites = high_ref.shape[1]
    width = high_ref.shape[2]
    for d in range(devices):
        data_ref[:, d * own : (d + 1) * own] = gathered_ref[d]
    cells = data_ref[0:1, :]
    lon = jnp.floor((cells + 0.5) * (1.0 / width))
    theta = (cells - lon * width + 0.5) * (1.0 / width)
    phi = lon * (1.0 / total_lon)

    def sin_whole(t):
        return sin_pi(jnp.minimum(t, 1.0 - t))

    def circle(t):
        u = t - jnp.round(t)
        s = sin_pi(u)
        y = jnp.abs(2.0 * u)
        wave = sin_pi(jnp.minimum(y, 1.0 - y))
        return 1.0 - 2.0 * s * s, jnp.where(u < 0, -wave, wave)

    site_cos, site_sin = circle(phi)
    first = lax.axis_index("lon") * 4 - 2 + total_lon
    col = (lax.broadcasted_iota(jnp.int32, (COLS, sites), 0) + first).astype(F32)
    turns = col * (1.0 / total_lon)
    col_cos, col_sin = circle(turns - jnp.floor(turns))
    rows_ref[0:8, :] = col_cos * site_cos + col_sin * site_sin
    rows_ref[8:9, :] = (-2.0 * TURNS) * sin_pi(0.5 - theta)
    rows_ref[9:10, :] = (-2.0 * TURNS) * sin_whole(theta)
    rows_ref[10:16, :] = jnp.zeros((6, sites), F32)
    columns = jnp.transpose(rows_ref[...])
    lat = (lax.broadcasted_iota(jnp.int32, (16, width), 1).astype(F32) + 0.5) * (1.0 / width)
    cos_lat = sin_pi(0.5 - lat)
    sin_lat = sin_whole(lat)
    for at in range(0, sites, 16):
        part = columns[at : at + 16, :]
        a = 2.0 * TURNS + part[:, 8:9] * cos_lat
        b = part[:, 9:10] * sin_lat
        for n in range(COLS):
            k = site_kernel(a + b * part[:, n : n + 1])
            high = k.astype(BF16)
            high_ref[n, at : at + 16, :] = high
            low_ref[n, at : at + 16, :] = (k - high.astype(F32)).astype(BF16)


def two_parts(x):
    high = x.astype(BF16).astype(F32)
    return jnp.concatenate([high, x - high], axis=0).astype(BF16)


def product(x, high, low, contract):
    dims = (((1,), (contract,)), ((), ()))
    parts = two_parts(x)
    both = lax.dot_general(parts, high, dims, preferred_element_type=F32)
    rest = lax.dot_general(parts, low, dims, preferred_element_type=F32)
    return both[0:8, :] + (both[8:16, :] + rest[0:8, :])


def forward_kernel(
    steps_ref, v_ref, s_ref, west_ref, east_ref, low_ref, high_ref, ice_ref, k_high_ref, k_low_ref,
    pred_ref, corner_low_ref, corner_high_ref,
    fluid_ref, fluid_north_ref, field_ref, north_ref, south_ref, h_east_ref, h_north_ref,
    h_south_ref, h_up_ref, h_cut_ref, next_ref, next_north_ref, surf_ref, *, rad_n,
):
    nr, nl, width = v_ref.shape
    shape = Shape(nr, width, rad_n)
    half = shape.half
    lower, lon = shape.lower, shape.lon
    ends = (lon == 0) | (lon == 3)

    bottom = lax.axis_index("rad") == 0
    for n in range(4):
        for k, ref in enumerate((west_ref, east_ref)):
            down, up = ref[n * nr], ref[n * nr + nr - 1]
            if rad_n == 2:
                corner_low_ref[2 * n + k] = jnp.where(bottom, up, down)
            else:
                corner_low_ref[2 * n + k] = down
                corner_high_ref[2 * n + k] = up
    if rad_n == 2:
        corner_high_ref[...] = jnp.zeros_like(corner_high_ref)

    for i in range(half):
        f = jnp.exp(-pack(v_ref[i], v_ref[i + half]))
        fluid_ref[i] = f
        fluid_north_ref[i] = lat_next(f)
        for c in range(3):
            x = pack(s_ref[c, i], s_ref[c, i + half])
            field_ref[c, i] = x
            north_ref[c, i] = lat_next(x)
            south_ref[c, i] = lat_prev(x)
    for i in range(half):
        h_north = jnp.where(shape.not_last, face(fluid_ref[i], fluid_north_ref[i]), 0.0)
        h_north_ref[i] = h_north
        h_south_ref[i] = lat_prev(h_north)

    ring = pack(shape.has_low * jnp.exp(-low_ref[0]), shape.has_high * jnp.exp(-high_ref[0]))
    h_ring = face(ring, jnp.where(lower, fluid_ref[0], fluid_ref[half - 1]))
    seam = face(swap_halves(fluid_ref[0]), fluid_ref[half - 1])
    h_up_ref[half] = jnp.where(lower, seam, 0.0)
    h_up_ref[0] = swap_halves(h_up_ref[half])
    load = ice_ref[steps_ref[0]] * (1.0 - shape.has_high)
    load = pack(jnp.zeros_like(load), load)
    carry = [h_up_ref[0] * (field_ref[c, 0] - swap_halves(field_ref[c, half - 1])) for c in range(3)]
    for i in range(half):

        def side(n):
            return shape.sides(
                (west_ref[n * nr + i], west_ref[n * nr + i + half]),
                (east_ref[n * nr + i], east_ref[n * nr + i + half]),
            )

        f = fluid_ref[i]
        h_cut = jnp.where(ends, face(f, jnp.exp(-side(0))), 0.0)
        h_cut_ref[i] = h_cut
        h_east = jnp.where(lon < 3, face(f, lon_next(f)), 0.0)
        h_east_ref[i] = h_east
        if i < half - 1:
            h_up_ref[i + 1] = face(f, fluid_ref[i + 1])
        h_north, h_south, h_up = h_north_ref[i], h_south_ref[i], h_up_ref[i + 1]
        for c in range(3):
            x = field_ref[c, i]
            above = field_ref[c, i + 1] if i < half - 1 else swap_halves(field_ref[c, 0])
            east = h_east * (lon_next(x) - x)
            up = h_up * (above - x)
            total = (east - lon_prev(east)) + (up - carry[c]) + h_cut * (side(1 + c) - x)
            total = total + h_north * (north_ref[c, i] - x) + h_south * (south_ref[c, i] - x)
            if i in (0, half - 1):
                beyond = h_ring * (pack(low_ref[1 + c], high_ref[1 + c]) - x)
                if i == 0:
                    total = total + jnp.where(lower, beyond, 0.0)
                if i == half - 1:
                    total = total + jnp.where(lower, 0.0, beyond)
            s1 = x + RELAX_RATE * total
            if c == 0 and i == half - 1:
                s1 = s1 - load
            next_ref[c, i] = s1
            next_north_ref[c, i] = lat_next(s1)
            carry[c] = up

    zero = jnp.zeros((8, width), F32)
    column, east, north, cut = [zero] * 3, [zero] * 3, [zero] * 3, [zero] * 3
    below = [swap_halves(next_ref[c, half - 1]) for c in range(3)]
    for i in range(half):
        weight = shape.step(i)
        g_east = weight * h_east_ref[i]
        g_north = weight * h_north_ref[i]
        g_cut = weight * h_cut_ref[i]
        g_low = (RELAX_RATE * (weight - shape.step(i - 1))) * h_up_ref[i]
        for c in range(3):
            x = next_ref[c, i]
            column[c] = column[c] + (weight * x - g_low * (x - below[c]))
            east[c] = east[c] + g_east * (lon_next(x) - x)
            north[c] = north[c] + g_north * (next_north_ref[c, i] - x)
            cut[c] = cut[c] + g_cut * x
            below[c] = x
    top = shape.step(half - 1)
    g_ring = (RELAX_RATE * h_ring) * jnp.where(
        lower, shape.step(-1) - 1.0, shape.step(half) - top
    )
    for c in range(3):
        inner = jnp.where(lower, next_ref[c, 0], next_ref[c, half - 1])

        def folded(x):
            x = shape.first_weight * x
            return x + swap_halves(x)

        sum_east = folded(east[c])
        sum_north = folded(north[c])
        sum_cut = folded(cut[c])
        own = folded(column[c] + g_ring * inner)
        spread = (sum_east - lon_prev(sum_east)) + (sum_north - lat_prev(sum_north)) - sum_cut
        own = own + RELAX_RATE * spread
        if c == 0:
            second = ice_ref[steps_ref[1]] * (1.0 - shape.has_high)
            own = own - pack(second, second)
        surf_ref[0, c : c + 1, :] = RELAX_RATE * sum_cut[0:1, :]
        for col in range(4):
            surf_ref[col + 1, c : c + 1, :] = own[col : col + 1, :]
        surf_ref[5, c : c + 1, :] = RELAX_RATE * sum_cut[3:4, :]
    total = None
    for col in range(6):
        surf_ref[col, 3:8, :] = jnp.zeros((5, width), F32)
        term = product(surf_ref[col], k_high_ref[col + 1], k_low_ref[col + 1], 1)
        total = term if total is None else total + term
    sites = total.shape[1]
    spare = pred_ref.shape[2] - 3 * sites
    flat = [total[c : c + 1, :] for c in range(3)]
    if spare > 0:
        flat.append(jnp.zeros((1, spare), F32))
    flat = jnp.concatenate(flat, axis=1)
    for n in range(pred_ref.shape[0]):
        pred_ref[n] = flat


FIELD, FIELD_SIDE, BOTH, BOTH_SIDE, SHARE, FLUID, SIDE, BASE, BLOCK = 0, 3, 6, 9, 12, 18, 19, 24, 25
RING, LAST, LOW, LOW_BOTH, HIGH, HIGH_BOTH, ENDS = 0, 5, 12, 15, 18, 21, 24


def prepare_kernel(
    steps_ref, v_ref, m_ref, s_ref, ice_ref, west_ref, east_ref, west2_ref, east2_ref, low_ref,
    high_ref, corner_low_ref, corner_high_ref, blocks_ref,
    fluid_ref, field_ref, fluid_side_ref, field_side_ref, north_ref, south_ref, out_ref, sems,
    *, rad_n,
):
    nr, nl, width = v_ref.shape
    shape = Shape(nr, width, rad_n)
    half = shape.half
    lower, lon, western = shape.lower, shape.lon, shape.western

    def share(f, other):
        return other * reciprocal(f + other)

    def safe_share(f, other):
        return other * reciprocal(jnp.maximum(f + other, 1e-30))

    def north_of(f):
        return jnp.where(shape.not_last, lat_next(f), 0.0)

    def south_of(f):
        return jnp.where(shape.not_first, lat_prev(f), 0.0)

    def two(ref, n, i):
        return ref[n * nr + i], ref[n * nr + i + half]

    def corner(ref, n):
        return jnp.where(western, ref[2 * n], ref[2 * n + 1])

    def pack_row(i):
        f = jnp.exp(-pack(v_ref[i], v_ref[i + half]))
        f_side = jnp.exp(-shape.sides(two(west_ref, 0, i), two(east_ref, 0, i)))
        fluid_ref[i + 1] = f
        fluid_side_ref[i + 1] = f_side
        north_ref[0, i], south_ref[0, i] = north_of(f), south_of(f)
        north_ref[1, i], south_ref[1, i] = north_of(f_side), south_of(f_side)
        for c in range(3):
            x = pack(s_ref[c, i], s_ref[c, i + half])
            x_side = shape.sides(two(west_ref, 1 + c, i), two(east_ref, 1 + c, i))
            field_ref[c, i + 1] = x
            field_side_ref[c, i + 1] = x_side
            north_ref[2 + c, i], south_ref[2 + c, i] = lat_next(x), lat_prev(x)
            north_ref[5 + c, i], south_ref[5 + c, i] = lat_next(x_side), lat_prev(x_side)

    lead = min(2, half - 1)
    for i in [half - 1] + list(range(lead)):
        pack_row(i)
    ring = pack(shape.has_low * jnp.exp(-low_ref[0]), shape.has_high * jnp.exp(-high_ref[0]))
    ring_side = jnp.where(
        lower,
        shape.has_low * jnp.exp(-corner(corner_low_ref, 0)),
        shape.has_high * jnp.exp(-corner(corner_high_ref, 0)),
    )
    ring_field = [pack(low_ref[1 + c], high_ref[1 + c]) for c in range(3)]
    ring_field_side = [
        jnp.where(lower, corner(corner_low_ref, 1 + c), corner(corner_high_ref, 1 + c))
        for c in range(3)
    ]

    def close(ref, ring):
        ref[0] = jnp.where(lower, ring, swap_halves(ref[half]))
        ref[half + 1] = jnp.where(lower, swap_halves(ref[1]), ring)

    close(fluid_ref, ring)
    close(fluid_side_ref, ring_side)
    for c in range(3):
        close(field_ref.at[c], ring_field[c])
        close(field_side_ref.at[c], ring_field_side[c])

    def coefficients(f, shares, here, above, below):
        scaled = (2.0 * RELAX_RATE) * f
        weighted = scaled * here
        radial = scaled * (shares[4] * (above - here) + shares[5] * (below - here))
        return [weighted * shares[n] for n in range(4)] + [radial]

    def relaxed(f, shares, s, others):
        total = shares[0] * (others[0] - s)
        for n in range(1, 6):
            total = total + shares[n] * (others[n] - s)
        return s + (2.0 * RELAX_RATE) * (f * total)

    load = ice_ref[steps_ref[0]]
    load = (1.0 - shape.has_high) * pack(jnp.zeros_like(load), load)
    load_side = jnp.where(
        western, west_ref[4 * nr + steps_ref[0]], east_ref[4 * nr + steps_ref[0]]
    )
    load_side = (1.0 - shape.has_high) * jnp.where(lower, 0.0, load_side)

    copies = []
    both_ends = {}

    def send(i):
        copies.append(pltpu.make_async_copy(out_ref.at[i], blocks_ref.at[i], sems.at[i]))
        copies[-1].start()

    for i in range(half):
        if i + lead < half - 1:
            pack_row(i + lead)
        f, f_side = fluid_ref[i + 1], fluid_side_ref[i + 1]
        shares = [
            share(f, jnp.where(lon == 3, f_side, lon_next(f))),
            share(f, jnp.where(lon == 0, f_side, lon_prev(f))),
            share(f, north_ref[0, i]),
            share(f, south_ref[0, i]),
            share(f, fluid_ref[i + 2]),
            share(f, fluid_ref[i]),
        ]
        for n in range(6):
            out_ref[i, SHARE + n] = shares[n]
        out_ref[i, FLUID] = f
        if i == half - 1:
            for n in range(6):
                out_ref[half, LAST + n] = shares[n]
            out_ref[half, LAST + 6] = f
        out_ref[i, BASE] = pack(
            m_ref[i] - (0.5 * PRIOR_WEIGHT) * v_ref[i],
            m_ref[i + half] - (0.5 * PRIOR_WEIGHT) * v_ref[i + half],
        )
        f_far = jnp.exp(-shape.sides(two(west2_ref, 0, i), two(east2_ref, 0, i)))
        side_shares = [
            share(f_side, jnp.where(western, f, f_far)),
            share(f_side, jnp.where(western, f_far, f)),
            share(f_side, north_ref[1, i]),
            share(f_side, south_ref[1, i]),
            share(f_side, fluid_side_ref[i + 2]),
            share(f_side, fluid_side_ref[i]),
        ]
        side = coefficients(
            f_side, side_shares, shape.step(i), shape.step(i + 1), shape.step(i - 1)
        )
        for n in range(5):
            out_ref[i, SIDE + n] = side[n]
        for c in range(3):
            s, s_side = field_ref[c, i + 1], field_side_ref[c, i + 1]
            s_far = shape.sides(two(west2_ref, 1 + c, i), two(east2_ref, 1 + c, i))
            others = [
                jnp.where(lon == 3, s_side, lon_next(s)),
                jnp.where(lon == 0, s_side, lon_prev(s)),
                north_ref[2 + c, i],
                south_ref[2 + c, i],
                field_ref[c, i + 2],
                field_ref[c, i],
            ]
            both = s + relaxed(f, shares, s, others)
            others = [
                jnp.where(western, s, s_far),
                jnp.where(western, s_far, s),
                north_ref[5 + c, i],
                south_ref[5 + c, i],
                field_side_ref[c, i + 2],
                field_side_ref[c, i],
            ]
            both_side = s_side + relaxed(f_side, side_shares, s_side, others)
            if c == 0 and i == half - 1:
                both = both - load
                both_side = both_side - load_side
            out_ref[i, FIELD + c] = s
            out_ref[i, FIELD_SIDE + c] = s_side
            out_ref[i, BOTH + c] = both
            out_ref[i, BOTH_SIDE + c] = both_side
            if i in (0, half - 1):
                both_ends[c, i] = both
        send(i)
    outer = pack(shape.has_low * jnp.exp(-low_ref[4]), shape.has_high * jnp.exp(-high_ref[4]))
    inner = jnp.where(lower, fluid_ref[1], fluid_ref[half])
    ring_shares = [
        safe_share(ring, jnp.where(lon == 3, ring_side, lon_next(ring))),
        safe_share(ring, jnp.where(lon == 0, ring_side, lon_prev(ring))),
        safe_share(ring, north_of(ring)),
        safe_share(ring, south_of(ring)),
        safe_share(ring, outer),
        safe_share(ring, inner),
    ]
    ring_coefficients = coefficients(
        ring,
        ring_shares,
        jnp.where(lower, shape.step(-1), shape.step(half)),
        jnp.where(lower, shape.step(-2), shape.step(half + 1)),
        jnp.where(lower, shape.step(0), shape.step(half - 1)),
    )
    for n in range(5):
        out_ref[half, RING + n] = ring_coefficients[n]
    ring_both = []
    for c in range(3):
        s, s_side = ring_field[c], ring_field_side[c]
        others = [
            jnp.where(lon == 3, s_side, lon_next(s)),
            jnp.where(lon == 0, s_side, lon_prev(s)),
            lat_next(s),
            lat_prev(s),
            pack(low_ref[5 + c], high_ref[5 + c]),
            jnp.where(lower, field_ref[c, 1], field_ref[c, half]),
        ]
        ring_both.append(s + relaxed(ring, ring_shares, s, others))
    low_step = shape.step(0) - shape.step(-1)
    high_step = shape.step(half) - shape.step(half - 1)
    for c in range(3):
        first, last = both_ends[c, 0], both_ends[c, half - 1]
        out_ref[half, LOW + c] = field_ref[c, 1] - field_ref[c, 0]
        out_ref[half, LOW_BOTH + c] = low_step * (
            first - jnp.where(lower, ring_both[c], swap_halves(last))
        )
        out_ref[half, HIGH + c] = field_ref[c, half + 1] - field_ref[c, half]
        out_ref[half, HIGH_BOTH + c] = high_step * (
            jnp.where(lower, swap_halves(first), ring_both[c]) - last
        )
    out_ref[half, ENDS:BLOCK] = jnp.zeros((BLOCK - ENDS, 8, width), F32)
    send(half)
    for copy in copies:
        copy.wait()


AHEAD = 8


def gradient_kernel(
    v_ref, pred_ref, data_ref, k_high_ref, k_low_ref, blocks_ref,
    new_ref, half_ref, misfit_ref, v_in_ref, new_out_ref, half_out_ref, sa_ref, d_ref, in_ref, e_ref, side_ref, north_ref, product_ref,
    total_ref, k_low_in_ref, sems, out_sems, *, scale, rad_n,
):
    nr, nl, width = v_ref.shape
    shape = Shape(nr, width, rad_n)
    half = shape.half
    sites = k_high_ref.shape[1]
    lon, lower = shape.lon, shape.lower
    copies = [
        pltpu.make_async_copy(blocks_ref.at[i], in_ref.at[i], sems.at[i]) for i in range(half + 1)
    ]
    low_copy = pltpu.make_async_copy(k_low_ref, k_low_in_ref, sems.at[half + 1])
    low_copy.start()
    copies[half].start()
    for i in range(min(AHEAD, half)):
        copies[i].start()
    v_copy = pltpu.make_async_copy(v_ref, v_in_ref, sems.at[half + 2])
    v_copy.start()
    groups = []
    for first in range(0, half, 6):
        group = []
        for at in (first, first + half):
            for inner, outer in ((half_out_ref, half_ref), (new_out_ref, new_ref)):
                rows = slice(at, at + min(6, half - first))
                sem = out_sems.at[4 * len(groups) + len(group)]
                group.append(pltpu.make_async_copy(inner.at[rows], outer.at[rows], sem))
        groups.append(group)
    ends_ref = in_ref.at[half]

    flat = pred_ref[0]
    for n in range(1, pred_ref.shape[0]):
        flat = flat + pred_ref[n]
    predicted = jnp.concatenate(
        [flat[:, c * sites : (c + 1) * sites] for c in range(3)], axis=0
    )
    weight = data_ref[4:7, :]
    weighted = weight * (predicted * scale - data_ref[1:4, :])
    squares = jnp.sum(weighted * weighted, axis=1, keepdims=True)
    misfit_ref[...] = jnp.sum(squares, axis=0, keepdims=True) * (1.0 / (3 * sites))
    pulled = (weight * weighted) * scale
    pulled = jnp.concatenate([pulled, jnp.zeros((5, sites), F32)], axis=0)
    for col in range(COLS):
        if col == 0:
            low_copy.wait()
        spread = product(pulled, k_high_ref[col], k_low_in_ref[col], 0)
        for c in range(3):
            sa_ref[c, col : col + 1, :] = spread[c : c + 1, :]

    for c in range(3):
        x = sa_ref[c]

        def window(start):
            return shape.first_weight * jnp.where(
                lower,
                x if start == 0 else pltpu.roll(x, 8 - start, 0),
                x if start == 4 else pltpu.roll(x, (4 - start) % 8, 0),
            )

        own = window(2)
        east = window(3)
        west = window(1)
        outside = jnp.where(lon < 2, west, east)
        d_ref[0, c] = east - own
        d_ref[1, c] = west - own
        d_ref[2, c] = lat_next(own) - own
        d_ref[3, c] = lat_prev(own) - own
        d_ref[4, c] = own
        d_ref[5, c] = jnp.where(lon < 2, own, window(4)) - outside
        d_ref[6, c] = jnp.where(lon < 2, window(0), own) - outside
        d_ref[7, c] = lat_next(outside) - outside
        d_ref[8, c] = lat_prev(outside) - outside
        d_ref[9, c] = outside

    def change(coeffs, first):
        out = []
        for c in range(3):
            total = coeffs[0] * d_ref[first, c]
            for n in range(1, 5):
                total = total + coeffs[n] * d_ref[first + n, c]
            out.append(total)
        return out

    above, below = shape.step(1) - 1.0, shape.step(-1) - 1.0

    def own_change(ref, at, fluid, i):
        shares = [ref[at + n] for n in range(6)]
        scaled = (2.0 * RELAX_RATE * shape.step(i)) * fluid
        coeffs = shares[:4] + [above * shares[4] + below * shares[5]]
        return [scaled * x for x in change(coeffs, 0)]

    def first_pass(i):
        if i % 2 == 0:

            @pl.when(lax.axis_index("rad") >= 0)
            def _():
                for n in range(i, min(i + 2, half)):
                    copies[n].wait()
                    if n + AHEAD < half:
                        copies[n + AHEAD].start()

        e = own_change(in_ref.at[i], SHARE, in_ref[i, FLUID], i)
        side = change([in_ref[i, SIDE + n] for n in range(5)], 5)
        for c in range(3):
            e_ref[c, i] = e[c]
            side_ref[c, i] = side[c]
            north_ref[c, i] = lat_next(in_ref[i, FIELD + c])
            north_ref[3 + c, i] = lat_next(in_ref[i, BOTH + c])
            north_ref[6 + c, i] = lat_next(e[c])

    def second_pass(i, p_down):
        here, step = shape.step(i), shape.step(i + 1) - shape.step(i)
        weighted = [0.0] * 4
        plain = [0.0] * 4
        for c in range(3):
            s, s_side = in_ref[i, FIELD + c], in_ref[i, FIELD_SIDE + c]
            both, both_side = in_ref[i, BOTH + c], in_ref[i, BOTH_SIDE + c]
            e, e_side = e_ref[c, i], side_ref[c, i]

            def differences(x, x_side, x_north):
                return [jnp.where(lon == 3, x_side, lon_next(x)) - x, x_side - x, x_north - x]

            d_field = differences(s, s_side, north_ref[c, i])
            d_both = differences(both, both_side, north_ref[3 + c, i])
            d_e = differences(e, e_side, north_ref[6 + c, i])
            if i < half - 1:
                d_field.append(in_ref[i + 1, FIELD + c] - s)
                d_both.append(step * (in_ref[i + 1, BOTH + c] - both))
                d_e.append(e_ref[c, i + 1] - e)
            else:
                d_field.append(ends_ref[HIGH + c])
                d_both.append(ends_ref[HIGH_BOTH + c])
                d_e.append(jnp.where(lower, swap_halves(e_ref[c, 0]), ring[c]) - e)
            slopes = [d_ref[0, c], d_ref[1, c], d_ref[2, c], d_ref[4, c]]
            for n in range(4):
                weighted[n] = weighted[n] + d_both[n] * slopes[n]
                plain[n] = plain[n] + d_field[n] * d_e[n]
        p_east, p_cut, p_north = [here * weighted[n] + plain[n] for n in range(3)]
        p_up = weighted[3] + plain[3]
        p_west = jnp.where(lon == 0, p_cut, lon_prev(p_east))
        product_ref[i] = lat_prev(p_north)
        total = None
        for n, x in ((0, p_east), (1, p_west), (2, p_north), (4, p_up), (5, p_down)):
            share = in_ref[i, SHARE + n]
            term = (share * share) * x
            total = term if total is None else total + term
        total_ref[i] = total
        return p_up

    def third_pass(i):
        share = in_ref[i, SHARE + 3]
        total = total_ref[i] + (share * share) * product_ref[i]
        total = in_ref[i, BASE] - RELAX_RATE * (in_ref[i, FLUID] * total)
        half_out_ref[i] = total[0:4, :]
        half_out_ref[i + half] = total[4:8, :]
        new_out_ref[i] = v_in_ref[i] + total[0:4, :]
        new_out_ref[i + half] = v_in_ref[i + half] + total[4:8, :]

    copies[half].wait()
    ring = change([ends_ref[RING + n] for n in range(5)], 0)
    e_last = own_change(ends_ref, LAST, ends_ref[LAST + 6], half - 1)
    lead = min(2, half)
    for i in range(lead):
        first_pass(i)
    p_down = None
    for c in range(3):
        e_low = jnp.where(lower, ring[c], swap_halves(e_last[c]))
        term = ends_ref[LOW_BOTH + c] * d_ref[4, c] + ends_ref[LOW + c] * (e_ref[c, 0] - e_low)
        p_down = term if p_down is None else p_down + term
    for i in range(half):
        if i + lead < half:
            first_pass(i + lead)
        p_down = second_pass(i, p_down)
        if i == 1:
            v_copy.wait()
        if i > 0:
            third_pass(i - 1)
        if i % 6 == 0 and i > 0:

            @pl.when(lax.axis_index("rad") >= 0)
            def _():
                for copy in groups[i // 6 - 1]:
                    copy.start()

    if half == 1:
        v_copy.wait()
    third_pass(half - 1)
    for copy in groups[-1]:
        copy.start()
    for group in groups:
        for copy in group:
            copy.wait()


def call(
    kernel, outs, ins, scratch=(), flops=1, name=None, held_in=(), held_out=(), far_in=(),
    far_out=(), near_out=(),
):
    spaces = {"s": pltpu.SMEM, "v": pltpu.VMEM, "h": pltpu.HBM}
    made = pl.pallas_call(
        kernel,
        out_shape=[
            pltpu.VMEM(shape, dtype)
            if n in held_out
            else pltpu.HBM(shape, dtype)
            if n in far_out or n in near_out
            else jax.ShapeDtypeStruct(shape, dtype)
            for n, (shape, dtype) in enumerate(outs)
        ],
        in_specs=[pl.BlockSpec(memory_space=spaces[k]) for k in ins],
        out_specs=[
            pl.BlockSpec(memory_space=pltpu.HBM if n in far_out else pltpu.VMEM)
            for n in range(len(outs))
        ],
        scratch_shapes=list(scratch),
        compiler_params=pltpu.CompilerParams(vmem_limit_bytes=VMEM_LIMIT),
        cost_estimate=pl.CostEstimate(flops=flops, bytes_accessed=1 << 20, transcendentals=0),
        name=name,
    )

    def run(*args):
        return made(
            *[
                pltpu.with_memory_space_constraint(a, pltpu.VMEM if n in held_in else pltpu.HBM)
                if n in held_in or n in far_in
                else a
                for n, a in enumerate(args)
            ]
        )

    return run


def body(
    logvisc, momentum, displacement, ice_history, load_steps, site_cells, observed, site_weight
):
    nr, nl, nlat = logvisc.shape
    own_sites = site_cells.shape[0]
    lon_n = lax.axis_size("lon")
    rad_n = lax.axis_size("rad")
    total_lon = nl * lon_n
    sites = own_sites * lon_n
    devices = lon_n * rad_n
    half = nr // 2
    scale = 1.0 / math.sqrt(total_lon * nlat)
    row = (8, nlat)

    def across_rad(down, up):
        if rad_n == 2:
            both = lax.ppermute(down, "rad", [(0, 1), (1, 0)])
            return both, both
        upward = [(i, i + 1) for i in range(rad_n - 1)]
        downward = [(t, s) for s, t in upward]
        return lax.ppermute(up, "rad", upward), lax.ppermute(down, "rad", downward)

    eastward = [(i, (i + 1) % lon_n) for i in range(lon_n)]
    westward = [(t, s) for s, t in eastward]
    column, layers = (4 * nr, 1, nlat), (8, nl, nlat)
    first_column = (4 * nr + ice_history.shape[0], 1, nlat)
    to_west, to_east, to_west2, to_east2, to_low, to_high, packets = call(
        functools.partial(message_kernel, rad_n=rad_n),
        [
            (shape, F32)
            for shape in [first_column] * 2 + [column] * 2 + [layers] * 2 + [(lon_n, 8, own_sites)]
        ],
        "vvvvvv",
        name="messages",
        flops=2875000000,
        far_in=(0, 1, 2, 3, 4, 5),
    )(logvisc, displacement, ice_history, site_cells[None], observed, site_weight)
    gathered = lax.all_to_all(packets, "lon", 0, 0)
    west = lax.ppermute(to_east, "lon", eastward)
    east = lax.ppermute(to_west, "lon", westward)
    low, high = across_rad(to_low, to_high)
    west2 = lax.ppermute(to_east2, "lon", eastward)
    east2 = lax.ppermute(to_west2, "lon", westward)

    k_high, k_low, data = call(
        functools.partial(weights_kernel, total_lon=total_lon),
        [((COLS, sites, nlat), BF16)] * 2 + [((8, sites), F32)],
        "v",
        scratch=[pltpu.VMEM((16, sites), F32)],
        name="site_weights",
        flops=3680000000,
        held_out=(0, 1, 2),
    )(gathered)

    padded = -(-3 * sites // 128) * 128
    partial, to_corner_low, to_corner_high = call(
        functools.partial(forward_kernel, rad_n=rad_n),
        [((devices, 1, padded), F32), ((8, 1, nlat), F32), ((8, 1, nlat), F32)],
        "s" + "v" * 9,
        scratch=[
            pltpu.VMEM(shape + row, F32)
            for shape in [(half,)] * 2 + [(3, half)] * 3 + [(half,)] * 3 + [(half + 1,), (half,)]
            + [(3, half)] * 2 + [(6,)]
        ],
        name="forward",
        flops=6325000000,
        held_in=(8, 9),
        far_in=(1, 2, 7),
        near_out=(0, 1, 2),
    )(load_steps, logvisc, displacement, west, east, low, high, ice_history, k_high, k_low)
    predicted = lax.all_to_all(partial, ("lon", "rad"), 0, 0)

    corner_low, corner_high = across_rad(to_corner_low, to_corner_high)
    (blocks,) = call(
        functools.partial(prepare_kernel, rad_n=rad_n),
        [((half + 1, BLOCK) + row, F32)],
        "s" + "v" * 12,
        scratch=[
            pltpu.VMEM(shape + row, F32)
            for shape in [(half + 2,), (3, half + 2)] * 2 + [(8, half)] * 2 + [(half + 1, BLOCK)]
        ]
        + [pltpu.SemaphoreType.DMA((half + 1,))],
        name="prepare",
        flops=8050000000,
        far_in=(1, 2, 3, 4),
        far_out=(0,),
    )(
        load_steps, logvisc, momentum, displacement, ice_history, west, east, west2, east2, low,
        high, corner_low, corner_high,
    )

    new_logvisc, half_momentum, misfit = call(
        functools.partial(gradient_kernel, scale=scale, rad_n=rad_n),
        [((nr, nl, nlat), F32), ((nr, nl, nlat), F32), ((1, 1), F32)],
        "hvvvhh",
        scratch=[pltpu.VMEM((nr, nl, nlat), F32)] * 3
        + [
            pltpu.VMEM(shape + row, F32)
            for shape in [(3,), (10, 3), (half + 1, BLOCK), (3, half), (3, half), (9, half)]
            + [(half,)] * 2
        ]
        + [
            pltpu.VMEM((COLS, sites, nlat), BF16),
            pltpu.SemaphoreType.DMA((half + 3,)),
            pltpu.SemaphoreType.DMA((4 * -(-half // 6),)),
        ],
        name="gradient",
        flops=6900000000,
        held_in=(2, 3),
        far_in=(0, 4, 5),
        far_out=(0, 1),
    )(logvisc, predicted, data, k_high, k_low, blocks)
    return (new_logvisc, half_momentum, misfit.reshape(1))


def solution(mesh):
    return jax.shard_map(
        body,
        mesh=mesh,
        in_specs=(
            P("rad", "lon", None),
            P("rad", "lon", None),
            P(None, "rad", "lon", None),
            P(None, "lon", None),
            P(),
            P("lon"),
            P(None, "lon"),
            P(None, "lon"),
        ),
        out_specs=(P("rad", "lon", None), P("rad", "lon", None), P()),
        check_vma=False,
    )
```

```python
import functools
import math

import jax
import jax.numpy as jnp
from jax import lax
from jax.experimental import pallas as pl
from jax.experimental.pallas import tpu as pltpu
from jax.sharding import PartitionSpec as P

RELAX_RATE = 0.05
KERNEL_WIDTH = 0.1
KERNEL_WAVE = 40.0
PRIOR_WEIGHT = 0.1
COLS = 8
F32 = jnp.float32
BF16 = jnp.bfloat16
VMEM_LIMIT = 40 * 1024 * 1024


def reciprocal(x):
    r = pl.reciprocal(x, approx=True)
    return r * (2.0 - x * r)


def lat_next(x):
    return pltpu.roll(x, x.shape[1] - 1, 1)


def lat_prev(x):
    return pltpu.roll(x, 1, 1)


def lon_next(x):
    return pltpu.roll(x, 7, 0)


def lon_prev(x):
    return pltpu.roll(x, 1, 0)


def swap_halves(x):
    return pltpu.roll(x, 4, 0)


def pack(low, high):
    return jnp.concatenate([low, high], axis=0)


class Shape:
    def __init__(self, nr, width, rad_n):
        self.nr, self.width, self.half = nr, width, nr // 2
        sub = lax.broadcasted_iota(jnp.int32, (8, width), 0)
        lane = lax.broadcasted_iota(jnp.int32, (8, width), 1)
        self.lon = sub % 4
        self.lower = sub < 4
        self.upper = sub >= 4
        self.western = self.lon < 2
        self.not_last = lane < width - 1
        self.not_first = lane > 0
        self.rate = 4.0 / (nr * rad_n)
        at = lax.axis_index("rad")
        self.has_low = (at > 0).astype(F32)
        self.has_high = (at < rad_n - 1).astype(F32)
        layer = jnp.where(self.lower, 0, self.half) + (at * nr - (nr * rad_n - 1))
        self.first_weight = jnp.exp(layer.astype(F32) * self.rate)

    def step(self, i):
        return math.exp(self.rate * i)

    def sides(self, west, east):
        return jnp.where(
            self.lower,
            jnp.where(self.western, west[0], east[0]),
            jnp.where(self.western, west[1], east[1]),
        )


def face(a, b):
    return 2.0 * a * b * reciprocal(a + b)


def sin_pi(u):
    z = u * u
    p = 0.0772201269865036
    p = p * z - 0.5980451703071594
    p = p * z + 2.5500314235687256
    p = p * z - 5.1677069664001465
    p = p * z + 3.141592502593994
    return p * u


TURNS = KERNEL_WAVE / (2.0 * math.pi)


def site_kernel(turns):
    s = sin_pi(turns - jnp.round(turns))
    return (reciprocal(1.0 + turns * (1.0 / (KERNEL_WIDTH * TURNS))) + 0.5) - s * s


def message_kernel(
    v_ref, s_ref, ice_ref, cells_ref, obs_ref, wt_ref,
    west_ref, east_ref, west2_ref, east2_ref, low_ref, high_ref, packet_ref, *, rad_n,
):
    nr, nl, width = v_ref.shape
    parts = [cells_ref[...].astype(F32)]
    parts += [ref[c : c + 1, :] for ref in (obs_ref, wt_ref) for c in range(3)]
    packet = jnp.concatenate(parts, axis=1)
    for n in range(packet_ref.shape[0]):
        packet_ref[n] = packet

    def field(n, r):
        return v_ref[r] if n == 0 else s_ref[n - 1, r]

    for r in range(nr):
        for n in range(4):
            x = field(n, r)
            west_ref[n * nr + r] = x[0:1, :]
            east_ref[n * nr + r] = x[nl - 1 : nl, :]
            west2_ref[n * nr + r] = x[1:2, :]
            east2_ref[n * nr + r] = x[nl - 2 : nl - 1, :]
    for n in range(ice_ref.shape[0]):
        west_ref[4 * nr + n] = ice_ref[n, 0:1, :]
        east_ref[4 * nr + n] = ice_ref[n, nl - 1 : nl, :]
    bottom = lax.axis_index("rad") == 0
    for n in range(4):
        for k in range(2):
            down, up = field(n, k), field(n, nr - 1 - k)
            if rad_n == 2:
                low_ref[n + 4 * k] = jnp.where(bottom, up, down)
            else:
                low_ref[n + 4 * k] = down
                high_ref[n + 4 * k] = up
    if rad_n == 2:
        high_ref[...] = jnp.zeros_like(high_ref)


def weights_kernel(gathered_ref, high_ref, low_ref, data_ref, rows_ref, *, total_lon):
    devices, _, own = gathered_ref.shape
    own = own // 7
    sites = high_ref.shape[1]
    width = high_ref.shape[2]
    for d in range(devices):
        packet = gathered_ref[d]
        for k in range(7):
            data_ref[k : k + 1, d * own : (d + 1) * own] = packet[:, k * own : (k + 1) * own]
    data_ref[7:8, :] = jnp.zeros((1, sites), F32)
    cells = data_ref[0:1, :]
    lon = jnp.floor((cells + 0.5) * (1.0 / width))
    theta = (cells - lon * width + 0.5) * (1.0 / width)
    phi = lon * (1.0 / total_lon)

    def sin_whole(t):
        return sin_pi(jnp.minimum(t, 1.0 - t))

    def circle(t):
        u = t - jnp.round(t)
        s = sin_pi(u)
        y = jnp.abs(2.0 * u)
        wave = sin_pi(jnp.minimum(y, 1.0 - y))
        return 1.0 - 2.0 * s * s, jnp.where(u < 0, -wave, wave)

    site_cos, site_sin = circle(phi)
    first = lax.axis_index("lon") * 4 - 2 + total_lon
    col = (lax.broadcasted_iota(jnp.int32, (COLS, sites), 0) + first).astype(F32)
    turns = col * (1.0 / total_lon)
    col_cos, col_sin = circle(turns - jnp.floor(turns))
    rows_ref[0:8, :] = col_cos * site_cos + col_sin * site_sin
    rows_ref[8:9, :] = (-2.0 * TURNS) * sin_pi(0.5 - theta)
    rows_ref[9:10, :] = (-2.0 * TURNS) * sin_whole(theta)
    rows_ref[10:16, :] = jnp.zeros((6, sites), F32)
    columns = jnp.transpose(rows_ref[...])
    lat = (lax.broadcasted_iota(jnp.int32, (16, width), 1).astype(F32) + 0.5) * (1.0 / width)
    cos_lat = sin_pi(0.5 - lat)
    sin_lat = sin_whole(lat)
    for at in range(0, sites, 16):
        part = columns[at : at + 16, :]
        a = 2.0 * TURNS + part[:, 8:9] * cos_lat
        b = part[:, 9:10] * sin_lat
        for n in range(COLS):
            k = site_kernel(a + b * part[:, n : n + 1])
            high = k.astype(BF16)
            high_ref[n, at : at + 16, :] = high
            low_ref[n, at : at + 16, :] = (k - high.astype(F32)).astype(BF16)


def two_parts(x):
    high = x.astype(BF16).astype(F32)
    return jnp.concatenate([high, x - high], axis=0).astype(BF16)


def product(x, high, low, contract):
    dims = (((1,), (contract,)), ((), ()))
    parts = two_parts(x)
    both = lax.dot_general(parts, high, dims, preferred_element_type=F32)
    rest = lax.dot_general(parts, low, dims, preferred_element_type=F32)
    return both[0:8, :] + (both[8:16, :] + rest[0:8, :])


def forward_kernel(
    steps_ref, v_ref, s_ref, west_ref, east_ref, low_ref, high_ref, ice_ref, k_high_ref, k_low_ref,
    pred_ref, corner_low_ref, corner_high_ref,
    fluid_ref, fluid_north_ref, field_ref, north_ref, south_ref, h_east_ref, h_north_ref,
    h_south_ref, h_up_ref, h_cut_ref, next_ref, next_north_ref, surf_ref, *, rad_n,
):
    nr, nl, width = v_ref.shape
    shape = Shape(nr, width, rad_n)
    half = shape.half
    lower, lon = shape.lower, shape.lon
    ends = (lon == 0) | (lon == 3)

    bottom = lax.axis_index("rad") == 0
    for n in range(4):
        for k, ref in enumerate((west_ref, east_ref)):
            down, up = ref[n * nr], ref[n * nr + nr - 1]
            if rad_n == 2:
                corner_low_ref[2 * n + k] = jnp.where(bottom, up, down)
            else:
                corner_low_ref[2 * n + k] = down
                corner_high_ref[2 * n + k] = up
    if rad_n == 2:
        corner_high_ref[...] = jnp.zeros_like(corner_high_ref)

    for i in range(half):
        f = jnp.exp(-pack(v_ref[i], v_ref[i + half]))
        fluid_ref[i] = f
        fluid_north_ref[i] = lat_next(f)
        for c in range(3):
            x = pack(s_ref[c, i], s_ref[c, i + half])
            field_ref[c, i] = x
            north_ref[c, i] = lat_next(x)
            south_ref[c, i] = lat_prev(x)
    for i in range(half):
        h_north = jnp.where(shape.not_last, face(fluid_ref[i], fluid_north_ref[i]), 0.0)
        h_north_ref[i] = h_north
        h_south_ref[i] = lat_prev(h_north)

    ring = pack(shape.has_low * jnp.exp(-low_ref[0]), shape.has_high * jnp.exp(-high_ref[0]))
    h_ring = face(ring, jnp.where(lower, fluid_ref[0], fluid_ref[half - 1]))
    seam = face(swap_halves(fluid_ref[0]), fluid_ref[half - 1])
    h_up_ref[half] = jnp.where(lower, seam, 0.0)
    h_up_ref[0] = swap_halves(h_up_ref[half])
    load = ice_ref[steps_ref[0]] * (1.0 - shape.has_high)
    load = pack(jnp.zeros_like(load), load)
    carry = [h_up_ref[0] * (field_ref[c, 0] - swap_halves(field_ref[c, half - 1])) for c in range(3)]
    for i in range(half):

        def side(n):
            return shape.sides(
                (west_ref[n * nr + i], west_ref[n * nr + i + half]),
                (east_ref[n * nr + i], east_ref[n * nr + i + half]),
            )

        f = fluid_ref[i]
        h_cut = jnp.where(ends, face(f, jnp.exp(-side(0))), 0.0)
        h_cut_ref[i] = h_cut
        h_east = jnp.where(lon < 3, face(f, lon_next(f)), 0.0)
        h_east_ref[i] = h_east
        if i < half - 1:
            h_up_ref[i + 1] = face(f, fluid_ref[i + 1])
        h_north, h_south, h_up = h_north_ref[i], h_south_ref[i], h_up_ref[i + 1]
        for c in range(3):
            x = field_ref[c, i]
            above = field_ref[c, i + 1] if i < half - 1 else swap_halves(field_ref[c, 0])
            east = h_east * (lon_next(x) - x)
            up = h_up * (above - x)
            total = (east - lon_prev(east)) + (up - carry[c]) + h_cut * (side(1 + c) - x)
            total = total + h_north * (north_ref[c, i] - x) + h_south * (south_ref[c, i] - x)
            if i in (0, half - 1):
                beyond = h_ring * (pack(low_ref[1 + c], high_ref[1 + c]) - x)
                if i == 0:
                    total = total + jnp.where(lower, beyond, 0.0)
                if i == half - 1:
                    total = total + jnp.where(lower, 0.0, beyond)
            s1 = x + RELAX_RATE * total
            if c == 0 and i == half - 1:
                s1 = s1 - load
            next_ref[c, i] = s1
            next_north_ref[c, i] = lat_next(s1)
            carry[c] = up

    zero = jnp.zeros((8, width), F32)
    column, east, north, cut = [zero] * 3, [zero] * 3, [zero] * 3, [zero] * 3
    below = [swap_halves(next_ref[c, half - 1]) for c in range(3)]
    for i in range(half):
        weight = shape.step(i)
        g_east = weight * h_east_ref[i]
        g_north = weight * h_north_ref[i]
        g_cut = weight * h_cut_ref[i]
        g_low = (RELAX_RATE * (weight - shape.step(i - 1))) * h_up_ref[i]
        for c in range(3):
            x = next_ref[c, i]
            column[c] = column[c] + (weight * x - g_low * (x - below[c]))
            east[c] = east[c] + g_east * (lon_next(x) - x)
            north[c] = north[c] + g_north * (next_north_ref[c, i] - x)
            cut[c] = cut[c] + g_cut * x
            below[c] = x
    top = shape.step(half - 1)
    g_ring = (RELAX_RATE * h_ring) * jnp.where(
        lower, shape.step(-1) - 1.0, shape.step(half) - top
    )
    for c in range(3):
        inner = jnp.where(lower, next_ref[c, 0], next_ref[c, half - 1])

        def folded(x):
            x = shape.first_weight * x
            return x + swap_halves(x)

        sum_east = folded(east[c])
        sum_north = folded(north[c])
        sum_cut = folded(cut[c])
        own = folded(column[c] + g_ring * inner)
        spread = (sum_east - lon_prev(sum_east)) + (sum_north - lat_prev(sum_north)) - sum_cut
        own = own + RELAX_RATE * spread
        if c == 0:
            second = ice_ref[steps_ref[1]] * (1.0 - shape.has_high)
            own = own - pack(second, second)
        surf_ref[0, c : c + 1, :] = RELAX_RATE * sum_cut[0:1, :]
        for col in range(4):
            surf_ref[col + 1, c : c + 1, :] = own[col : col + 1, :]
        surf_ref[5, c : c + 1, :] = RELAX_RATE * sum_cut[3:4, :]
    total = None
    for col in range(6):
        surf_ref[col, 3:8, :] = jnp.zeros((5, width), F32)
        term = product(surf_ref[col], k_high_ref[col + 1], k_low_ref[col + 1], 1)
        total = term if total is None else total + term
    sites = total.shape[1]
    spare = pred_ref.shape[2] - 3 * sites
    flat = [total[c : c + 1, :] for c in range(3)]
    if spare > 0:
        flat.append(jnp.zeros((1, spare), F32))
    flat = jnp.concatenate(flat, axis=1)
    for n in range(pred_ref.shape[0]):
        pred_ref[n] = flat


FIELD, FIELD_SIDE, BOTH, BOTH_SIDE, SHARE, FLUID, SIDE, BASE, BLOCK = 0, 3, 6, 9, 12, 18, 19, 24, 25
RING, LAST, LOW, LOW_BOTH, HIGH, HIGH_BOTH, ENDS = 0, 5, 12, 15, 18, 21, 24


def prepare_kernel(
    steps_ref, v_ref, m_ref, s_ref, ice_ref, west_ref, east_ref, west2_ref, east2_ref, low_ref,
    high_ref, corner_low_ref, corner_high_ref, blocks_ref,
    fluid_ref, field_ref, fluid_side_ref, field_side_ref, north_ref, south_ref, out_ref, sems,
    *, rad_n,
):
    nr, nl, width = v_ref.shape
    shape = Shape(nr, width, rad_n)
    half = shape.half
    lower, lon, western = shape.lower, shape.lon, shape.western

    def share(f, other):
        return other * reciprocal(f + other)

    def safe_share(f, other):
        return other * reciprocal(jnp.maximum(f + other, 1e-30))

    def north_of(f):
        return jnp.where(shape.not_last, lat_next(f), 0.0)

    def south_of(f):
        return jnp.where(shape.not_first, lat_prev(f), 0.0)

    def two(ref, n, i):
        return ref[n * nr + i], ref[n * nr + i + half]

    def corner(ref, n):
        return jnp.where(western, ref[2 * n], ref[2 * n + 1])

    def pack_row(i):
        f = jnp.exp(-pack(v_ref[i], v_ref[i + half]))
        f_side = jnp.exp(-shape.sides(two(west_ref, 0, i), two(east_ref, 0, i)))
        fluid_ref[i + 1] = f
        fluid_side_ref[i + 1] = f_side
        north_ref[0, i], south_ref[0, i] = north_of(f), south_of(f)
        north_ref[1, i], south_ref[1, i] = north_of(f_side), south_of(f_side)
        for c in range(3):
            x = pack(s_ref[c, i], s_ref[c, i + half])
            x_side = shape.sides(two(west_ref, 1 + c, i), two(east_ref, 1 + c, i))
            field_ref[c, i + 1] = x
            field_side_ref[c, i + 1] = x_side
            north_ref[2 + c, i], south_ref[2 + c, i] = lat_next(x), lat_prev(x)
            north_ref[5 + c, i], south_ref[5 + c, i] = lat_next(x_side), lat_prev(x_side)

    lead = min(2, half - 1)
    for i in [half - 1] + list(range(lead)):
        pack_row(i)
    ring = pack(shape.has_low * jnp.exp(-low_ref[0]), shape.has_high * jnp.exp(-high_ref[0]))
    ring_side = jnp.where(
        lower,
        shape.has_low * jnp.exp(-corner(corner_low_ref, 0)),
        shape.has_high * jnp.exp(-corner(corner_high_ref, 0)),
    )
    ring_field = [pack(low_ref[1 + c], high_ref[1 + c]) for c in range(3)]
    ring_field_side = [
        jnp.where(lower, corner(corner_low_ref, 1 + c), corner(corner_high_ref, 1 + c))
        for c in range(3)
    ]

    def close(ref, ring):
        ref[0] = jnp.where(lower, ring, swap_halves(ref[half]))
        ref[half + 1] = jnp.where(lower, swap_halves(ref[1]), ring)

    close(fluid_ref, ring)
    close(fluid_side_ref, ring_side)
    for c in range(3):
        close(field_ref.at[c], ring_field[c])
        close(field_side_ref.at[c], ring_field_side[c])

    def coefficients(f, shares, here, above, below):
        scaled = (2.0 * RELAX_RATE) * f
        weighted = scaled * here
        radial = scaled * (shares[4] * (above - here) + shares[5] * (below - here))
        return [weighted * shares[n] for n in range(4)] + [radial]

    def relaxed(f, shares, s, others):
        total = shares[0] * (others[0] - s)
        for n in range(1, 6):
            total = total + shares[n] * (others[n] - s)
        return s + (2.0 * RELAX_RATE) * (f * total)

    load = ice_ref[steps_ref[0]]
    load = (1.0 - shape.has_high) * pack(jnp.zeros_like(load), load)
    load_side = jnp.where(
        western, west_ref[4 * nr + steps_ref[0]], east_ref[4 * nr + steps_ref[0]]
    )
    load_side = (1.0 - shape.has_high) * jnp.where(lower, 0.0, load_side)

    copies = []
    both_ends = {}

    def send(i):
        copies.append(pltpu.make_async_copy(out_ref.at[i], blocks_ref.at[i], sems.at[i]))
        copies[-1].start()

    for i in range(half):
        if i + lead < half - 1:
            pack_row(i + lead)
        f, f_side = fluid_ref[i + 1], fluid_side_ref[i + 1]
        shares = [
            share(f, jnp.where(lon == 3, f_side, lon_next(f))),
            share(f, jnp.where(lon == 0, f_side, lon_prev(f))),
            share(f, north_ref[0, i]),
            share(f, south_ref[0, i]),
            share(f, fluid_ref[i + 2]),
            share(f, fluid_ref[i]),
        ]
        for n in range(6):
            out_ref[i, SHARE + n] = shares[n]
        out_ref[i, FLUID] = f
        if i == half - 1:
            for n in range(6):
                out_ref[half, LAST + n] = shares[n]
            out_ref[half, LAST + 6] = f
        out_ref[i, BASE] = pack(
            m_ref[i] - (0.5 * PRIOR_WEIGHT) * v_ref[i],
            m_ref[i + half] - (0.5 * PRIOR_WEIGHT) * v_ref[i + half],
        )
        f_far = jnp.exp(-shape.sides(two(west2_ref, 0, i), two(east2_ref, 0, i)))
        side_shares = [
            share(f_side, jnp.where(western, f, f_far)),
            share(f_side, jnp.where(western, f_far, f)),
            share(f_side, north_ref[1, i]),
            share(f_side, south_ref[1, i]),
            share(f_side, fluid_side_ref[i + 2]),
            share(f_side, fluid_side_ref[i]),
        ]
        side = coefficients(
            f_side, side_shares, shape.step(i), shape.step(i + 1), shape.step(i - 1)
        )
        for n in range(5):
            out_ref[i, SIDE + n] = side[n]
        for c in range(3):
            s, s_side = field_ref[c, i + 1], field_side_ref[c, i + 1]
            s_far = shape.sides(two(west2_ref, 1 + c, i), two(east2_ref, 1 + c, i))
            others = [
                jnp.where(lon == 3, s_side, lon_next(s)),
                jnp.where(lon == 0, s_side, lon_prev(s)),
                north_ref[2 + c, i],
                south_ref[2 + c, i],
                field_ref[c, i + 2],
                field_ref[c, i],
            ]
            both = s + relaxed(f, shares, s, others)
            others = [
                jnp.where(western, s, s_far),
                jnp.where(western, s_far, s),
                north_ref[5 + c, i],
                south_ref[5 + c, i],
                field_side_ref[c, i + 2],
                field_side_ref[c, i],
            ]
            both_side = s_side + relaxed(f_side, side_shares, s_side, others)
            if c == 0 and i == half - 1:
                both = both - load
                both_side = both_side - load_side
            out_ref[i, FIELD + c] = s
            out_ref[i, FIELD_SIDE + c] = s_side
            out_ref[i, BOTH + c] = both
            out_ref[i, BOTH_SIDE + c] = both_side
            if i in (0, half - 1):
                both_ends[c, i] = both
        send(i)
    outer = pack(shape.has_low * jnp.exp(-low_ref[4]), shape.has_high * jnp.exp(-high_ref[4]))
    inner = jnp.where(lower, fluid_ref[1], fluid_ref[half])
    ring_shares = [
        safe_share(ring, jnp.where(lon == 3, ring_side, lon_next(ring))),
        safe_share(ring, jnp.where(lon == 0, ring_side, lon_prev(ring))),
        safe_share(ring, north_of(ring)),
        safe_share(ring, south_of(ring)),
        safe_share(ring, outer),
        safe_share(ring, inner),
    ]
    ring_coefficients = coefficients(
        ring,
        ring_shares,
        jnp.where(lower, shape.step(-1), shape.step(half)),
        jnp.where(lower, shape.step(-2), shape.step(half + 1)),
        jnp.where(lower, shape.step(0), shape.step(half - 1)),
    )
    for n in range(5):
        out_ref[half, RING + n] = ring_coefficients[n]
    ring_both = []
    for c in range(3):
        s, s_side = ring_field[c], ring_field_side[c]
        others = [
            jnp.where(lon == 3, s_side, lon_next(s)),
            jnp.where(lon == 0, s_side, lon_prev(s)),
            lat_next(s),
            lat_prev(s),
            pack(low_ref[5 + c], high_ref[5 + c]),
            jnp.where(lower, field_ref[c, 1], field_ref[c, half]),
        ]
        ring_both.append(s + relaxed(ring, ring_shares, s, others))
    low_step = shape.step(0) - shape.step(-1)
    high_step = shape.step(half) - shape.step(half - 1)
    for c in range(3):
        first, last = both_ends[c, 0], both_ends[c, half - 1]
        out_ref[half, LOW + c] = field_ref[c, 1] - field_ref[c, 0]
        out_ref[half, LOW_BOTH + c] = low_step * (
            first - jnp.where(lower, ring_both[c], swap_halves(last))
        )
        out_ref[half, HIGH + c] = field_ref[c, half + 1] - field_ref[c, half]
        out_ref[half, HIGH_BOTH + c] = high_step * (
            jnp.where(lower, swap_halves(first), ring_both[c]) - last
        )
    out_ref[half, ENDS:BLOCK] = jnp.zeros((BLOCK - ENDS, 8, width), F32)
    send(half)
    for copy in copies:
        copy.wait()


AHEAD = 8


def gradient_kernel(
    v_ref, pred_ref, data_ref, k_high_ref, k_low_ref, blocks_ref,
    new_ref, half_ref, misfit_ref, v_in_ref, new_out_ref, half_out_ref, sa_ref, d_ref, in_ref, e_ref, side_ref, north_ref, product_ref,
    total_ref, k_low_in_ref, sems, out_sems, *, scale, rad_n,
):
    nr, nl, width = v_ref.shape
    shape = Shape(nr, width, rad_n)
    half = shape.half
    sites = k_high_ref.shape[1]
    lon, lower = shape.lon, shape.lower
    copies = [
        pltpu.make_async_copy(blocks_ref.at[i], in_ref.at[i], sems.at[i]) for i in range(half + 1)
    ]
    low_copy = pltpu.make_async_copy(k_low_ref, k_low_in_ref, sems.at[half + 1])
    low_copy.start()
    copies[half].start()
    for i in range(min(AHEAD, half)):
        copies[i].start()
    v_copy = pltpu.make_async_copy(v_ref, v_in_ref, sems.at[half + 2])
    v_copy.start()
    groups = []
    for first in range(0, half, 6):
        group = []
        for at in (first, first + half):
            for inner, outer in ((half_out_ref, half_ref), (new_out_ref, new_ref)):
                rows = slice(at, at + min(6, half - first))
                sem = out_sems.at[4 * len(groups) + len(group)]
                group.append(pltpu.make_async_copy(inner.at[rows], outer.at[rows], sem))
        groups.append(group)
    ends_ref = in_ref.at[half]

    flat = pred_ref[0]
    for n in range(1, pred_ref.shape[0]):
        flat = flat + pred_ref[n]
    predicted = jnp.concatenate(
        [flat[:, c * sites : (c + 1) * sites] for c in range(3)], axis=0
    )
    weight = data_ref[4:7, :]
    weighted = weight * (predicted * scale - data_ref[1:4, :])
    squares = jnp.sum(weighted * weighted, axis=1, keepdims=True)
    misfit_ref[...] = jnp.sum(squares, axis=0, keepdims=True) * (1.0 / (3 * sites))
    pulled = (weight * weighted) * scale
    pulled = jnp.concatenate([pulled, jnp.zeros((5, sites), F32)], axis=0)
    for col in range(COLS):
        if col == 0:
            low_copy.wait()
        spread = product(pulled, k_high_ref[col], k_low_in_ref[col], 0)
        for c in range(3):
            sa_ref[c, col : col + 1, :] = spread[c : c + 1, :]

    for c in range(3):
        x = sa_ref[c]

        def window(start):
            return shape.first_weight * jnp.where(
                lower,
                x if start == 0 else pltpu.roll(x, 8 - start, 0),
                x if start == 4 else pltpu.roll(x, (4 - start) % 8, 0),
            )

        own = window(2)
        east = window(3)
        west = window(1)
        outside = jnp.where(lon < 2, west, east)
        d_ref[0, c] = east - own
        d_ref[1, c] = west - own
        d_ref[2, c] = lat_next(own) - own
        d_ref[3, c] = lat_prev(own) - own
        d_ref[4, c] = own
        d_ref[5, c] = jnp.where(lon < 2, own, window(4)) - outside
        d_ref[6, c] = jnp.where(lon < 2, window(0), own) - outside
        d_ref[7, c] = lat_next(outside) - outside
        d_ref[8, c] = lat_prev(outside) - outside
        d_ref[9, c] = outside

    def change(coeffs, first):
        out = []
        for c in range(3):
            total = coeffs[0] * d_ref[first, c]
            for n in range(1, 5):
                total = total + coeffs[n] * d_ref[first + n, c]
            out.append(total)
        return out

    above, below = shape.step(1) - 1.0, shape.step(-1) - 1.0

    def own_change(ref, at, fluid, i):
        shares = [ref[at + n] for n in range(6)]
        scaled = (2.0 * RELAX_RATE * shape.step(i)) * fluid
        coeffs = shares[:4] + [above * shares[4] + below * shares[5]]
        return [scaled * x for x in change(coeffs, 0)]

    def first_pass(i):
        if i % 2 == 0:

            @pl.when(lax.axis_index("rad") >= 0)
            def _():
                for n in range(i, min(i + 2, half)):
                    copies[n].wait()
                    if n + AHEAD < half:
                        copies[n + AHEAD].start()

        e = own_change(in_ref.at[i], SHARE, in_ref[i, FLUID], i)
        side = change([in_ref[i, SIDE + n] for n in range(5)], 5)
        for c in range(3):
            e_ref[c, i] = e[c]
            side_ref[c, i] = side[c]
            north_ref[c, i] = lat_next(in_ref[i, FIELD + c])
            north_ref[3 + c, i] = lat_next(in_ref[i, BOTH + c])
            north_ref[6 + c, i] = lat_next(e[c])

    def second_pass(i, p_down):
        here, step = shape.step(i), shape.step(i + 1) - shape.step(i)
        weighted = [0.0] * 4
        plain = [0.0] * 4
        for c in range(3):
            s, s_side = in_ref[i, FIELD + c], in_ref[i, FIELD_SIDE + c]
            both, both_side = in_ref[i, BOTH + c], in_ref[i, BOTH_SIDE + c]
            e, e_side = e_ref[c, i], side_ref[c, i]

            def differences(x, x_side, x_north):
                return [jnp.where(lon == 3, x_side, lon_next(x)) - x, x_side - x, x_north - x]

            d_field = differences(s, s_side, north_ref[c, i])
            d_both = differences(both, both_side, north_ref[3 + c, i])
            d_e = differences(e, e_side, north_ref[6 + c, i])
            if i < half - 1:
                d_field.append(in_ref[i + 1, FIELD + c] - s)
                d_both.append(step * (in_ref[i + 1, BOTH + c] - both))
                d_e.append(e_ref[c, i + 1] - e)
            else:
                d_field.append(ends_ref[HIGH + c])
                d_both.append(ends_ref[HIGH_BOTH + c])
                d_e.append(jnp.where(lower, swap_halves(e_ref[c, 0]), ring[c]) - e)
            slopes = [d_ref[0, c], d_ref[1, c], d_ref[2, c], d_ref[4, c]]
            for n in range(4):
                weighted[n] = weighted[n] + d_both[n] * slopes[n]
                plain[n] = plain[n] + d_field[n] * d_e[n]
        p_east, p_cut, p_north = [here * weighted[n] + plain[n] for n in range(3)]
        p_up = weighted[3] + plain[3]
        p_west = jnp.where(lon == 0, p_cut, lon_prev(p_east))
        product_ref[i] = lat_prev(p_north)
        total = None
        for n, x in ((0, p_east), (1, p_west), (2, p_north), (4, p_up), (5, p_down)):
            share = in_ref[i, SHARE + n]
            term = (share * share) * x
            total = term if total is None else total + term
        total_ref[i] = total
        return p_up

    def third_pass(i):
        share = in_ref[i, SHARE + 3]
        total = total_ref[i] + (share * share) * product_ref[i]
        total = in_ref[i, BASE] - RELAX_RATE * (in_ref[i, FLUID] * total)
        half_out_ref[i] = total[0:4, :]
        half_out_ref[i + half] = total[4:8, :]
        new_out_ref[i] = v_in_ref[i] + total[0:4, :]
        new_out_ref[i + half] = v_in_ref[i + half] + total[4:8, :]

    copies[half].wait()
    ring = change([ends_ref[RING + n] for n in range(5)], 0)
    e_last = own_change(ends_ref, LAST, ends_ref[LAST + 6], half - 1)
    lead = min(2, half)
    for i in range(lead):
        first_pass(i)
    p_down = None
    for c in range(3):
        e_low = jnp.where(lower, ring[c], swap_halves(e_last[c]))
        term = ends_ref[LOW_BOTH + c] * d_ref[4, c] + ends_ref[LOW + c] * (e_ref[c, 0] - e_low)
        p_down = term if p_down is None else p_down + term
    for i in range(half):
        if i + lead < half:
            first_pass(i + lead)
        p_down = second_pass(i, p_down)
        if i == 1:
            v_copy.wait()
        if i > 0:
            third_pass(i - 1)
        if i % 6 == 0 and i > 0:

            @pl.when(lax.axis_index("rad") >= 0)
            def _():
                for copy in groups[i // 6 - 1]:
                    copy.start()

    if half == 1:
        v_copy.wait()
    third_pass(half - 1)
    for copy in groups[-1]:
        copy.start()
    for group in groups:
        for copy in group:
            copy.wait()


def call(
    kernel, outs, ins, scratch=(), flops=1, name=None, held_in=(), held_out=(), far_in=(),
    far_out=(), near_out=(),
):
    spaces = {"s": pltpu.SMEM, "v": pltpu.VMEM, "h": pltpu.HBM}
    made = pl.pallas_call(
        kernel,
        out_shape=[
            pltpu.VMEM(shape, dtype)
            if n in held_out
            else pltpu.HBM(shape, dtype)
            if n in far_out or n in near_out
            else jax.ShapeDtypeStruct(shape, dtype)
            for n, (shape, dtype) in enumerate(outs)
        ],
        in_specs=[pl.BlockSpec(memory_space=spaces[k]) for k in ins],
        out_specs=[
            pl.BlockSpec(memory_space=pltpu.HBM if n in far_out else pltpu.VMEM)
            for n in range(len(outs))
        ],
        scratch_shapes=list(scratch),
        compiler_params=pltpu.CompilerParams(vmem_limit_bytes=VMEM_LIMIT),
        cost_estimate=pl.CostEstimate(flops=flops, bytes_accessed=1 << 20, transcendentals=0),
        name=name,
    )

    def run(*args):
        return made(
            *[
                pltpu.with_memory_space_constraint(a, pltpu.VMEM if n in held_in else pltpu.HBM)
                if n in held_in or n in far_in
                else a
                for n, a in enumerate(args)
            ]
        )

    return run


def body(
    logvisc, momentum, displacement, ice_history, load_steps, site_cells, observed, site_weight
):
    nr, nl, nlat = logvisc.shape
    own_sites = site_cells.shape[0]
    lon_n = lax.axis_size("lon")
    rad_n = lax.axis_size("rad")
    total_lon = nl * lon_n
    sites = own_sites * lon_n
    devices = lon_n * rad_n
    half = nr // 2
    scale = 1.0 / math.sqrt(total_lon * nlat)
    row = (8, nlat)

    def across_rad(down, up):
        if rad_n == 2:
            both = lax.ppermute(down, "rad", [(0, 1), (1, 0)])
            return both, both
        upward = [(i, i + 1) for i in range(rad_n - 1)]
        downward = [(t, s) for s, t in upward]
        return lax.ppermute(up, "rad", upward), lax.ppermute(down, "rad", downward)

    eastward = [(i, (i + 1) % lon_n) for i in range(lon_n)]
    westward = [(t, s) for s, t in eastward]
    column, layers = (4 * nr, 1, nlat), (8, nl, nlat)
    first_column = (4 * nr + ice_history.shape[0], 1, nlat)
    to_west, to_east, to_west2, to_east2, to_low, to_high, packets = call(
        functools.partial(message_kernel, rad_n=rad_n),
        [
            (shape, F32)
            for shape in [first_column] * 2 + [column] * 2 + [layers] * 2 + [(lon_n, 1, 7 * own_sites)]
        ],
        "vvvvvv",
        name="messages",
        flops=2875000000,
        far_in=(0, 1, 2, 3, 4, 5),
    )(logvisc, displacement, ice_history, site_cells[None], observed, site_weight)
    gathered = lax.all_to_all(packets, "lon", 0, 0)
    west = lax.ppermute(to_east, "lon", eastward)
    east = lax.ppermute(to_west, "lon", westward)
    low, high = across_rad(to_low, to_high)
    west2 = lax.ppermute(to_east2, "lon", eastward)
    east2 = lax.ppermute(to_west2, "lon", westward)

    k_high, k_low, data = call(
        functools.partial(weights_kernel, total_lon=total_lon),
        [((COLS, sites, nlat), BF16)] * 2 + [((8, sites), F32)],
        "v",
        scratch=[pltpu.VMEM((16, sites), F32)],
        name="site_weights",
        flops=3680000000,
        held_out=(0, 1, 2),
    )(gathered)

    padded = -(-3 * sites // 128) * 128
    partial, to_corner_low, to_corner_high = call(
        functools.partial(forward_kernel, rad_n=rad_n),
        [((devices, 1, padded), F32), ((8, 1, nlat), F32), ((8, 1, nlat), F32)],
        "s" + "v" * 9,
        scratch=[
            pltpu.VMEM(shape + row, F32)
            for shape in [(half,)] * 2 + [(3, half)] * 3 + [(half,)] * 3 + [(half + 1,), (half,)]
            + [(3, half)] * 2 + [(6,)]
        ],
        name="forward",
        flops=6325000000,
        held_in=(8, 9),
        far_in=(1, 2, 7),
        near_out=(0, 1, 2),
    )(load_steps, logvisc, displacement, west, east, low, high, ice_history, k_high, k_low)
    predicted = lax.all_to_all(partial, ("lon", "rad"), 0, 0)

    corner_low, corner_high = across_rad(to_corner_low, to_corner_high)
    (blocks,) = call(
        functools.partial(prepare_kernel, rad_n=rad_n),
        [((half + 1, BLOCK) + row, F32)],
        "s" + "v" * 12,
        scratch=[
            pltpu.VMEM(shape + row, F32)
            for shape in [(half + 2,), (3, half + 2)] * 2 + [(8, half)] * 2 + [(half + 1, BLOCK)]
        ]
        + [pltpu.SemaphoreType.DMA((half + 1,))],
        name="prepare",
        flops=8050000000,
        far_in=(1, 2, 3, 4),
        far_out=(0,),
    )(
        load_steps, logvisc, momentum, displacement, ice_history, west, east, west2, east2, low,
        high, corner_low, corner_high,
    )

    new_logvisc, half_momentum, misfit = call(
        functools.partial(gradient_kernel, scale=scale, rad_n=rad_n),
        [((nr, nl, nlat), F32), ((nr, nl, nlat), F32), ((1, 1), F32)],
        "hvvvhh",
        scratch=[pltpu.VMEM((nr, nl, nlat), F32)] * 3
        + [
            pltpu.VMEM(shape + row, F32)
            for shape in [(3,), (10, 3), (half + 1, BLOCK), (3, half), (3, half), (9, half)]
            + [(half,)] * 2
        ]
        + [
            pltpu.VMEM((COLS, sites, nlat), BF16),
            pltpu.SemaphoreType.DMA((half + 3,)),
            pltpu.SemaphoreType.DMA((4 * -(-half // 6),)),
        ],
        name="gradient",
        flops=6900000000,
        held_in=(2, 3),
        far_in=(0, 4, 5),
        far_out=(0, 1),
    )(logvisc, predicted, data, k_high, k_low, blocks)
    return (new_logvisc, half_momentum, misfit.reshape(1))


def solution(mesh):
    return jax.shard_map(
        body,
        mesh=mesh,
        in_specs=(
            P("rad", "lon", None),
            P("rad", "lon", None),
            P(None, "rad", "lon", None),
            P(None, "lon", None),
            P(),
            P("lon"),
            P(None, "lon"),
            P(None, "lon"),
        ),
        out_specs=(P("rad", "lon", None), P("rad", "lon", None), P()),
        check_vma=False,
    )
```

```python
import functools
import math

import jax
import jax.numpy as jnp
from jax import lax
from jax.experimental import pallas as pl
from jax.experimental.pallas import tpu as pltpu
from jax.sharding import PartitionSpec as P

RELAX_RATE = 0.05
KERNEL_WIDTH = 0.1
KERNEL_WAVE = 40.0
PRIOR_WEIGHT = 0.1
COLS = 8
F32 = jnp.float32
BF16 = jnp.bfloat16
VMEM_LIMIT = 40 * 1024 * 1024


def reciprocal(x):
    r = pl.reciprocal(x, approx=True)
    return r * (2.0 - x * r)


def lat_next(x):
    return pltpu.roll(x, x.shape[1] - 1, 1)


def lat_prev(x):
    return pltpu.roll(x, 1, 1)


def lon_next(x):
    return pltpu.roll(x, 7, 0)


def lon_prev(x):
    return pltpu.roll(x, 1, 0)


def swap_halves(x):
    return pltpu.roll(x, 4, 0)


def pack(low, high):
    return jnp.concatenate([low, high], axis=0)


class Shape:
    def __init__(self, nr, width, rad_n):
        self.nr, self.width, self.half = nr, width, nr // 2
        sub = lax.broadcasted_iota(jnp.int32, (8, width), 0)
        lane = lax.broadcasted_iota(jnp.int32, (8, width), 1)
        self.lon = sub % 4
        self.lower = sub < 4
        self.upper = sub >= 4
        self.western = self.lon < 2
        self.not_last = lane < width - 1
        self.not_first = lane > 0
        self.rate = 4.0 / (nr * rad_n)
        at = lax.axis_index("rad")
        self.has_low = (at > 0).astype(F32)
        self.has_high = (at < rad_n - 1).astype(F32)
        layer = jnp.where(self.lower, 0, self.half) + (at * nr - (nr * rad_n - 1))
        self.first_weight = jnp.exp(layer.astype(F32) * self.rate)

    def step(self, i):
        return math.exp(self.rate * i)

    def sides(self, west, east):
        return jnp.where(
            self.lower,
            jnp.where(self.western, west[0], east[0]),
            jnp.where(self.western, west[1], east[1]),
        )


def face(a, b):
    return 2.0 * a * b * reciprocal(a + b)


def sin_pi(u):
    z = u * u
    p = 0.0772201269865036
    p = p * z - 0.5980451703071594
    p = p * z + 2.5500314235687256
    p = p * z - 5.1677069664001465
    p = p * z + 3.141592502593994
    return p * u


TURNS = KERNEL_WAVE / (2.0 * math.pi)


def site_kernel(turns):
    s = sin_pi(turns - jnp.round(turns))
    return (reciprocal(1.0 + turns * (1.0 / (KERNEL_WIDTH * TURNS))) + 0.5) - s * s


def message_kernel(
    v_ref, s_ref, ice_ref, cells_ref, obs_ref, wt_ref,
    west_ref, east_ref, west2_ref, east2_ref, low_ref, high_ref, packet_ref, *, rad_n,
):
    nr, nl, width = v_ref.shape
    parts = [cells_ref[...].astype(F32)]
    parts += [ref[c : c + 1, :] for ref in (obs_ref, wt_ref) for c in range(3)]
    packet = jnp.concatenate(parts, axis=1)
    for n in range(packet_ref.shape[0]):
        packet_ref[n] = packet

    def field(n, r):
        return v_ref[r] if n == 0 else s_ref[n - 1, r]

    for r in range(nr):
        for n in range(4):
            x = field(n, r)
            west_ref[n * nr + r] = x[0:1, :]
            east_ref[n * nr + r] = x[nl - 1 : nl, :]
            west2_ref[n * nr + r] = x[1:2, :]
            east2_ref[n * nr + r] = x[nl - 2 : nl - 1, :]
    for n in range(ice_ref.shape[0]):
        west_ref[4 * nr + n] = ice_ref[n, 0:1, :]
        east_ref[4 * nr + n] = ice_ref[n, nl - 1 : nl, :]
    bottom = lax.axis_index("rad") == 0
    for n in range(4):
        for k in range(2):
            down, up = field(n, k), field(n, nr - 1 - k)
            if rad_n == 2:
                low_ref[n + 4 * k] = jnp.where(bottom, up, down)
            else:
                low_ref[n + 4 * k] = down
                high_ref[n + 4 * k] = up
    if rad_n == 2:
        high_ref[...] = jnp.zeros_like(high_ref)


def weights_kernel(gathered_ref, high_ref, low_ref, data_ref, rows_ref, *, total_lon):
    devices, _, own = gathered_ref.shape
    own = own // 7
    sites = high_ref.shape[1]
    width = high_ref.shape[2]
    for d in range(devices):
        packet = gathered_ref[d]
        for k in range(7):
            data_ref[k : k + 1, d * own : (d + 1) * own] = packet[:, k * own : (k + 1) * own]
    data_ref[7:8, :] = jnp.zeros((1, sites), F32)
    cells = data_ref[0:1, :]
    lon = jnp.floor((cells + 0.5) * (1.0 / width))
    theta = (cells - lon * width + 0.5) * (1.0 / width)
    phi = lon * (1.0 / total_lon)

    def sin_whole(t):
        return sin_pi(jnp.minimum(t, 1.0 - t))

    def circle(t):
        u = t - jnp.round(t)
        s = sin_pi(u)
        y = jnp.abs(2.0 * u)
        wave = sin_pi(jnp.minimum(y, 1.0 - y))
        return 1.0 - 2.0 * s * s, jnp.where(u < 0, -wave, wave)

    site_cos, site_sin = circle(phi)
    first = lax.axis_index("lon") * 4 - 2 + total_lon
    col = (lax.broadcasted_iota(jnp.int32, (COLS, sites), 0) + first).astype(F32)
    turns = col * (1.0 / total_lon)
    col_cos, col_sin = circle(turns - jnp.floor(turns))
    rows_ref[0:8, :] = col_cos * site_cos + col_sin * site_sin
    rows_ref[8:9, :] = (-2.0 * TURNS) * sin_pi(0.5 - theta)
    rows_ref[9:10, :] = (-2.0 * TURNS) * sin_whole(theta)
    rows_ref[10:16, :] = jnp.zeros((6, sites), F32)
    columns = jnp.transpose(rows_ref[...])
    lat = (lax.broadcasted_iota(jnp.int32, (16, width), 1).astype(F32) + 0.5) * (1.0 / width)
    cos_lat = sin_pi(0.5 - lat)
    sin_lat = sin_whole(lat)
    for at in range(0, sites, 16):
        part = columns[at : at + 16, :]
        a = 2.0 * TURNS + part[:, 8:9] * cos_lat
        b = part[:, 9:10] * sin_lat
        for n in range(COLS):
            k = site_kernel(a + b * part[:, n : n + 1])
            high = k.astype(BF16)
            high_ref[n, at : at + 16, :] = high
            low_ref[n, at : at + 16, :] = (k - high.astype(F32)).astype(BF16)


def two_parts(x):
    high = x.astype(BF16).astype(F32)
    return jnp.concatenate([high, x - high], axis=0).astype(BF16)


def product(x, high, low, contract):
    dims = (((1,), (contract,)), ((), ()))
    parts = two_parts(x)
    both = lax.dot_general(parts, high, dims, preferred_element_type=F32)
    rest = lax.dot_general(parts, low, dims, preferred_element_type=F32)
    return both[0:8, :] + (both[8:16, :] + rest[0:8, :])


def forward_kernel(
    steps_ref, v_ref, s_ref, west_ref, east_ref, low_ref, high_ref, ice_ref, k_high_ref, k_low_ref,
    pred_ref, corner_low_ref, corner_high_ref,
    fluid_ref, fluid_north_ref, field_ref, north_ref, south_ref, h_east_ref, h_north_ref,
    h_south_ref, h_up_ref, h_cut_ref, next_ref, next_north_ref, surf_ref, *, rad_n,
):
    nr, nl, width = v_ref.shape
    shape = Shape(nr, width, rad_n)
    half = shape.half
    lower, lon = shape.lower, shape.lon
    ends = (lon == 0) | (lon == 3)

    bottom = lax.axis_index("rad") == 0
    for n in range(4):
        for k, ref in enumerate((west_ref, east_ref)):
            down, up = ref[n * nr], ref[n * nr + nr - 1]
            if rad_n == 2:
                corner_low_ref[2 * n + k] = jnp.where(bottom, up, down)
            else:
                corner_low_ref[2 * n + k] = down
                corner_high_ref[2 * n + k] = up
    if rad_n == 2:
        corner_high_ref[...] = jnp.zeros_like(corner_high_ref)

    for i in range(half):
        f = jnp.exp(-pack(v_ref[i], v_ref[i + half]))
        fluid_ref[i] = f
        fluid_north_ref[i] = lat_next(f)
        for c in range(3):
            x = pack(s_ref[c, i], s_ref[c, i + half])
            field_ref[c, i] = x
            north_ref[c, i] = lat_next(x)
            south_ref[c, i] = lat_prev(x)
    for i in range(half):
        h_north = jnp.where(shape.not_last, face(fluid_ref[i], fluid_north_ref[i]), 0.0)
        h_north_ref[i] = h_north
        h_south_ref[i] = lat_prev(h_north)

    ring = pack(shape.has_low * jnp.exp(-low_ref[0]), shape.has_high * jnp.exp(-high_ref[0]))
    h_ring = face(ring, jnp.where(lower, fluid_ref[0], fluid_ref[half - 1]))
    seam = face(swap_halves(fluid_ref[0]), fluid_ref[half - 1])
    h_up_ref[half] = jnp.where(lower, seam, 0.0)
    h_up_ref[0] = swap_halves(h_up_ref[half])
    load = ice_ref[steps_ref[0]] * (1.0 - shape.has_high)
    load = pack(jnp.zeros_like(load), load)
    carry = [h_up_ref[0] * (field_ref[c, 0] - swap_halves(field_ref[c, half - 1])) for c in range(3)]
    for i in range(half):

        def side(n):
            return shape.sides(
                (west_ref[n * nr + i], west_ref[n * nr + i + half]),
                (east_ref[n * nr + i], east_ref[n * nr + i + half]),
            )

        f = fluid_ref[i]
        h_cut = jnp.where(ends, face(f, jnp.exp(-side(0))), 0.0)
        h_cut_ref[i] = h_cut
        h_east = jnp.where(lon < 3, face(f, lon_next(f)), 0.0)
        h_east_ref[i] = h_east
        if i < half - 1:
            h_up_ref[i + 1] = face(f, fluid_ref[i + 1])
        h_north, h_south, h_up = h_north_ref[i], h_south_ref[i], h_up_ref[i + 1]
        for c in range(3):
            x = field_ref[c, i]
            above = field_ref[c, i + 1] if i < half - 1 else swap_halves(field_ref[c, 0])
            east = h_east * (lon_next(x) - x)
            up = h_up * (above - x)
            total = (east - lon_prev(east)) + (up - carry[c]) + h_cut * (side(1 + c) - x)
            total = total + h_north * (north_ref[c, i] - x) + h_south * (south_ref[c, i] - x)
            if i in (0, half - 1):
                beyond = h_ring * (pack(low_ref[1 + c], high_ref[1 + c]) - x)
                if i == 0:
                    total = total + jnp.where(lower, beyond, 0.0)
                if i == half - 1:
                    total = total + jnp.where(lower, 0.0, beyond)
            s1 = x + RELAX_RATE * total
            if c == 0 and i == half - 1:
                s1 = s1 - load
            next_ref[c, i] = s1
            next_north_ref[c, i] = lat_next(s1)
            carry[c] = up

    zero = jnp.zeros((8, width), F32)
    column, east, north, cut = [zero] * 3, [zero] * 3, [zero] * 3, [zero] * 3
    below = [swap_halves(next_ref[c, half - 1]) for c in range(3)]
    for i in range(half):
        weight = shape.step(i)
        g_east = weight * h_east_ref[i]
        g_north = weight * h_north_ref[i]
        g_cut = weight * h_cut_ref[i]
        g_low = (RELAX_RATE * (weight - shape.step(i - 1))) * h_up_ref[i]
        for c in range(3):
            x = next_ref[c, i]
            column[c] = column[c] + (weight * x - g_low * (x - below[c]))
            east[c] = east[c] + g_east * (lon_next(x) - x)
            north[c] = north[c] + g_north * (next_north_ref[c, i] - x)
            cut[c] = cut[c] + g_cut * x
            below[c] = x
    top = shape.step(half - 1)
    g_ring = (RELAX_RATE * h_ring) * jnp.where(
        lower, shape.step(-1) - 1.0, shape.step(half) - top
    )
    for c in range(3):
        inner = jnp.where(lower, next_ref[c, 0], next_ref[c, half - 1])

        def folded(x):
            x = shape.first_weight * x
            return x + swap_halves(x)

        sum_east = folded(east[c])
        sum_north = folded(north[c])
        sum_cut = folded(cut[c])
        own = folded(column[c] + g_ring * inner)
        spread = (sum_east - lon_prev(sum_east)) + (sum_north - lat_prev(sum_north)) - sum_cut
        own = own + RELAX_RATE * spread
        if c == 0:
            second = ice_ref[steps_ref[1]] * (1.0 - shape.has_high)
            own = own - pack(second, second)
        surf_ref[0, c : c + 1, :] = RELAX_RATE * sum_cut[0:1, :]
        for col in range(4):
            surf_ref[col + 1, c : c + 1, :] = own[col : col + 1, :]
        surf_ref[5, c : c + 1, :] = RELAX_RATE * sum_cut[3:4, :]
    total = None
    for col in range(6):
        surf_ref[col, 3:8, :] = jnp.zeros((5, width), F32)
        term = product(surf_ref[col], k_high_ref[col + 1], k_low_ref[col + 1], 1)
        total = term if total is None else total + term
    sites = total.shape[1]
    spare = pred_ref.shape[2] - 3 * sites
    flat = [total[c : c + 1, :] for c in range(3)]
    if spare > 0:
        flat.append(jnp.zeros((1, spare), F32))
    flat = jnp.concatenate(flat, axis=1)
    for n in range(pred_ref.shape[0]):
        pred_ref[n] = flat


FIELD, FIELD_SIDE, BOTH, BOTH_SIDE, SHARE, FLUID, SIDE, BASE, BLOCK = 0, 3, 6, 9, 12, 18, 19, 24, 25
RING, LAST, LOW, LOW_BOTH, HIGH, HIGH_BOTH, ENDS = 0, 5, 12, 15, 18, 21, 24


def prepare_kernel(
    steps_ref, v_ref, m_ref, s_ref, ice_ref, west_ref, east_ref, west2_ref, east2_ref, low_ref,
    high_ref, corner_low_ref, corner_high_ref, blocks_ref,
    fluid_ref, field_ref, fluid_side_ref, field_side_ref, north_ref, south_ref, out_ref, sems,
    *, rad_n,
):
    nr, nl, width = v_ref.shape
    shape = Shape(nr, width, rad_n)
    half = shape.half
    lower, lon, western = shape.lower, shape.lon, shape.western

    def share(f, other):
        return other * reciprocal(f + other)

    def safe_share(f, other):
        return other * reciprocal(jnp.maximum(f + other, 1e-30))

    def north_of(f):
        return jnp.where(shape.not_last, lat_next(f), 0.0)

    def south_of(f):
        return jnp.where(shape.not_first, lat_prev(f), 0.0)

    def two(ref, n, i):
        return ref[n * nr + i], ref[n * nr + i + half]

    def corner(ref, n):
        return jnp.where(western, ref[2 * n], ref[2 * n + 1])

    def pack_row(i):
        f = jnp.exp(-pack(v_ref[i], v_ref[i + half]))
        f_side = jnp.exp(-shape.sides(two(west_ref, 0, i), two(east_ref, 0, i)))
        fluid_ref[i + 1] = f
        fluid_side_ref[i + 1] = f_side
        north_ref[0, i], south_ref[0, i] = north_of(f), south_of(f)
        north_ref[1, i], south_ref[1, i] = north_of(f_side), south_of(f_side)
        for c in range(3):
            x = pack(s_ref[c, i], s_ref[c, i + half])
            x_side = shape.sides(two(west_ref, 1 + c, i), two(east_ref, 1 + c, i))
            field_ref[c, i + 1] = x
            field_side_ref[c, i + 1] = x_side
            north_ref[2 + c, i], south_ref[2 + c, i] = lat_next(x), lat_prev(x)
            north_ref[5 + c, i], south_ref[5 + c, i] = lat_next(x_side), lat_prev(x_side)

    lead = min(2, half - 1)
    for i in [half - 1] + list(range(lead)):
        pack_row(i)
    ring = pack(shape.has_low * jnp.exp(-low_ref[0]), shape.has_high * jnp.exp(-high_ref[0]))
    ring_side = jnp.where(
        lower,
        shape.has_low * jnp.exp(-corner(corner_low_ref, 0)),
        shape.has_high * jnp.exp(-corner(corner_high_ref, 0)),
    )
    ring_field = [pack(low_ref[1 + c], high_ref[1 + c]) for c in range(3)]
    ring_field_side = [
        jnp.where(lower, corner(corner_low_ref, 1 + c), corner(corner_high_ref, 1 + c))
        for c in range(3)
    ]

    def close(ref, ring):
        ref[0] = jnp.where(lower, ring, swap_halves(ref[half]))
        ref[half + 1] = jnp.where(lower, swap_halves(ref[1]), ring)

    close(fluid_ref, ring)
    close(fluid_side_ref, ring_side)
    for c in range(3):
        close(field_ref.at[c], ring_field[c])
        close(field_side_ref.at[c], ring_field_side[c])

    def coefficients(f, shares, here, above, below):
        scaled = (2.0 * RELAX_RATE) * f
        weighted = scaled * here
        radial = scaled * (shares[4] * (above - here) + shares[5] * (below - here))
        return [weighted * shares[n] for n in range(4)] + [radial]

    def relaxed(f, shares, s, others):
        total = shares[0] * (others[0] - s)
        for n in range(1, 6):
            total = total + shares[n] * (others[n] - s)
        return s + (2.0 * RELAX_RATE) * (f * total)

    load = ice_ref[steps_ref[0]]
    load = (1.0 - shape.has_high) * pack(jnp.zeros_like(load), load)
    load_side = jnp.where(
        western, west_ref[4 * nr + steps_ref[0]], east_ref[4 * nr + steps_ref[0]]
    )
    load_side = (1.0 - shape.has_high) * jnp.where(lower, 0.0, load_side)

    copies = []
    both_ends = {}

    def send(i):
        copies.append(pltpu.make_async_copy(out_ref.at[i], blocks_ref.at[i], sems.at[i]))
        copies[-1].start()

    for i in range(half):
        if i + lead < half - 1:
            pack_row(i + lead)
        f, f_side = fluid_ref[i + 1], fluid_side_ref[i + 1]
        shares = [
            share(f, jnp.where(lon == 3, f_side, lon_next(f))),
            share(f, jnp.where(lon == 0, f_side, lon_prev(f))),
            share(f, north_ref[0, i]),
            share(f, south_ref[0, i]),
            share(f, fluid_ref[i + 2]),
            share(f, fluid_ref[i]),
        ]
        for n in range(6):
            out_ref[i, SHARE + n] = shares[n]
        out_ref[i, FLUID] = f
        if i == half - 1:
            for n in range(6):
                out_ref[half, LAST + n] = shares[n]
            out_ref[half, LAST + 6] = f
        out_ref[i, BASE] = pack(
            m_ref[i] - (0.5 * PRIOR_WEIGHT) * v_ref[i],
            m_ref[i + half] - (0.5 * PRIOR_WEIGHT) * v_ref[i + half],
        )
        f_far = jnp.exp(-shape.sides(two(west2_ref, 0, i), two(east2_ref, 0, i)))
        side_shares = [
            share(f_side, jnp.where(western, f, f_far)),
            share(f_side, jnp.where(western, f_far, f)),
            share(f_side, north_ref[1, i]),
            share(f_side, south_ref[1, i]),
            share(f_side, fluid_side_ref[i + 2]),
            share(f_side, fluid_side_ref[i]),
        ]
        side = coefficients(
            f_side, side_shares, shape.step(i), shape.step(i + 1), shape.step(i - 1)
        )
        for n in range(5):
            out_ref[i, SIDE + n] = side[n]
        for c in range(3):
            s, s_side = field_ref[c, i + 1], field_side_ref[c, i + 1]
            s_far = shape.sides(two(west2_ref, 1 + c, i), two(east2_ref, 1 + c, i))
            others = [
                jnp.where(lon == 3, s_side, lon_next(s)),
                jnp.where(lon == 0, s_side, lon_prev(s)),
                north_ref[2 + c, i],
                south_ref[2 + c, i],
                field_ref[c, i + 2],
                field_ref[c, i],
            ]
            both = s + relaxed(f, shares, s, others)
            others = [
                jnp.where(western, s, s_far),
                jnp.where(western, s_far, s),
                north_ref[5 + c, i],
                south_ref[5 + c, i],
                field_side_ref[c, i + 2],
                field_side_ref[c, i],
            ]
            both_side = s_side + relaxed(f_side, side_shares, s_side, others)
            if c == 0 and i == half - 1:
                both = both - load
                both_side = both_side - load_side
            out_ref[i, FIELD + c] = s
            out_ref[i, FIELD_SIDE + c] = s_side
            out_ref[i, BOTH + c] = both
            out_ref[i, BOTH_SIDE + c] = both_side
            if i in (0, half - 1):
                both_ends[c, i] = both
        send(i)
    outer = pack(shape.has_low * jnp.exp(-low_ref[4]), shape.has_high * jnp.exp(-high_ref[4]))
    inner = jnp.where(lower, fluid_ref[1], fluid_ref[half])
    ring_shares = [
        safe_share(ring, jnp.where(lon == 3, ring_side, lon_next(ring))),
        safe_share(ring, jnp.where(lon == 0, ring_side, lon_prev(ring))),
        safe_share(ring, north_of(ring)),
        safe_share(ring, south_of(ring)),
        safe_share(ring, outer),
        safe_share(ring, inner),
    ]
    ring_coefficients = coefficients(
        ring,
        ring_shares,
        jnp.where(lower, shape.step(-1), shape.step(half)),
        jnp.where(lower, shape.step(-2), shape.step(half + 1)),
        jnp.where(lower, shape.step(0), shape.step(half - 1)),
    )
    for n in range(5):
        out_ref[half, RING + n] = ring_coefficients[n]
    ring_both = []
    for c in range(3):
        s, s_side = ring_field[c], ring_field_side[c]
        others = [
            jnp.where(lon == 3, s_side, lon_next(s)),
            jnp.where(lon == 0, s_side, lon_prev(s)),
            lat_next(s),
            lat_prev(s),
            pack(low_ref[5 + c], high_ref[5 + c]),
            jnp.where(lower, field_ref[c, 1], field_ref[c, half]),
        ]
        ring_both.append(s + relaxed(ring, ring_shares, s, others))
    low_step = shape.step(0) - shape.step(-1)
    high_step = shape.step(half) - shape.step(half - 1)
    for c in range(3):
        first, last = both_ends[c, 0], both_ends[c, half - 1]
        out_ref[half, LOW + c] = field_ref[c, 1] - field_ref[c, 0]
        out_ref[half, LOW_BOTH + c] = low_step * (
            first - jnp.where(lower, ring_both[c], swap_halves(last))
        )
        out_ref[half, HIGH + c] = field_ref[c, half + 1] - field_ref[c, half]
        out_ref[half, HIGH_BOTH + c] = high_step * (
            jnp.where(lower, swap_halves(first), ring_both[c]) - last
        )
    out_ref[half, ENDS:BLOCK] = jnp.zeros((BLOCK - ENDS, 8, width), F32)
    send(half)
    for copy in copies:
        copy.wait()


AHEAD = 8


def gradient_kernel(
    v_ref, pred_ref, data_ref, k_high_ref, k_low_ref, blocks_ref,
    new_ref, half_ref, misfit_ref, v_in_ref, new_out_ref, half_out_ref, sa_ref, d_ref, in_ref, e_ref, side_ref, north_ref, product_ref,
    total_ref, k_low_in_ref, sems, out_sems, *, scale, rad_n,
):
    nr, nl, width = v_ref.shape
    shape = Shape(nr, width, rad_n)
    half = shape.half
    sites = k_high_ref.shape[1]
    lon, lower = shape.lon, shape.lower
    copies = [
        pltpu.make_async_copy(blocks_ref.at[i], in_ref.at[i], sems.at[i]) for i in range(half + 1)
    ]
    low_copy = pltpu.make_async_copy(k_low_ref, k_low_in_ref, sems.at[half + 1])
    low_copy.start()
    copies[half].start()
    for i in range(min(AHEAD, half)):
        copies[i].start()
    v_copy = pltpu.make_async_copy(v_ref, v_in_ref, sems.at[half + 2])
    v_copy.start()
    groups = []
    for first in range(0, half, 6):
        group = []
        for at in (first, first + half):
            for inner, outer in ((half_out_ref, half_ref), (new_out_ref, new_ref)):
                rows = slice(at, at + min(6, half - first))
                sem = out_sems.at[4 * len(groups) + len(group)]
                group.append(pltpu.make_async_copy(inner.at[rows], outer.at[rows], sem))
        groups.append(group)
    ends_ref = in_ref.at[half]

    flat = pred_ref[0]
    for n in range(1, pred_ref.shape[0]):
        flat = flat + pred_ref[n]
    predicted = jnp.concatenate(
        [flat[:, c * sites : (c + 1) * sites] for c in range(3)], axis=0
    )
    weight = data_ref[4:7, :]
    weighted = weight * (predicted * scale - data_ref[1:4, :])
    squares = jnp.sum(weighted * weighted, axis=1, keepdims=True)
    misfit_ref[...] = jnp.sum(squares, axis=0, keepdims=True) * (1.0 / (3 * sites))
    pulled = (weight * weighted) * scale
    pulled = jnp.concatenate([pulled, jnp.zeros((5, sites), F32)], axis=0)
    for col in range(COLS):
        if col == 0:
            low_copy.wait()
        spread = product(pulled, k_high_ref[col], k_low_in_ref[col], 0)
        for c in range(3):
            sa_ref[c, col : col + 1, :] = spread[c : c + 1, :]

    for c in range(3):
        x = sa_ref[c]

        def window(start):
            return shape.first_weight * jnp.where(
                lower,
                x if start == 0 else pltpu.roll(x, 8 - start, 0),
                x if start == 4 else pltpu.roll(x, (4 - start) % 8, 0),
            )

        own = window(2)
        east = window(3)
        west = window(1)
        outside = jnp.where(lon < 2, west, east)
        d_ref[0, c] = east - own
        d_ref[1, c] = west - own
        d_ref[2, c] = lat_next(own) - own
        d_ref[3, c] = lat_prev(own) - own
        d_ref[4, c] = own
        d_ref[5, c] = jnp.where(lon < 2, own, window(4)) - outside
        d_ref[6, c] = jnp.where(lon < 2, window(0), own) - outside
        d_ref[7, c] = lat_next(outside) - outside
        d_ref[8, c] = lat_prev(outside) - outside
        d_ref[9, c] = outside

    def change(coeffs, first):
        out = []
        for c in range(3):
            total = coeffs[0] * d_ref[first, c]
            for n in range(1, 5):
                total = total + coeffs[n] * d_ref[first + n, c]
            out.append(total)
        return out

    above, below = shape.step(1) - 1.0, shape.step(-1) - 1.0

    def own_change(ref, at, fluid, i):
        shares = [ref[at + n] for n in range(6)]
        scaled = (2.0 * RELAX_RATE * shape.step(i)) * fluid
        coeffs = shares[:4] + [above * shares[4] + below * shares[5]]
        return [scaled * x for x in change(coeffs, 0)]

    def first_pass(i):
        if i % 2 == 0:

            @pl.when(lax.axis_index("rad") >= 0)
            def _():
                for n in range(i, min(i + 2, half)):
                    copies[n].wait()
                    if n + AHEAD < half:
                        copies[n + AHEAD].start()

        e = own_change(in_ref.at[i], SHARE, in_ref[i, FLUID], i)
        side = change([in_ref[i, SIDE + n] for n in range(5)], 5)
        for c in range(3):
            e_ref[c, i] = e[c]
            side_ref[c, i] = side[c]
            north_ref[c, i] = lat_next(in_ref[i, FIELD + c])
            north_ref[3 + c, i] = lat_next(in_ref[i, BOTH + c])
            north_ref[6 + c, i] = lat_next(e[c])

    def second_pass(i, p_down):
        here, step = shape.step(i), shape.step(i + 1) - shape.step(i)
        weighted = [0.0] * 4
        plain = [0.0] * 4
        for c in range(3):
            s, s_side = in_ref[i, FIELD + c], in_ref[i, FIELD_SIDE + c]
            both, both_side = in_ref[i, BOTH + c], in_ref[i, BOTH_SIDE + c]
            e, e_side = e_ref[c, i], side_ref[c, i]

            def differences(x, x_side, x_north):
                return [jnp.where(lon == 3, x_side, lon_next(x)) - x, x_side - x, x_north - x]

            d_field = differences(s, s_side, north_ref[c, i])
            d_both = differences(both, both_side, north_ref[3 + c, i])
            d_e = differences(e, e_side, north_ref[6 + c, i])
            if i < half - 1:
                d_field.append(in_ref[i + 1, FIELD + c] - s)
                d_both.append(step * (in_ref[i + 1, BOTH + c] - both))
                d_e.append(e_ref[c, i + 1] - e)
            else:
                d_field.append(ends_ref[HIGH + c])
                d_both.append(ends_ref[HIGH_BOTH + c])
                d_e.append(jnp.where(lower, swap_halves(e_ref[c, 0]), ring[c]) - e)
            slopes = [d_ref[0, c], d_ref[1, c], d_ref[2, c], d_ref[4, c]]
            for n in range(4):
                weighted[n] = weighted[n] + d_both[n] * slopes[n]
                plain[n] = plain[n] + d_field[n] * d_e[n]
        p_east, p_cut, p_north = [here * weighted[n] + plain[n] for n in range(3)]
        p_up = weighted[3] + plain[3]
        p_west = jnp.where(lon == 0, p_cut, lon_prev(p_east))
        product_ref[i] = lat_prev(p_north)
        total = None
        for n, x in ((0, p_east), (1, p_west), (2, p_north), (4, p_up), (5, p_down)):
            share = in_ref[i, SHARE + n]
            term = (share * share) * x
            total = term if total is None else total + term
        total_ref[i] = total
        return p_up

    def third_pass(i):
        share = in_ref[i, SHARE + 3]
        total = total_ref[i] + (share * share) * product_ref[i]
        total = in_ref[i, BASE] - RELAX_RATE * (in_ref[i, FLUID] * total)
        half_out_ref[i] = total[0:4, :]
        half_out_ref[i + half] = total[4:8, :]
        new_out_ref[i] = v_in_ref[i] + total[0:4, :]
        new_out_ref[i + half] = v_in_ref[i + half] + total[4:8, :]

    copies[half].wait()
    ring = change([ends_ref[RING + n] for n in range(5)], 0)
    e_last = own_change(ends_ref, LAST, ends_ref[LAST + 6], half - 1)
    lead = min(2, half)
    for i in range(lead):
        first_pass(i)
    p_down = None
    for c in range(3):
        e_low = jnp.where(lower, ring[c], swap_halves(e_last[c]))
        term = ends_ref[LOW_BOTH + c] * d_ref[4, c] + ends_ref[LOW + c] * (e_ref[c, 0] - e_low)
        p_down = term if p_down is None else p_down + term
    for i in range(half):
        if i + lead < half:
            first_pass(i + lead)
        p_down = second_pass(i, p_down)
        if i == 1:
            v_copy.wait()
        if i > 0:
            third_pass(i - 1)
        if i % 6 == 0 and i > 0:

            @pl.when(lax.axis_index("rad") >= 0)
            def _():
                for copy in groups[i // 6 - 1]:
                    copy.start()

    if half == 1:
        v_copy.wait()
    third_pass(half - 1)
    for copy in groups[-1]:
        copy.start()
    for group in groups:
        for copy in group:
            copy.wait()


def call(
    kernel, outs, ins, scratch=(), flops=1, name=None, held_in=(), held_out=(), far_in=(),
    far_out=(), near_out=(),
):
    spaces = {"s": pltpu.SMEM, "v": pltpu.VMEM, "h": pltpu.HBM}
    made = pl.pallas_call(
        kernel,
        out_shape=[
            pltpu.VMEM(shape, dtype)
            if n in held_out
            else pltpu.HBM(shape, dtype)
            if n in far_out or n in near_out
            else jax.ShapeDtypeStruct(shape, dtype)
            for n, (shape, dtype) in enumerate(outs)
        ],
        in_specs=[pl.BlockSpec(memory_space=spaces[k]) for k in ins],
        out_specs=[
            pl.BlockSpec(memory_space=pltpu.HBM if n in far_out else pltpu.VMEM)
            for n in range(len(outs))
        ],
        scratch_shapes=list(scratch),
        compiler_params=pltpu.CompilerParams(vmem_limit_bytes=VMEM_LIMIT),
        cost_estimate=pl.CostEstimate(flops=flops, bytes_accessed=1 << 20, transcendentals=0),
        name=name,
    )

    def run(*args):
        return made(
            *[
                pltpu.with_memory_space_constraint(a, pltpu.VMEM if n in held_in else pltpu.HBM)
                if n in held_in or n in far_in
                else a
                for n, a in enumerate(args)
            ]
        )

    return run


def body(
    logvisc, momentum, displacement, ice_history, load_steps, site_cells, observed, site_weight
):
    nr, nl, nlat = logvisc.shape
    own_sites = site_cells.shape[0]
    lon_n = lax.axis_size("lon")
    rad_n = lax.axis_size("rad")
    total_lon = nl * lon_n
    sites = own_sites * lon_n
    devices = lon_n * rad_n
    half = nr // 2
    scale = 1.0 / math.sqrt(total_lon * nlat)
    row = (8, nlat)

    def across_rad(down, up):
        if rad_n == 2:
            both = lax.ppermute(down, "rad", [(0, 1), (1, 0)])
            return both, both
        upward = [(i, i + 1) for i in range(rad_n - 1)]
        downward = [(t, s) for s, t in upward]
        return lax.ppermute(up, "rad", upward), lax.ppermute(down, "rad", downward)

    eastward = [(i, (i + 1) % lon_n) for i in range(lon_n)]
    westward = [(t, s) for s, t in eastward]
    column, layers = (4 * nr, 1, nlat), (8, nl, nlat)
    first_column = (4 * nr + ice_history.shape[0], 1, nlat)
    to_west, to_east, to_west2, to_east2, to_low, to_high, packets = call(
        functools.partial(message_kernel, rad_n=rad_n),
        [
            (shape, F32)
            for shape in [first_column] * 2 + [column] * 2 + [layers] * 2 + [(lon_n, 1, 7 * own_sites)]
        ],
        "vvvvvv",
        name="messages",
        flops=2875000000,
        far_in=(0, 1, 2, 3, 4, 5),
    )(logvisc, displacement, ice_history, site_cells[None], observed, site_weight)
    gathered = lax.all_to_all(packets, "lon", 0, 0)
    west = lax.ppermute(to_east, "lon", eastward)
    east = lax.ppermute(to_west, "lon", westward)
    low, high = across_rad(to_low, to_high)
    west2 = lax.ppermute(to_east2, "lon", eastward)
    east2 = lax.ppermute(to_west2, "lon", westward)

    k_high, k_low, data = call(
        functools.partial(weights_kernel, total_lon=total_lon),
        [((COLS, sites, nlat), BF16)] * 2 + [((8, sites), F32)],
        "v",
        scratch=[pltpu.VMEM((16, sites), F32)],
        name="site_weights",
        flops=3680000000,
        held_out=(0, 1, 2),
    )(gathered)

    padded = -(-3 * sites // 128) * 128
    partial, to_corner_low, to_corner_high = call(
        functools.partial(forward_kernel, rad_n=rad_n),
        [((devices, 1, padded), F32), ((8, 1, nlat), F32), ((8, 1, nlat), F32)],
        "s" + "v" * 9,
        scratch=[
            pltpu.VMEM(shape + row, F32)
            for shape in [(half,)] * 2 + [(3, half)] * 3 + [(half,)] * 3 + [(half + 1,), (half,)]
            + [(3, half)] * 2 + [(6,)]
        ],
        name="forward",
        flops=6325000000,
        held_in=(8, 9),
        far_in=(7,),
        near_out=(0, 1, 2),
    )(load_steps, logvisc, displacement, west, east, low, high, ice_history, k_high, k_low)
    predicted = lax.all_to_all(partial, ("lon", "rad"), 0, 0)

    corner_low, corner_high = across_rad(to_corner_low, to_corner_high)
    (blocks,) = call(
        functools.partial(prepare_kernel, rad_n=rad_n),
        [((half + 1, BLOCK) + row, F32)],
        "s" + "v" * 12,
        scratch=[
            pltpu.VMEM(shape + row, F32)
            for shape in [(half + 2,), (3, half + 2)] * 2 + [(8, half)] * 2 + [(half + 1, BLOCK)]
        ]
        + [pltpu.SemaphoreType.DMA((half + 1,))],
        name="prepare",
        flops=8050000000,
        far_in=(1, 2, 3, 4),
        far_out=(0,),
    )(
        load_steps, logvisc, momentum, displacement, ice_history, west, east, west2, east2, low,
        high, corner_low, corner_high,
    )

    new_logvisc, half_momentum, misfit = call(
        functools.partial(gradient_kernel, scale=scale, rad_n=rad_n),
        [((nr, nl, nlat), F32), ((nr, nl, nlat), F32), ((1, 1), F32)],
        "hvvvhh",
        scratch=[pltpu.VMEM((nr, nl, nlat), F32)] * 3
        + [
            pltpu.VMEM(shape + row, F32)
            for shape in [(3,), (10, 3), (half + 1, BLOCK), (3, half), (3, half), (9, half)]
            + [(half,)] * 2
        ]
        + [
            pltpu.VMEM((COLS, sites, nlat), BF16),
            pltpu.SemaphoreType.DMA((half + 3,)),
            pltpu.SemaphoreType.DMA((4 * -(-half // 6),)),
        ],
        name="gradient",
        flops=6900000000,
        held_in=(2, 3),
        far_in=(0, 4, 5),
        far_out=(0, 1),
    )(logvisc, predicted, data, k_high, k_low, blocks)
    return (new_logvisc, half_momentum, misfit.reshape(1))


def solution(mesh):
    return jax.shard_map(
        body,
        mesh=mesh,
        in_specs=(
            P("rad", "lon", None),
            P("rad", "lon", None),
            P(None, "rad", "lon", None),
            P(None, "lon", None),
            P(),
            P("lon"),
            P(None, "lon"),
            P(None, "lon"),
        ),
        out_specs=(P("rad", "lon", None), P("rad", "lon", None), P()),
        check_vma=False,
    )
```
